32 devices in a mesh: section: 2 (over core), ctx: 4 (over z), fsdp: 4 (over y, x).
Axes of the slice: x: 2, y: 2, z: 4, core: 2. Of those that a mesh axis runs over, the one named last changes fastest.
Arguments:
- inputs: bfloat16 [2, 4, 2048, 1024], P(None, 'fsdp', 'ctx'), may hold values from -6 to 6
- cotangent: bfloat16 [2, 4, 2048, 1024], P(None, 'fsdp', 'ctx'), may hold values from -6 to 6
- segments: int32 [2, 4, 2048], P(None, 'fsdp', 'ctx'), may hold values from 0 to 2047, as said below
- w_qkv: bfloat16 [2, 1024, 3072], P('section', 'fsdp'), may hold values from -0.1875 to 0.1875
- w_out: bfloat16 [2, 1024, 1024], P('section', 'fsdp'), may hold values from -0.5 to 0.5
- w_up: bfloat16 [2, 1024, 4096], P('section', 'fsdp'), may hold values from -0.1875 to 0.1875
- w_down: bfloat16 [2, 4096, 1024], P('section', 'fsdp'), may hold values from -0.09375 to 0.09375
- vectors: bfloat16 [2, 12288], P('section', 'fsdp'), may hold values from -0.8 to 1.25, as said below
Outputs:
- activations: bfloat16 [2, 2, 4, 2048, 1024], P('section', None, 'fsdp', 'ctx')
- input_grad: float32 [2, 2, 4, 2048, 1024], P('section', None, 'fsdp', 'ctx')
- grad_qkv: float32 [2, 1024, 3072], P('section', 'fsdp')
- grad_out: float32 [2, 1024, 1024], P('section', 'fsdp')
- grad_up: float32 [2, 1024, 4096], P('section', 'fsdp')
- grad_down: float32 [2, 4096, 1024], P('section', 'fsdp')
- grad_vectors: float32 [2, 12288], P('section', 'fsdp')
The draws below stay inside these ranges and needn't reach their ends.
Inputs may be any that keep to these rules, and one draw needn't show every extreme that they name: `segments`: along a sequence the entries never fall and each is at most its own position; documents are contiguous. In every sequence slot of the micro-batches, one micro-batch drawn from the seed holds a single document over all 2048 positions. `vectors`: gains (entries 0 .. 1023 and 5120 .. 6143 of each section) lie in 0.75 to 1.25; the other entries are biases.
All inputs are finite; a program needn't handle non-finite values.
Results may differ from the reference program's by a relative error of at most 0.017.
Values may be sent and summed in bfloat16 or wider, within the bound.
No kernel may reach another device: no remote copies, remote signals or barrier semaphores. Data moves between devices by JAX's collectives and lax.ppermute only.
A program may use at most 640 MiB of HBM per device.

```python
import jax
import jax.numpy as jnp
from jax import lax

D = 1024
HEADS = 16
FF = 4096
NVEC = 12288
WIN = 1024
MICRO = 2
LEN = 2048
SEQUENCES = 4


def draw_segments(key, part):
    key = jax.random.fold_in(key, 11)
    first_key, second_key = jax.random.split(key)
    position = jnp.arange(LEN, dtype=jnp.int32)
    breaks = jax.random.randint(first_key, (MICRO, SEQUENCES, LEN), 0, WIN) == 0
    breaks = breaks | (position == LEN - 1)[None, None, :]
    whole_doc = jax.random.randint(second_key, (SEQUENCES,), 0, MICRO)
    single = jnp.arange(MICRO, dtype=jnp.int32)[:, None] == whole_doc[None, :]
    breaks = jnp.where(single[:, :, None], False, breaks) | (position == 0)[None, None, :]
    marked = jnp.where(breaks, position[None, None, :], 0)
    return lax.cummax(marked, axis=2).astype(jnp.int32)


def draw_vectors(key, part):
    key = jax.random.fold_in(key, 23)
    gain_key, bias_key = jax.random.split(key)
    column_index = jnp.arange(NVEC)
    is_gain = (column_index < D) | (column_index >= 5 * D) & (column_index < 6 * D)
    gains = 1.0 + jax.random.uniform(gain_key, (2, NVEC), jnp.float32, -0.25, 0.25)
    biases = 0.2 * jax.random.truncated_normal(bias_key, -4.0, 4.0, (2, NVEC), jnp.float32)
    return jnp.where(is_gain[None, :], gains, biases).astype(jnp.bfloat16)


def levels(rng, shape, shards, smallest, top_value):
    level = 1.0
    for axis_at, parts in shards:
        heights = jax.random.uniform(jax.random.fold_in(jax.random.fold_in(rng, 6), axis_at), (parts,), jnp.float32, smallest / len(shards), top_value / len(shards))
        level = level * jnp.repeat(jnp.exp(heights), shape[axis_at] // parts).reshape((-1,) + (1,) * (len(shape) - 1 - axis_at))
    return level


def gaussian(rng, dims, scale, bound, cuts=(), kind=jnp.bfloat16):
    result = jax.random.normal(rng, dims, jnp.float32) * scale
    if len(cuts) > 0:
        result = levels(rng, dims, cuts, -0.22, 0.18) * result
    return jnp.clip(result, min=-bound, max=bound).astype(kind)


def setup_inputs(seed: int = 0) -> dict:
    splits = jax.random.split(jax.random.key(seed), 9)
    return {
        "inputs": gaussian(splits[0], (MICRO, SEQUENCES, LEN, D), 1.0, 6.0, ((1, 4), (2, 4))),
        "cotangent": gaussian(splits[1], (MICRO, SEQUENCES, LEN, D), 1.0, 6.0, ((1, 4), (2, 4))),
        "segments": draw_segments(jax.random.fold_in(splits[8], 71), 0),
        "w_qkv": gaussian(splits[3], (2, D, 3 * D), D ** -0.5, 0.1875, ((0, 2), (1, 4))),
        "w_out": gaussian(splits[4], (2, D, D), (D // 8) ** -0.5, 0.5, ((0, 2), (1, 4))),
        "w_up": gaussian(splits[5], (2, D, FF), D ** -0.5, 0.1875, ((0, 2), (1, 4))),
        "w_down": gaussian(splits[6], (2, FF, D), FF ** -0.5, 0.09375, ((0, 2), (1, 4))),
        "vectors": draw_vectors(jax.random.fold_in(splits[8], 71), 0),
    }


EPSILON = 1e-05

@jax.custom_vjp
def low(v):
    return lax.optimization_barrier(v.astype(jnp.bfloat16)).astype(jnp.float32)

@jax.custom_vjp
def low_back(v):
    return v

def low_keep(v):
    return (low(v), None)

def low_pass(kept, grad):
    return (grad,)

def back_keep(v):
    return (v, None)

def back_low(kept, grad):
    return (low(grad),)
low.defvjp(low_keep, low_pass)
low_back.defvjp(back_keep, back_low)

def layer_norm(values, gain, shift):
    centred = values - lax.optimization_barrier(jnp.mean(values, axis=-1, keepdims=True))
    spread = lax.optimization_barrier(jnp.mean(centred * centred, axis=-1, keepdims=True))
    return centred * lax.rsqrt(spread + EPSILON) * gain + shift

def unpack(packed):
    pieces = []
    offset = 0
    for length in (D, D, D, D, D, D, D, FF, D):
        pieces.append(packed[offset:offset + length])
        offset = offset + length
    return pieces

def layer(hidden, starts, mat_qkv, mat_out, mat_up, mat_down, packed):
    gain_one, bias_one, query_bias, value_bias, out_bias, gain_two, bias_two, up_bias, down_bias = unpack(packed)
    highest = lax.Precision.HIGHEST
    normed = low(layer_norm(hidden, gain_one, bias_one))
    mixed = jnp.dot(normed, mat_qkv, precision=highest)
    queries = low_back(low(mixed[:, :D] + query_bias))
    keys = low_back(low(mixed[:, D:2 * D]))
    values = low_back(low(mixed[:, 2 * D:] + value_bias))
    head_dim = D // HEADS
    scale = 1.0 / head_dim ** 0.5
    block = min(512, LEN)
    blocks = LEN // block
    slopes = (jnp.exp2(-0.5 * (jnp.arange(HEADS) + 1.0)) * (4.0 / WIN)).astype(jnp.float32)
    padding = jnp.zeros((WIN, D), jnp.float32)
    keys_pad = jnp.concatenate([padding, keys], 0).reshape(WIN + LEN, HEADS, head_dim)
    values_pad = jnp.concatenate([padding, values], 0).reshape(WIN + LEN, HEADS, head_dim)
    query_heads = queries.reshape(LEN, HEADS, head_dim)

    def attend(number):
        first = number * block
        query_part = lax.dynamic_slice_in_dim(query_heads, first, block, 0)
        key_part = lax.dynamic_slice_in_dim(keys_pad, first, WIN + block, 0)
        value_part = lax.dynamic_slice_in_dim(values_pad, first, WIN + block, 0)
        start_part = lax.dynamic_slice_in_dim(starts, first, block, 0)
        query_pos = first + jnp.arange(block, dtype=jnp.int32)
        key_pos = first - WIN + jnp.arange(WIN + block, dtype=jnp.int32)
        distance = query_pos[:, None] - key_pos[None, :]
        scores = jnp.einsum('qhd,khd->hqk', query_part, key_part, precision=highest) * scale
        scores = low_back(scores - slopes[:, None, None] * distance.astype(jnp.float32)[None])
        allowed = (key_pos[None, :] >= start_part[:, None]) & (distance >= 0) & (distance < WIN)
        scores = jnp.where(allowed[None], scores, -1e+30)
        weights = low(jax.nn.softmax(scores, axis=-1))
        return jnp.einsum('hqk,khd->qhd', weights, value_part, precision=highest).reshape(block, D)
    attended = lax.map(jax.checkpoint(attend), jnp.arange(blocks, dtype=jnp.int32))
    attended = low_back(low(attended.reshape(LEN, D)))
    branch = low_back(jnp.dot(attended, mat_out, precision=highest) + out_bias)
    middle = hidden + branch
    normed_two = low(layer_norm(middle, gain_two, bias_two))
    upward = low_back(jnp.dot(normed_two, mat_up, precision=highest) + up_bias)
    activated = low(jax.nn.gelu(upward, approximate=True))
    return middle + low_back(jnp.dot(activated, mat_down, precision=highest) + down_bias)

def reference(inputs, cotangent, segments, w_qkv, w_out, w_up, w_down, vectors):
    count = MICRO * SEQUENCES
    flat_inputs = inputs.reshape(count, LEN, D)
    flat_cotangent = cotangent.reshape(count, LEN, D)
    flat_segments = segments.reshape(count, LEN)
    weights_first = tuple((w[0].astype(jnp.float32) for w in (w_qkv, w_out, w_up, w_down, vectors)))
    weights_second = tuple((w[1].astype(jnp.float32) for w in (w_qkv, w_out, w_up, w_down, vectors)))
    empty_sums = jax.tree.map(jnp.zeros_like, (weights_first, weights_second))

    def advance(totals, entries):
        hidden, grad_top, starts = entries

        def first_layer(source, *weights):
            return layer(source, starts, *weights)
        first_out, first_back = jax.vjp(first_layer, hidden.astype(jnp.float32), *weights_first)
        boundary = low(first_out)
        second_out, second_back = jax.vjp(first_layer, boundary, *weights_second)
        second_grads = second_back(grad_top.astype(jnp.float32))
        returned = low(second_grads[0])
        first_grads = first_back(returned)
        new_first = tuple((total + grad for total, grad in zip(totals[0], first_grads[1:])))
        new_second = tuple((total + grad for total, grad in zip(totals[1], second_grads[1:])))
        results = (first_out.astype(jnp.bfloat16), second_out.astype(jnp.bfloat16), first_grads[0], returned)
        return ((new_first, new_second), results)
    totals, results = lax.scan(advance, empty_sums, (flat_inputs, flat_cotangent, flat_segments))
    activations = jnp.stack([results[0], results[1]]).reshape(2, MICRO, SEQUENCES, LEN, D)
    input_grad = jnp.stack([results[2], results[3]]).reshape(2, MICRO, SEQUENCES, LEN, D)
    stacked = [jnp.stack([totals[0][number], totals[1][number]]) for number in range(5)]
    return (activations, input_grad, stacked[0], stacked[1], stacked[2], stacked[3], stacked[4])
```

```python
import functools
import math

import jax
import jax.numpy as jnp
from jax import lax
from jax.experimental import pallas as pl
from jax.experimental.pallas import tpu as pltpu
from jax.sharding import PartitionSpec as P

D = 1024
HEADS = 16
FF = 4096
WIN = 1024

EPSILON = 1e-05
F32 = jnp.float32
BF16 = jnp.bfloat16
LANES = 128
MASKED = -1e30


def flip(block, axis, bit):
    count = lax.axis_size(axis)
    return lax.ppermute(block, axis, [(i, i ^ bit) for i in range(count)])


def step_along(block, axis, distance):
    devices = range(lax.axis_size(axis))
    route = [(i - distance, i) for i in devices if i - distance in devices]
    return lax.ppermute(block, axis, route)


def gather_rows(shard):
    me = lax.axis_index("fsdp")
    half = shard.shape[0] // 2
    from_x = flip(shard, "fsdp", 1)
    from_y = flip(shard, "fsdp", 2)
    far_top = flip(from_x[:half], "fsdp", 2)
    far_low = flip(from_y[half:], "fsdp", 1)
    whole = jnp.zeros((4,) + shard.shape, shard.dtype)
    whole = lax.dynamic_update_slice(whole, shard[None], (me, 0, 0))
    whole = lax.dynamic_update_slice(whole, from_x[None], (me ^ 1, 0, 0))
    whole = lax.dynamic_update_slice(whole, from_y[None], (me ^ 2, 0, 0))
    whole = lax.dynamic_update_slice(whole, far_top[None], (me ^ 3, 0, 0))
    return lax.dynamic_update_slice(whole, far_low[None], (me ^ 3, half, 0))


def scatter_rows(parts):
    me = lax.axis_index("fsdp")
    half = parts.shape[1] // 2

    def piece(bit, top):
        start = 0 if top else half
        return lax.dynamic_slice(parts, (me ^ bit, start, 0), (1, half, parts.shape[2]))

    def both(first, second):
        return (first.astype(F32) + second.astype(F32)).astype(BF16)

    top_in = flip(jnp.concatenate([piece(1, True), piece(3, True)]), "fsdp", 1)
    low_in = flip(jnp.concatenate([piece(2, False), piece(3, False)]), "fsdp", 2)
    top_far = flip(both(piece(2, True), top_in[1:]), "fsdp", 2)
    low_far = flip(both(piece(1, False), low_in[1:]), "fsdp", 1)
    top = piece(0, True).astype(F32) + top_in[:1].astype(F32) + top_far.astype(F32)
    low = piece(0, False).astype(F32) + low_in[:1].astype(F32) + low_far.astype(F32)
    return jnp.concatenate([top[0], low[0]]).astype(BF16)


def sum_ctx(block):
    count = lax.axis_size("ctx")
    if count != 4:
        return lax.psum(block, "ctx")
    me = lax.axis_index("ctx")
    rows = block.shape[0]
    for bit, part in ((1, rows // 2), (2, rows // 4)):
        high = (me & bit) != 0
        lower, upper = block[:part], block[part:]
        kept = jnp.where(high, upper, lower)
        got = flip(jnp.where(high, lower, upper), "ctx", bit)
        block = (kept.astype(F32) + got.astype(F32)).astype(BF16)
    for bit in (2, 1):
        high = (me & bit) != 0
        got = flip(block, "ctx", bit)
        block = jnp.concatenate([jnp.where(high, got, block), jnp.where(high, block, got)])
    return block


def lanes_of(rows, low):
    lane = lax.broadcasted_iota(jnp.int32, (rows, LANES), 1)
    return lane < LANES // 2 if low else lane >= LANES // 2


def split3(values):
    first = values.astype(BF16)
    rest = values - first.astype(F32)
    second = rest.astype(BF16)
    third = (rest - second.astype(F32)).astype(BF16)
    return first, second, third


def dot_nt(left, right):
    return lax.dot_general(left, right, (((1,), (1,)), ((), ())), preferred_element_type=F32)


def dot_nn(left, right):
    return lax.dot_general(left, right, (((1,), (0,)), ((), ())), preferred_element_type=F32)


def forward_kernel(rows, halo, block, q_ref, k_ref, v_ref, lo_ref, ek_ref, eq_ref, o_ref, e_ref):
    lane = lax.broadcasted_iota(jnp.int32, (block, LANES), 1)
    for q0 in range(0, rows, block):
        k0 = max(0, halo + q0 - WIN) // block * block
        k1 = halo + q0 + block
        q = q_ref[0, q0 : q0 + block, :]
        lo = lo_ref[0, q0 : q0 + block, :]
        outs = []
        for t in range(2):
            keep = lanes_of(block, t == 0)
            eq = jnp.broadcast_to(eq_ref[0, t : t + 1, :], (block, LANES))
            qcat = jnp.concatenate([q, eq.astype(BF16)], axis=1)
            tiles = []
            for kb in range(k0, k1, block):
                k = k_ref[0, kb : kb + block, :]
                kcat = jnp.concatenate(
                    [jnp.where(keep, k, jnp.zeros_like(k)), ek_ref[kb : kb + block, :]], axis=1
                )
                s = dot_nt(qcat, kcat)
                kidx = lax.broadcasted_iota(jnp.int32, (block, block), 1) + kb
                allowed = kidx >= lo
                if kb + block == k1:
                    qidx = lax.broadcasted_iota(jnp.int32, (block, block), 0) + (halo + q0)
                    allowed = allowed & (kidx <= qidx)
                tiles.append(jnp.where(allowed, s, MASKED))
            top = functools.reduce(jnp.maximum, tiles)
            m = jnp.max(top, axis=1, keepdims=True)
            ps = [jnp.exp(s - m) for s in tiles]
            total = jnp.sum(functools.reduce(jnp.add, ps), axis=1, keepdims=True)
            pcat = jnp.concatenate([p.astype(BF16) for p in ps], axis=1)
            o = dot_nn(pcat, v_ref[0, k0:k1, :])
            outs.append(o / total)
            first, second, third = split3(-(m + jnp.log(total)))
            e = jnp.where(lane == 6, first.astype(F32), eq)
            e = jnp.where(lane == 7, second.astype(F32), e)
            e = jnp.where(lane == 8, third.astype(F32), e)
            e_ref[0, t, q0 : q0 + block, :] = e.astype(BF16)
        o_ref[0, q0 : q0 + block, :] = jnp.where(lanes_of(block, True), outs[0], outs[1]).astype(
            BF16
        )


def attend(q, k_all, v_all, lo, ek, eq):
    micro, rows, width = q.shape
    keys = k_all.shape[1]
    halo = keys - rows
    pairs = width // LANES
    block = min(256, rows)
    spec = lambda n: pl.BlockSpec((1, n, LANES), lambda m, p: (m, 0, p))
    pairs_in_window = micro * pairs * 2 * rows * (WIN + block)
    return pl.pallas_call(
        functools.partial(forward_kernel, rows, halo, block),
        grid=(micro, pairs),
        in_specs=[
            spec(rows),
            spec(keys),
            spec(keys),
            pl.BlockSpec((1, rows, 1), lambda m, p: (m, 0, 0)),
            pl.BlockSpec((keys, LANES), lambda m, p: (0, 0)),
            pl.BlockSpec((1, 2, LANES), lambda m, p: (p, 0, 0)),
        ],
        out_specs=[spec(rows), pl.BlockSpec((1, 2, rows, LANES), lambda m, p: (m, p, 0, 0))],
        out_shape=[
            jax.ShapeDtypeStruct(q.shape, BF16),
            jax.ShapeDtypeStruct((micro, 2 * pairs, rows, LANES), BF16),
        ],
        compiler_params=pltpu.CompilerParams(vmem_limit_bytes=48 * 1024 * 1024),
        cost_estimate=pl.CostEstimate(
            flops=pairs_in_window * 1024, bytes_accessed=8 << 20, transcendentals=pairs_in_window
        ),
        name="attention_forward",
    )(q, k_all, v_all, lo[:, :, None], ek, eq)


def backward_kernel(
    rows, halo, block,
    q_ref, k_ref, v_ref, o_ref, do_ref, e_ref, lo_ref, ek_ref,
    dq_ref, dk_ref, dv_ref,
    acc_ref,
):
    keys = halo + rows
    q = q_ref[0]
    do = do_ref[0]
    lo = lo_ref[0]
    lane = lax.broadcasted_iota(jnp.int32, (rows, LANES), 1)
    ones = jnp.where(lax.broadcasted_iota(jnp.int32, (block, LANES), 1) < 3, 1.0, 0.0).astype(BF16)
    product = do.astype(F32) * o_ref[0].astype(F32)
    qcats, docats, qts, dots = [], [], [], []
    for t in range(2):
        keep = lanes_of(rows, t == 0)
        delta = jnp.sum(jnp.where(keep, product, 0.0), axis=1, keepdims=True)
        first, second, third = split3(-delta)
        ed = jnp.where(lane == 0, first.astype(F32), 0.0)
        ed = jnp.where(lane == 1, second.astype(F32), ed)
        ed = jnp.where(lane == 2, third.astype(F32), ed)
        qcats.append(jnp.concatenate([q, e_ref[0, t]], axis=1))
        docats.append(jnp.concatenate([do, ed.astype(BF16)], axis=1))
        qts.append(jnp.where(keep, q, jnp.zeros_like(q)))
        dots.append(jnp.where(keep, do, jnp.zeros_like(do)))
    acc_ref[...] = jnp.zeros_like(acc_ref)
    for kb in range(0, keys, block):
        qlo = max(0, kb - halo)
        qhi = min(rows, -(-(kb + block - 1 + WIN - halo) // block) * block)
        if qhi <= qlo:
            dk_ref[0, kb : kb + block, :] = jnp.zeros((block, LANES), BF16)
            dv_ref[0, kb : kb + block, :] = jnp.zeros((block, LANES), BF16)
            continue
        k = k_ref[0, kb : kb + block, :]
        v = v_ref[0, kb : kb + block, :]
        ek = ek_ref[kb : kb + block, :]
        kidx = lax.broadcasted_iota(jnp.int32, (block, qhi - qlo), 0) + kb
        allowed = kidx >= lo[:, qlo:qhi]
        if kb + block > halo + qlo:
            qidx = lax.broadcasted_iota(jnp.int32, (block, qhi - qlo), 1) + (halo + qlo)
            allowed = allowed & (kidx <= qidx)
        pts, dss, kts = [], [], []
        for t in range(2):
            keep = lanes_of(block, t == 0)
            kt = jnp.where(keep, k, jnp.zeros_like(k))
            vt = jnp.where(keep, v, jnp.zeros_like(v))
            st = dot_nt(jnp.concatenate([kt, ek], axis=1), qcats[t][qlo:qhi])
            pt = jnp.exp(jnp.where(allowed, st, MASKED))
            dpt = dot_nt(jnp.concatenate([vt, ones], axis=1), docats[t][qlo:qhi])
            pts.append(pt.astype(BF16))
            dss.append((pt * dpt).astype(BF16))
            kts.append(kt)
        dv = dot_nn(jnp.concatenate(pts, axis=1), jnp.concatenate([d[qlo:qhi] for d in dots], axis=0))
        dk = dot_nn(jnp.concatenate(dss, axis=1), jnp.concatenate([d[qlo:qhi] for d in qts], axis=0))
        dv_ref[0, kb : kb + block, :] = dv.astype(BF16)
        dk_ref[0, kb : kb + block, :] = dk.astype(BF16)
        kcat = jnp.concatenate(kts, axis=0)
        dqt = lax.dot_general(
            kcat, jnp.concatenate(dss, axis=0), (((0,), (0,)), ((), ())), preferred_element_type=F32
        )
        acc_ref[:, qlo:qhi] += dqt
    scale = 1.0 / math.sqrt(LANES // 2)
    dq_ref[0] = (acc_ref[...].T * scale).astype(BF16)


def attend_back(q, k_all, v_all, o, do, e, lo, ek):
    micro, rows, width = q.shape
    keys = k_all.shape[1]
    halo = keys - rows
    pairs = width // LANES
    block = min(256, rows)
    spec = lambda n: pl.BlockSpec((1, n, LANES), lambda m, p: (m, 0, p))
    pairs_in_window = micro * pairs * 2 * rows * (WIN + block)
    return pl.pallas_call(
        functools.partial(backward_kernel, rows, halo, block),
        grid=(micro, pairs),
        in_specs=[
            spec(rows),
            spec(keys),
            spec(keys),
            spec(rows),
            spec(rows),
            pl.BlockSpec((1, 2, rows, LANES), lambda m, p: (m, p, 0, 0)),
            pl.BlockSpec((1, 1, rows), lambda m, p: (m, 0, 0)),
            pl.BlockSpec((keys, LANES), lambda m, p: (0, 0)),
        ],
        out_specs=[spec(rows), spec(keys), spec(keys)],
        out_shape=[
            jax.ShapeDtypeStruct(q.shape, BF16),
            jax.ShapeDtypeStruct(k_all.shape, BF16),
            jax.ShapeDtypeStruct(k_all.shape, BF16),
        ],
        scratch_shapes=[pltpu.VMEM((LANES, rows), F32)],
        compiler_params=pltpu.CompilerParams(vmem_limit_bytes=48 * 1024 * 1024),
        cost_estimate=pl.CostEstimate(
            flops=pairs_in_window * 2304, bytes_accessed=16 << 20, transcendentals=pairs_in_window
        ),
        name="attention_backward",
    )(q, k_all, v_all, o, do, e, lo[:, None, :], ek)


def mean_last(values):
    return jnp.mean(values, axis=-1, keepdims=True)


def normalize(values):
    centred = values - mean_last(values)
    inverse = lax.rsqrt(mean_last(centred * centred) + EPSILON)
    return centred * inverse, inverse


def norm_back(grad_norm, normal, inverse):
    return inverse * (grad_norm - mean_last(grad_norm) - normal * mean_last(grad_norm * normal))


def mm(left, right):
    return jnp.dot(left, right, preferred_element_type=F32)


def mm_t(left, right):
    return lax.dot_general(left, right, (((1,), (1,)), ((), ())), preferred_element_type=F32)


def mm_rows(left, right):
    return lax.dot_general(left, right, (((0,), (0,)), ((), ())), preferred_element_type=F32)


def gelu_and_slope(u):
    c = math.sqrt(2.0 / math.pi)
    t = jnp.tanh(c * (u + 0.044715 * (u * u * u)))
    value = 0.5 * u * (1.0 + t)
    slope = 0.5 * (1.0 + t) + 0.5 * u * (1.0 - t * t) * (c * (1.0 + 3 * 0.044715 * (u * u)))
    return value, slope


def swap(block):
    return flip(block, "section", 1)


def shards(inputs, cotangent, segments, w_qkv, w_out, w_up, w_down, vectors):
    core = lax.axis_index("section")
    column = lax.axis_index("ctx")
    fs = lax.axis_index("fsdp")
    nf = lax.axis_size("fsdp")
    rows = inputs.shape[2]
    reach = (WIN - 1) // rows + 1
    halo = reach * rows
    first_core = core == 0

    def halves(weight, split):
        parts = split(weight)
        mine = jnp.where(first_core, parts[0], parts[1])
        other = jnp.where(first_core, parts[1], parts[0])
        got = swap(other)
        return jnp.where(first_core, mine, got), jnp.where(first_core, got, mine)

    def split_columns(groups):
        def split(weight):
            view = weight.reshape(weight.shape[0], groups, 2, -1)
            return [view[:, :, i, :].reshape(weight.shape[0], -1) for i in range(2)]

        return split

    def split_rows(weight):
        half = weight.shape[0] // 2
        return [weight[:half], weight[half:]]

    shard_qkv = halves(w_qkv[0], split_columns(3 * nf))
    shard_out = halves(w_out[0], split_rows)
    shard_up = halves(w_up[0], split_columns(nf))
    shard_down = halves(w_down[0], split_rows)
    packed = vectors[0][None]
    other_packed = swap(packed)
    both_packed = jnp.concatenate(
        [jnp.where(first_core, packed, other_packed), jnp.where(first_core, other_packed, packed)]
    )
    all_packed = gather_vectors(both_packed)

    mine = lambda values: lax.dynamic_index_in_dim(values, core, 0, keepdims=False)
    theirs = lambda values: lax.dynamic_index_in_dim(values, 1 - core, 0, keepdims=False)
    own_first = lambda values: jnp.stack([mine(values), theirs(values)])

    x_rel = own_first(inputs[:, 0])
    cot_rel = own_first(cotangent[:, 0])
    starts = own_first(segments[:, 0])
    position = column * rows + jnp.arange(rows, dtype=jnp.int32)
    lo = jnp.maximum(starts, position[None] - (WIN - 1)) - (column * rows - halo)

    key_index = jnp.arange(halo + rows, dtype=jnp.int32)
    high = (key_index // 256 * 256).astype(F32)
    low = (key_index % 256).astype(F32)
    unit = jnp.ones_like(low)
    nothing = jnp.zeros((halo + rows, LANES - 9), F32)
    ek = jnp.concatenate(
        [jnp.stack([high, low, high, low, high, low, unit, unit, unit], 1), nothing], 1
    ).astype(BF16)
    local_heads = HEADS // 2
    per_group = local_heads // nf
    local = jnp.arange(local_heads)
    head = (local // per_group) * (2 * per_group) + core * per_group + local % per_group
    slopes = jnp.exp2(-0.5 * (head.astype(F32) + 1.0)) * (4.0 / WIN)
    first, second, third = [part.astype(F32) for part in split3(slopes)]
    eq = jnp.concatenate(
        [
            jnp.stack([first, first, second, second, third, third], 1),
            jnp.zeros((local_heads, LANES - 6), F32),
        ],
        1,
    ).reshape(local_heads // 2, 2, LANES)

    def fetch_halo(own):
        pieces = []
        block = own
        for _ in range(reach):
            block = step_along(block, "ctx", 1)
            pieces.insert(0, block)
        mine_halo = jnp.concatenate(pieces, 0)
        return jnp.stack([mine_halo, swap(mine_halo)])

    def return_halo(partial):
        carried = None
        for hop in range(reach, 0, -1):
            start = (reach - hop) * rows
            piece = partial[start : start + rows]
            if carried is not None:
                piece = piece + carried.astype(F32)
            carried = step_along(piece.astype(BF16), "ctx", -1)
        return carried.astype(F32)

    def my_half(values, groups):
        view = values.reshape(groups, 2, -1)
        return jnp.where(first_core, view[:, 0], view[:, 1]).reshape(-1)

    def widen(values, groups):
        view = values.reshape(groups, 1, -1)
        zero = jnp.zeros_like(view)
        return jnp.where(
            first_core, jnp.concatenate([view, zero], 1), jnp.concatenate([zero, view], 1)
        ).reshape(-1)

    def unpack(values):
        pieces, offset = [], 0
        for length in (D, D, D, D, D, D, D, FF, D):
            pieces.append(values[offset : offset + length])
            offset += length
        return pieces

    half_d = D // 2
    half_ff = FF // 2

    def forward(layer, x_pair, halo_pair):
        gain_one, bias_one, bq, bv, bo, gain_two, bias_two, bu, bd = unpack(
            all_packed[layer].astype(F32)
        )
        mat_qkv = gather_rows(shard_qkv[layer]).reshape(D, 3 * half_d)
        mat_out = gather_rows(shard_out[layer]).reshape(half_d, D)
        mat_up = gather_rows(shard_up[layer]).reshape(D, half_ff)
        mat_down = gather_rows(shard_down[layer]).reshape(half_ff, D)
        x_all = jnp.concatenate([halo_pair, x_pair], 1).astype(F32)
        normed_all = (normalize(x_all)[0] * gain_one + bias_one).astype(BF16)
        normed = normed_all[:, halo:]
        q = mm(normed.reshape(-1, D), mat_qkv[:, :half_d]) + my_half(bq, nf)
        q = (q.astype(BF16) * BF16(1.0 / math.sqrt(D // HEADS))).reshape(2, rows, half_d)
        flat = normed_all.reshape(-1, D)
        k_all = mm(flat, mat_qkv[:, half_d : 2 * half_d]).astype(BF16)
        k_all = k_all.reshape(2, halo + rows, half_d)
        v_all = (mm(flat, mat_qkv[:, 2 * half_d :]) + my_half(bv, nf)).astype(BF16)
        v_all = v_all.reshape(2, halo + rows, half_d)
        o, e = attend(q, k_all, v_all, lo, ek, eq)
        branch_in = swap(mm(o[1], mat_out).astype(BF16))
        x1 = x_pair[0].astype(F32) + (mm(o[0], mat_out) + branch_in.astype(F32) + bo)
        normal_two, inverse_two = normalize(x1)
        normed_two = (normal_two * gain_two + bias_two).astype(BF16)
        normed_two = jnp.stack([normed_two, swap(normed_two)])
        bu_half = my_half(bu, nf)
        act, slope = gelu_and_slope(mm(normed_two.reshape(-1, D), mat_up) + bu_half)
        act = act.astype(BF16).reshape(2, rows, half_ff)
        slope = slope.astype(BF16)
        down_in = swap(mm(act[1], mat_down).astype(BF16))
        y = x1 + (mm(act[0], mat_down) + down_in.astype(F32) + bd)
        y = y.astype(BF16)
        stored = (
            x_pair, normed_all, q, k_all, v_all, o, e, x1, normed_two, act, slope,
            mat_qkv, mat_out, mat_up, mat_down, gain_one, gain_two,
        )
        return y, stored

    def backward(layer, dy, stored):
        (
            x_pair, normed_all, q, k_all, v_all, o, e, x1, normed_two, act, slope,
            mat_qkv, mat_out, mat_up, mat_down, gain_one, gain_two,
        ) = stored
        flat_dy = dy.reshape(-1, D)
        du = (mm_t(flat_dy, mat_down) * slope.astype(F32)).astype(BF16)
        d_down = mm_rows(act.reshape(-1, half_ff), flat_dy).astype(BF16)
        sum_down = scatter_rows(d_down.reshape(nf, -1, D))
        d_up = mm_rows(normed_two.reshape(-1, D), du).astype(BF16)
        sum_up = scatter_rows(d_up.reshape(nf, -1, half_ff))
        dbd = jnp.sum(dy[0].astype(F32), 0)
        dbu = jnp.sum(du.astype(F32), 0)
        du = du.reshape(2, rows, half_ff)
        dh_in = swap(mm_t(du[1], mat_up).astype(BF16))
        dh = mm_t(du[0], mat_up) + dh_in.astype(F32)
        normal_two, inverse_two = normalize(x1)
        dg2 = jnp.sum(dh * normal_two, 0)
        db2 = jnp.sum(dh, 0)
        dx1 = dy[0].astype(F32) + norm_back(dh * gain_two, normal_two, inverse_two)
        db = dx1.astype(BF16)
        dbo = jnp.sum(db.astype(F32), 0)
        db = jnp.stack([db, swap(db)])
        flat_db = db.reshape(-1, D)
        do = mm_t(flat_db, mat_out).astype(BF16).reshape(2, rows, half_d)
        d_out = mm_rows(o.reshape(-1, half_d), flat_db).astype(BF16)
        sum_out = scatter_rows(d_out.reshape(nf, -1, D))
        dq, dk, dv = attend_back(q, k_all, v_all, o, do, e, lo, ek)
        kv = mat_qkv[:, half_d:]

        def back_rows(m):
            return mm_t(dk[m, :halo], kv[:, :half_d]) + mm_t(dv[m, :halo], kv[:, half_d:])

        early_in = swap(back_rows(1).astype(BF16))
        returned = return_halo(back_rows(0) + early_in.astype(F32))

        def back_own(m):
            return mm_t(
                jnp.concatenate([dq[m], dk[m, halo:], dv[m, halo:]], 1), mat_qkv
            )

        own_in = swap(back_own(1).astype(BF16))
        flat = normed_all.reshape(-1, D)
        d_q = mm_rows(normed_all[:, halo:].reshape(-1, D), dq.reshape(-1, half_d)).astype(BF16)
        d_k = mm_rows(flat, dk.reshape(-1, half_d)).astype(BF16)
        d_v = mm_rows(flat, dv.reshape(-1, half_d)).astype(BF16)
        sum_qkv = scatter_rows(
            jnp.concatenate([d_q, d_k, d_v], 1).reshape(nf, -1, 3 * half_d)
        )
        dbq = jnp.sum(dq.reshape(-1, half_d).astype(F32), 0)
        dbv = jnp.sum(dv.reshape(-1, half_d).astype(F32), 0)
        da = back_own(0) + own_in.astype(F32) + returned
        normal_one, inverse_one = normalize(x_pair[0].astype(F32))
        dg1 = jnp.sum(da * normal_one, 0)
        db1 = jnp.sum(da, 0)
        dx = dx1 + norm_back(da * gain_one, normal_one, inverse_one)
        vector = jnp.concatenate(
            [dg1, db1, widen(dbq, nf), widen(dbv, nf), dbo, dg2, db2, widen(dbu, nf), dbd]
        )
        sums = tuple(sum_ctx(block) for block in (sum_qkv, sum_out, sum_up, sum_down))
        return dx, sums, vector

    y0, stored0 = forward(0, x_rel, fetch_halo(x_rel[0]))
    y0_pair = jnp.stack([y0, swap(y0)])
    y1, stored1 = forward(1, y0_pair, fetch_halo(y0))
    y1_other = swap(y1)

    dx1, sums1, vector1 = backward(1, cot_rel, stored1)
    dx1 = dx1.astype(BF16)
    dx1_pair = jnp.stack([dx1, swap(dx1)])
    dx0, sums0, vector0 = backward(0, dx1_pair, stored0)
    dx0_other = swap(dx0)

    def by_micro(own, other):
        return jnp.where(first_core, jnp.stack([own, other]), jnp.stack([other, own]))

    activations = jnp.where(
        first_core, by_micro(y0_pair[0], y0_pair[1]), by_micro(y1, y1_other)
    )[None, :, None]
    input_grad = jnp.where(
        first_core,
        by_micro(dx0, dx0_other),
        by_micro(dx1_pair[0], dx1_pair[1]).astype(F32),
    )[None, :, None]

    def whole(pair, join):
        kept = jnp.where(first_core, pair[0], pair[1])
        got = swap(jnp.where(first_core, pair[1], pair[0]))
        return join(
            jnp.where(first_core, kept, got), jnp.where(first_core, got, kept)
        ).astype(F32)[None]

    def join_columns(groups):
        def join(left, right):
            split = lambda part: part.reshape(part.shape[0], groups, 1, -1)
            return jnp.concatenate([split(left), split(right)], 2).reshape(left.shape[0], -1)

        return join

    def join_rows(left, right):
        return jnp.concatenate([left, right], 0)

    grad_qkv = whole((sums0[0], sums1[0]), join_columns(3 * nf))
    grad_out = whole((sums0[1], sums1[1]), join_rows)
    grad_up = whole((sums0[2], sums1[2]), join_columns(nf))
    grad_down = whole((sums0[3], sums1[3]), join_rows)
    summed = lax.psum(jnp.stack([vector0, vector1]), ("section", "ctx", "fsdp"))
    length = summed.shape[1] // nf
    grad_vectors = lax.dynamic_slice(summed, (core, fs * length), (1, length))
    return (activations, input_grad, grad_qkv, grad_out, grad_up, grad_down, grad_vectors)


def gather_vectors(packed):
    me = lax.axis_index("fsdp")
    parts = gather_rows(packed)
    return parts.transpose(1, 0, 2).reshape(packed.shape[0], -1)


def solution(mesh):
    placed = (
        P(None, "fsdp", "ctx", None),
        P(None, "fsdp", "ctx", None),
        P(None, "fsdp", "ctx"),
        P("section", "fsdp", None),
        P("section", "fsdp", None),
        P("section", "fsdp", None),
        P("section", "fsdp", None),
        P("section", "fsdp"),
    )
    return jax.shard_map(
        shards,
        mesh=mesh,
        in_specs=placed,
        out_specs=(
            P("section", None, "fsdp", "ctx", None),
            P("section", None, "fsdp", "ctx", None),
            P("section", "fsdp", None),
            P("section", "fsdp", None),
            P("section", "fsdp", None),
            P("section", "fsdp", None),
            P("section", "fsdp"),
        ),
        check_vma=False,
    )
```

```python
import functools
import math

import jax
import jax.numpy as jnp
from jax import lax
from jax.experimental import pallas as pl
from jax.experimental.pallas import tpu as pltpu
from jax.sharding import PartitionSpec as P

D = 1024
HEADS = 16
FF = 4096
WIN = 1024

EPSILON = 1e-05
F32 = jnp.float32
BF16 = jnp.bfloat16
LANES = 128
MASKED = -1e30


LEAST = 256
ROLL = (3, 1, 2, 0)


def flip(block, axis, bit):
    count = lax.axis_size(axis)
    return lax.ppermute(block, axis, [(i, i ^ bit) for i in range(count)])


def step_along(block, axis, distance):
    devices = range(lax.axis_size(axis))
    route = [(i - distance, i) for i in devices if i - distance in devices]
    return lax.ppermute(block, axis, route)


def swap(block):
    return flip(block, "section", 1)


def tie(value, *after):
    return lax.optimization_barrier((value, after))[0]


class Gather:
    def __init__(self, shard, *after, then=()):
        shard = tie(shard, *after) if after else shard
        half = shard.shape[0] // 2
        self.near = flip(shard, "fsdp", 1), flip(shard, "fsdp", 2)
        from_x, from_y = tie(self.near, *then) if then else self.near
        self.far = flip(from_x[:half], "fsdp", 2), flip(from_y[half:], "fsdp", 1)
        self.pieces = (shard, *self.near, *self.far)


def add_bf16(*terms):
    return sum(term.astype(F32) for term in terms).astype(BF16)


class Scatter:
    def __init__(self, send_x, send_y, keep_x, keep_y):
        self.near = flip(send_x, "fsdp", 1), flip(send_y, "fsdp", 2)
        self.keep = keep_x, keep_y

    def second(self, *after):
        (got_x, got_y), (keep_x, keep_y) = tie(self.near, *after), self.keep
        self.half = add_bf16(keep_x[0], got_x[0]), add_bf16(keep_y[0], got_y[0])
        self.far = flip(self.half[0], "fsdp", 2), flip(self.half[1], "fsdp", 1)

    def third(self, *after):
        far_x, far_y = tie(self.far, *after)
        (got_x, got_y), (keep_x, keep_y) = self.near, self.keep
        self.piece = jnp.concatenate(
            [add_bf16(keep_x[1], got_x[1], far_x), add_bf16(keep_y[1], got_y[1], far_y)]
        )


class Column:
    def __init__(self):
        self.line = lax.axis_size("ctx") == 4
        me = lax.axis_index("ctx")
        self.inner = (me == 1) | (me == 2)
        self.block = self.half = self.total = self.outer_got = self.inner_got = None
        self.sums = []
        self.sent = ()

    def step(self, block, *after):
        if not self.line:
            if block is not None:
                self.sums.append(lax.psum(block, "ctx"))
            return
        outer_got, inner_got, block = tie((self.outer_got, self.inner_got, block), *after)
        half = total = None
        if self.block is not None:
            half = add_bf16(self.block, outer_got)
        if self.half is not None:
            total = add_bf16(self.half, inner_got)
        if self.total is not None:
            self.sums.append(jnp.where(self.inner, self.total, outer_got))
        self.block, self.half, self.total = block, half, total
        self.sent = ()
        if block is not None or total is not None:
            sent = total if block is None else block
            if block is not None and total is not None:
                sent = jnp.where(self.inner, total, block)
            self.outer_got = flip(sent, "ctx", 1)
            self.sent += (sent,)
        if half is not None:
            self.inner_got = lax.ppermute(half, "ctx", [(1, 2), (2, 1)])
            self.sent += (half,)


class Line:
    def __init__(self):
        self.token = ()
        self.also = ()

    def run(self, kernel, word, *args, after=()):
        word = tie(word, self.token, self.also, after)
        self.also = ()
        out = kernel(word, *args)
        self.token = out[0] if isinstance(out, (list, tuple)) else out
        return out


def sum_all(block):
    for axis in ("fsdp", "ctx", "section"):
        bit = 1
        while bit < lax.axis_size(axis):
            block = block + flip(block, axis, bit)
            bit *= 2
    return block


def call(kernel, out_shape, *operands, limit=32, flops=0, moved=0, exps=0, name=None, **rest):
    return pl.pallas_call(
        kernel,
        out_shape=out_shape,
        compiler_params=pltpu.CompilerParams(vmem_limit_bytes=limit * 1024 * 1024),
        cost_estimate=pl.CostEstimate(flops=flops, bytes_accessed=moved, transcendentals=exps),
        name=name,
        **rest,
    )(*operands)


def sds(*shape, dtype=BF16):
    return jax.ShapeDtypeStruct(shape, dtype)


def kept(*shape, dtype=BF16):
    return pltpu.HBM(shape, dtype)


ANYWHERE = pl.BlockSpec(memory_space=pltpu.HBM)
SCALARS = pl.BlockSpec(memory_space=pltpu.SMEM)
INSIDE = pl.BlockSpec(memory_space=pltpu.VMEM)


def fixed(*shape):
    return pl.BlockSpec(shape, lambda *_: (0,) * len(shape))


def fetches(me, pieces, wanted, sems):
    half = pieces[0].shape[0] // 2
    copies = []
    for number, (row, count, place) in enumerate(wanted):
        group = []
        for r in range(4):
            if r < 3:
                source = pieces[r].at[row : row + count]
            elif row < half:
                source = pieces[3].at[row : row + count]
            else:
                source = pieces[4].at[row - half : row - half + count]
            group.append(pltpu.make_async_copy(source, place(me ^ r), sems.at[number, r]))
        copies.append(group)
    return copies


def start_all(copies):
    for group in copies:
        for copy in group:
            copy.start()


def wait_group(group):
    for copy in group:
        copy.wait()


def part(a, size):
    return pl.ds(pl.multiple_of(a * size, size), size)


def wanted_qkv(w, which=(0, 1, 2)):
    return [
        (g * LEAST, LEAST, lambda a, i=i: w.at[i, part(a, LEAST)]) for i, g in enumerate(which)
    ]


def wanted_out(w):
    return [
        (3 * LEAST + j * 128, 128, lambda a, j=j: w.at[part(a, 128), j * 512 : (j + 1) * 512])
        for j in range(2)
    ]


def wanted_up(w):
    return [
        (j * LEAST, LEAST, lambda a, j=j: w.at[part(a, LEAST), j * 512 : (j + 1) * 512])
        for j in range(4)
    ]


def wanted_down(w):
    def place(a, rh, j):
        return w.at[pl.ds(pl.multiple_of(a * 512 + rh * 256, 256), 256), j * 512 : (j + 1) * 512]

    return [
        (
            (rh * 2 + j) * LEAST,
            LEAST,
            lambda a, rh=rh, j=j: place(a, rh, j),
        )
        for j in range(2)
        for rh in range(2)
    ]


def dot_nn(left, right):
    return lax.dot_general(left, right, (((1,), (0,)), ((), ())), preferred_element_type=F32)


def dot_nt(left, right):
    return lax.dot_general(left, right, (((1,), (1,)), ((), ())), preferred_element_type=F32)


def dot_tn(left, right):
    return lax.dot_general(left, right, (((0,), (0,)), ((), ())), preferred_element_type=F32)


def mean_last(values):
    return jnp.mean(values, axis=-1, keepdims=True)


def normalize(values):
    centred = values - mean_last(values)
    inverse = lax.rsqrt(mean_last(centred * centred) + EPSILON)
    return centred * inverse, inverse


def norm_back(grad_norm, normal, inverse):
    return inverse * (grad_norm - mean_last(grad_norm) - normal * mean_last(grad_norm * normal))


def column_sum(values):
    return jnp.sum(values.astype(F32), axis=0, keepdims=True)


def pack_kernel(
    core_ref, qkv, out, up, down, keep_a, send_a, keep_u, send_u, keep_d, send_d, sems
):
    core = core_ref[0]
    number = 0
    copies = []
    for target_a, target_u, target_d, half in (
        (send_a, send_u, send_d, 1 - core), (keep_a, keep_u, keep_d, core)
    ):
        for g in range(3):
            for f in range(4):
                columns = pl.ds(pl.multiple_of((g * 4 + f) * 256 + half * 128, 128), 128)
                copies.append(
                    (
                        qkv.at[0, :, columns],
                        target_a.at[g * LEAST : (g + 1) * LEAST, f * 128 : (f + 1) * 128],
                    )
                )
        for j in range(2):
            rows = pl.ds(pl.multiple_of(half * 128, 128), 128)
            copies.append(
                (
                    out.at[0, rows, j * 512 : (j + 1) * 512],
                    target_a.at[3 * LEAST + j * 128 : 3 * LEAST + (j + 1) * 128],
                )
            )
        for j in range(4):
            columns = pl.ds(pl.multiple_of(j * 1024 + half * 512, 512), 512)
            copies.append((up.at[0, :, columns], target_u.at[j * LEAST : (j + 1) * LEAST]))
        for rh in range(2):
            for j in range(2):
                rows = pl.ds(pl.multiple_of(half * 512 + rh * 256, 256), 256)
                at = (rh * 2 + j) * LEAST
                copies.append(
                    (down.at[0, rows, j * 512 : (j + 1) * 512], target_d.at[at : at + LEAST])
                )
    started = []
    for number, (source, target) in enumerate(copies):
        copy = pltpu.make_async_copy(source, target, sems.at[number])
        copy.start()
        started.append(copy)
    for copy in started:
        copy.wait()


def pack_weights(core, qkv, out, up, down):
    return call(
        pack_kernel,
        [kept(4 * LEAST, 512)] * 6,
        core, qkv, out, up, down,
        in_specs=[SCALARS] + [ANYWHERE] * 4,
        out_specs=[ANYWHERE] * 6,
        scratch_shapes=[pltpu.SemaphoreType.DMA((44,))],
        moved=12 << 20,
        limit=16,
        name="pack_weights",
    )


def qkv_kernel(
    me_ref, own_ref, other_ref, gain, bias, bq, bv, w0, w1, w2, w3, w4,
    a_ref, q_ref, k_ref, v_ref, w, sems,
):
    copies = fetches(me_ref[0], (w0, w1, w2, w3, w4), wanted_qkv(w), sems)
    start_all(copies)
    scale = BF16(1.0 / math.sqrt(D // HEADS))
    for m, x_ref in enumerate((own_ref, other_ref)):
        normed = (normalize(x_ref[...].astype(F32))[0] * gain[...] + bias[...]).astype(BF16)
        a_ref[m] = normed
        if m == 0:
            for group in copies:
                wait_group(group)
        q_ref[m] = (dot_nn(normed, w[0]) + bq[...]).astype(BF16) * scale
        k_ref[m] = dot_nn(normed, w[1]).astype(BF16)
        v_ref[m] = (dot_nn(normed, w[2]) + bv[...]).astype(BF16)


def make_qkv(me, own, other, gain, bias, bq, bv, pieces):
    rows = own.shape[0]
    half = D // 2
    return call(
        qkv_kernel,
        [kept(2, rows, D)] + [kept(2, rows, half)] * 3,
        me, own, other, gain, bias, bq, bv, *pieces,
        grid=(1,),
        in_specs=[SCALARS, fixed(rows, D), fixed(rows, D)]
        + [fixed(1, D), fixed(1, D), fixed(1, half), fixed(1, half)]
        + [ANYWHERE] * 5,
        out_specs=[fixed(2, rows, D)] + [fixed(2, rows, half)] * 3,
        scratch_shapes=[pltpu.VMEM((3, D, half), BF16), pltpu.SemaphoreType.DMA((3, 4))],
        flops=4 * rows * D * 3 * half,
        moved=14 << 20,
        name="project_qkv",
    )


def kv_kernel(
    me_ref, own_ref, other_ref, gain, bias, bv, w0, w1, w2, w3, w4,
    a_ref, k_ref, v_ref, w, sems,
):
    copies = fetches(me_ref[0], (w0, w1, w2, w3, w4), wanted_qkv(w, (1, 2)), sems)

    @pl.when(pl.program_id(0) == 0)
    def _():
        start_all(copies)

    for m, x_ref in enumerate((own_ref, other_ref)):
        normed = (normalize(x_ref[...].astype(F32))[0] * gain[...] + bias[...]).astype(BF16)
        a_ref[m] = normed
        if m == 0:

            @pl.when(pl.program_id(0) == 0)
            def _():
                for group in copies:
                    wait_group(group)

        k_ref[m] = dot_nn(normed, w[0]).astype(BF16)
        v_ref[m] = (dot_nn(normed, w[1]) + bv[...]).astype(BF16)


def make_kv(me, own, other, rows, gain, bias, bv, pieces):
    halo = own.shape[0]
    half = D // 2
    row = lambda width: pl.BlockSpec((2, rows, width), lambda i: (0, i, 0))
    flat = pl.BlockSpec((rows, D), lambda i: (i, 0))
    return call(
        kv_kernel,
        [kept(2, halo, D), kept(2, halo, half), kept(2, halo, half)],
        me, own, other, gain, bias, bv, *pieces,
        grid=(halo // rows,),
        in_specs=[SCALARS, flat, flat, fixed(1, D), fixed(1, D), fixed(1, half)] + [ANYWHERE] * 5,
        out_specs=[row(D), row(half), row(half)],
        scratch_shapes=[pltpu.VMEM((2, D, half), BF16), pltpu.SemaphoreType.DMA((2, 4))],
        flops=2 * 2 * halo * D * 2 * half,
        moved=14 << 20,
        name="project_earlier",
    )


def out_kernel(me_ref, o_ref, w0, w1, w2, w3, w4, p_ref, w, sems):
    copies = fetches(me_ref[0], (w0, w1, w2, w3, w4), wanted_out(w), sems)
    start_all(copies)
    for group in copies:
        wait_group(group)
    p_ref[...] = dot_nn(o_ref[0], w[...]).astype(BF16)


def out_other(me, o, pieces):
    _, rows, half = o.shape
    return call(
        out_kernel,
        sds(rows, D),
        me, o, *pieces,
        grid=(1,),
        in_specs=[SCALARS, fixed(1, rows, half)] + [ANYWHERE] * 5,
        out_specs=fixed(rows, D),
        scratch_shapes=[pltpu.VMEM((half, D), BF16), pltpu.SemaphoreType.DMA((2, 4))],
        flops=2 * rows * half * D,
        moved=3 << 20,
        name="out_other",
    )


def middle_kernel(
    me_ref, o_ref, got, x_ref, bo, gain, bias, w0, w1, w2, w3, w4, x1_ref, h_ref, w, sems
):
    copies = fetches(me_ref[0], (w0, w1, w2, w3, w4), wanted_out(w), sems)
    start_all(copies)
    base = x_ref[...].astype(F32) + got[...].astype(F32) + bo[...]
    for group in copies:
        wait_group(group)
    x1 = base + dot_nn(o_ref[0], w[...])
    x1_ref[...] = x1
    h_ref[...] = (normalize(x1)[0] * gain[...] + bias[...]).astype(BF16)


def middle(me, o, got, x, bo, gain, bias, pieces):
    _, rows, half = o.shape
    return call(
        middle_kernel,
        [sds(rows, D, dtype=F32), sds(rows, D)],
        me, o, got, x, bo, gain, bias, *pieces,
        grid=(1,),
        in_specs=[SCALARS, fixed(1, rows, half)]
        + [fixed(rows, D)] * 2
        + [fixed(1, D)] * 3
        + [ANYWHERE] * 5,
        out_specs=[fixed(rows, D)] * 2,
        scratch_shapes=[pltpu.VMEM((half, D), BF16), pltpu.SemaphoreType.DMA((2, 4))],
        flops=2 * rows * half * D,
        moved=8 << 20,
        name="middle",
    )


def gelu_and_slope(u):
    c = math.sqrt(2.0 / math.pi)
    square = u * u
    half = 0.5 + 0.5 * jnp.tanh(u * (c + (c * 0.044715) * square))
    value = u * half
    slope = half + value * (1.0 - half) * (2.0 * c + (6.0 * c * 0.044715) * square)
    return value, slope


def up_kernel(me_ref, h_ref, bu, w0, w1, w2, w3, w4, act_ref, slope_ref, w, sems):
    copies = fetches(me_ref[0], (w0, w1, w2, w3, w4), wanted_up(w), sems)
    step = pl.program_id(0)

    @pl.when(step == 0)
    def _():
        start_all(copies)

    for j in range(4):

        @pl.when(step == j)
        def _(j=j):
            wait_group(copies[j])
            columns = slice(j * 512, (j + 1) * 512)
            rows = h_ref.shape[0]
            piece = min(256, rows)
            for r in range(0, rows, piece):
                u = dot_nn(h_ref[r : r + piece], w[:, columns]) + bu[:, columns]
                value, slope = gelu_and_slope(u)
                act_ref[r : r + piece] = value.astype(BF16)
                slope_ref[r : r + piece] = slope.astype(BF16)


def up(me, h, bu, pieces):
    rows = h.shape[0]
    half = FF // 2
    out = pl.BlockSpec((rows, 512), lambda j: (0, j))
    return call(
        up_kernel,
        [sds(rows, half), kept(rows, half)],
        me, h, bu, *pieces,
        grid=(4,),
        in_specs=[SCALARS, fixed(rows, D), fixed(1, half)] + [ANYWHERE] * 5,
        out_specs=[out, out],
        scratch_shapes=[pltpu.VMEM((D, half), BF16), pltpu.SemaphoreType.DMA((4, 4))],
        flops=2 * rows * half * D,
        moved=9 << 20,
        exps=rows * half,
        name="up",
    )


def down_kernel(me_ref, act, w0, w1, w2, w3, w4, p_ref, w, sems):
    copies = fetches(me_ref[0], (w0, w1, w2, w3, w4), wanted_down(w), sems)
    start_all(copies)
    for j in range(2):
        wait_group(copies[2 * j])
        wait_group(copies[2 * j + 1])
        columns = slice(j * 512, (j + 1) * 512)
        p_ref[:, columns] = dot_nn(act[...], w[:, columns]).astype(BF16)


def down_other(me, act, pieces):
    rows, half = act.shape
    return call(
        down_kernel,
        sds(rows, D),
        me, act, *pieces,
        grid=(1,),
        in_specs=[SCALARS, fixed(rows, half)] + [ANYWHERE] * 5,
        out_specs=fixed(rows, D),
        scratch_shapes=[pltpu.VMEM((half, D), BF16), pltpu.SemaphoreType.DMA((4, 4))],
        flops=2 * rows * half * D,
        moved=7 << 20,
        name="down_other",
    )


def last_kernel(me_ref, act, got, x1, bd, w0, w1, w2, w3, w4, y_ref, w, sems):
    copies = fetches(me_ref[0], (w0, w1, w2, w3, w4), wanted_down(w), sems)
    start_all(copies)
    for j in range(2):
        wait_group(copies[2 * j])
        wait_group(copies[2 * j + 1])
        columns = slice(j * 512, (j + 1) * 512)
        base = x1[:, columns] + got[:, columns].astype(F32) + bd[:, columns]
        y_ref[:, columns] = (base + dot_nn(act[...], w[:, columns])).astype(BF16)


def last(me, act, got, x1, bd, pieces):
    rows, half = act.shape
    return call(
        last_kernel,
        sds(rows, D),
        me, act, got, x1, bd, *pieces,
        grid=(1,),
        in_specs=[SCALARS, fixed(rows, half), fixed(rows, D), fixed(rows, D), fixed(1, D)]
        + [ANYWHERE] * 5,
        out_specs=fixed(rows, D),
        scratch_shapes=[pltpu.VMEM((half, D), BF16), pltpu.SemaphoreType.DMA((4, 4))],
        flops=2 * rows * half * D,
        moved=10 << 20,
        name="down_own",
    )


def lanes_of(rows, low):
    lane = lax.broadcasted_iota(jnp.int32, (rows, LANES), 1)
    return lane < LANES // 2 if low else lane >= LANES // 2


def split3(values):
    first = values.astype(BF16)
    rest = values - first.astype(F32)
    second = rest.astype(BF16)
    third = (rest - second.astype(F32)).astype(BF16)
    return first, second, third


def forward_kernel(
    rows, halo, block,
    word, q_ref, kh_ref, ko_ref, vh_ref, vo_ref, lo_ref, ek_ref, eq_ref, o_ref, e_ref,
):
    lane = lax.broadcasted_iota(jnp.int32, (block, LANES), 1)
    for q0 in range(0, rows, block):
        k0 = max(0, halo + q0 - WIN) // block * block
        k1 = halo + q0 + block
        q = q_ref[0, q0 : q0 + block, :]
        lo = lo_ref[0, q0 : q0 + block, :]
        outs = []
        for t in range(2):
            keep = lanes_of(block, t == 0)
            eq = jnp.broadcast_to(eq_ref[0, t : t + 1, :], (block, LANES))
            qcat = jnp.concatenate([q, eq.astype(BF16)], axis=1)
            tiles = []
            for kb in range(k0, k1, block):
                k = kh_ref[0, kb : kb + block, :] if kb < halo else ko_ref[0, kb - halo : kb - halo + block, :]
                kcat = jnp.concatenate(
                    [jnp.where(keep, k, jnp.zeros_like(k)), ek_ref[kb : kb + block, :]], axis=1
                )
                s = dot_nt(qcat, kcat)
                kidx = lax.broadcasted_iota(jnp.int32, (block, block), 1) + kb
                allowed = kidx >= lo
                if kb + block == k1:
                    qidx = lax.broadcasted_iota(jnp.int32, (block, block), 0) + (halo + q0)
                    allowed = allowed & (kidx <= qidx)
                tiles.append(jnp.where(allowed, s, MASKED))
            top = functools.reduce(jnp.maximum, tiles)
            m = jnp.max(top, axis=1, keepdims=True)
            ps = [jnp.exp(s - m) for s in tiles]
            total = jnp.sum(functools.reduce(jnp.add, ps), axis=1, keepdims=True)
            early = (halo - k0) // block
            pcat = [p.astype(BF16) for p in ps]
            o = dot_nn(jnp.concatenate(pcat[early:], axis=1), vo_ref[0, : q0 + block, :])
            if early > 0:
                o += dot_nn(jnp.concatenate(pcat[:early], axis=1), vh_ref[0, k0:halo, :])
            outs.append(o / total)
            first, second, third = split3(-(m + jnp.log(total)))
            e = jnp.where(lane == 6, first.astype(F32), eq)
            e = jnp.where(lane == 7, second.astype(F32), e)
            e = jnp.where(lane == 8, third.astype(F32), e)
            e_ref[0, t, q0 : q0 + block, :] = e.astype(BF16)
        o_ref[0, q0 : q0 + block, :] = jnp.where(lanes_of(block, True), outs[0], outs[1]).astype(
            BF16
        )


def attend(word, which, q, kh, ko, vh, vo, lo, ek, eq):
    _, rows, width = q.shape
    halo = kh.shape[1]
    pairs = width // LANES
    block = min(256, rows)
    spec = lambda n: pl.BlockSpec((1, n, LANES), lambda p: (which, 0, p))
    count = pairs * 2 * rows * (WIN + block)
    return call(
        functools.partial(forward_kernel, rows, halo, block),
        [sds(1, rows, width), kept(1, 2 * pairs, rows, LANES)],
        word, q, kh, ko, vh, vo, lo, ek, eq,
        grid=(pairs,),
        in_specs=[
            SCALARS,
            spec(rows), spec(halo), spec(rows), spec(halo), spec(rows),
            pl.BlockSpec((1, rows, 1), lambda p: (which, 0, 0)),
            fixed(halo + rows, LANES),
            pl.BlockSpec((1, 2, LANES), lambda p: (p, 0, 0)),
        ],
        out_specs=[
            pl.BlockSpec((1, rows, LANES), lambda p: (0, 0, p)),
            pl.BlockSpec((1, 2, rows, LANES), lambda p: (0, p, 0, 0)),
        ],
        flops=count * 1024,
        moved=6 << 20,
        exps=count,
        name="attention_forward",
    )


def backward_kernel(
    rows, halo, block, begin, end, final,
    word, q_ref, kh_ref, ko_ref, vh_ref, vo_ref, o_ref, do_ref, e_ref, lo_ref, ek_ref, *refs,
):
    acc_ref = refs[-1]
    refs = list(refs[:-1])
    start_ref = refs.pop(0) if begin > 0 else None
    dq_ref = refs.pop(0)
    dkh_ref, dvh_ref = (refs.pop(0), refs.pop(0)) if begin == 0 else (None, None)
    dko_ref, dvo_ref = (refs.pop(0), refs.pop(0)) if final else (None, None)
    q = q_ref[0]
    do = do_ref[0]
    lo = lo_ref[0]
    lane = lax.broadcasted_iota(jnp.int32, (rows, LANES), 1)
    ones = jnp.where(lax.broadcasted_iota(jnp.int32, (block, LANES), 1) < 3, 1.0, 0.0).astype(BF16)
    product = do.astype(F32) * o_ref[0].astype(F32)
    qcats, docats, qts, dots = [], [], [], []
    for t in range(2):
        keep = lanes_of(rows, t == 0)
        delta = jnp.sum(jnp.where(keep, product, 0.0), axis=1, keepdims=True)
        first, second, third = split3(-delta)
        ed = jnp.where(lane == 0, first.astype(F32), 0.0)
        ed = jnp.where(lane == 1, second.astype(F32), ed)
        ed = jnp.where(lane == 2, third.astype(F32), ed)
        qcats.append(jnp.concatenate([q, e_ref[0, t]], axis=1))
        docats.append(jnp.concatenate([do, ed.astype(BF16)], axis=1))
        qts.append(jnp.where(keep, q, jnp.zeros_like(q)))
        dots.append(jnp.where(keep, do, jnp.zeros_like(do)))
    acc_ref[...] = jnp.zeros_like(acc_ref) if start_ref is None else start_ref[0]
    for kb in range(begin, end, block):
        if kb < halo:
            k_in, v_in, dk_out, dv_out, at = kh_ref, vh_ref, dkh_ref, dvh_ref, kb
        else:
            k_in, v_in, dk_out, dv_out, at = ko_ref, vo_ref, dko_ref, dvo_ref, kb - halo
        qlo = max(0, kb - halo)
        qhi = min(rows, -(-(kb + block - 1 + WIN - halo) // block) * block)
        if qhi <= qlo:
            dk_out[0, at : at + block, :] = jnp.zeros((block, LANES), BF16)
            dv_out[0, at : at + block, :] = jnp.zeros((block, LANES), BF16)
            continue
        k = k_in[0, at : at + block, :]
        v = v_in[0, at : at + block, :]
        ek = ek_ref[kb : kb + block, :]
        kidx = lax.broadcasted_iota(jnp.int32, (block, qhi - qlo), 0) + kb
        allowed = kidx >= lo[:, qlo:qhi]
        if kb + block > halo + qlo:
            qidx = lax.broadcasted_iota(jnp.int32, (block, qhi - qlo), 1) + (halo + qlo)
            allowed = allowed & (kidx <= qidx)
        pts, dss, kts = [], [], []
        for t in range(2):
            keep = lanes_of(block, t == 0)
            kt = jnp.where(keep, k, jnp.zeros_like(k))
            vt = jnp.where(keep, v, jnp.zeros_like(v))
            st = dot_nt(jnp.concatenate([kt, ek], axis=1), qcats[t][qlo:qhi])
            pt = jnp.exp(jnp.where(allowed, st, MASKED))
            dpt = dot_nt(jnp.concatenate([vt, ones], axis=1), docats[t][qlo:qhi])
            pts.append(pt.astype(BF16))
            dss.append((pt * dpt).astype(BF16))
            kts.append(kt)
        dv = dot_nn(jnp.concatenate(pts, axis=1), jnp.concatenate([d[qlo:qhi] for d in dots], axis=0))
        dk = dot_nn(jnp.concatenate(dss, axis=1), jnp.concatenate([d[qlo:qhi] for d in qts], axis=0))
        dv_out[0, at : at + block, :] = dv.astype(BF16)
        dk_out[0, at : at + block, :] = dk.astype(BF16)
        acc_ref[:, qlo:qhi] += dot_tn(jnp.concatenate(kts, axis=0), jnp.concatenate(dss, axis=0))
    if final:
        scale = 1.0 / math.sqrt(LANES // 2)
        dq_ref[0] = (acc_ref[...].T * scale).astype(BF16)
    else:
        dq_ref[0] = acc_ref[...]


def attend_back(word, which, q, kh, ko, vh, vo, o, do, e, lo, ek, start=None):
    _, rows, width = q.shape
    halo = kh.shape[1]
    pairs = width // LANES
    block = min(256, rows)
    begin, end, final = (0, halo, False) if start is None else (halo, halo + rows, True)
    spec = lambda n: pl.BlockSpec((1, n, LANES), lambda p: (which, 0, p))
    only = lambda n: pl.BlockSpec((1, n, LANES), lambda p: (0, 0, p))
    sums = pl.BlockSpec((1, LANES, rows), lambda p: (0, p, 0))
    count = pairs * 2 * rows * (WIN + block) * (end - begin) // (halo + rows)
    if final:
        shapes, specs = [sds(1, rows, width)] * 3, [only(rows)] * 3
    else:
        shapes = [sds(1, width, rows, dtype=F32)] + [sds(1, halo, width)] * 2
        specs = [sums, only(halo), only(halo)]
    return call(
        functools.partial(backward_kernel, rows, halo, block, begin, end, final),
        shapes,
        word, q, kh, ko, vh, vo, o, do, e, lo, ek, *([] if start is None else [start]),
        grid=(pairs,),
        in_specs=[
            SCALARS,
            spec(rows), spec(halo), spec(rows), spec(halo), spec(rows), only(rows), spec(rows),
            pl.BlockSpec((1, 2, rows, LANES), lambda p: (0, p, 0, 0)),
            pl.BlockSpec((1, 1, rows), lambda p: (which, 0, 0)),
            fixed(halo + rows, LANES),
        ]
        + ([] if start is None else [sums]),
        out_specs=specs,
        scratch_shapes=[pltpu.VMEM((LANES, rows), F32)],
        flops=count * 2304,
        moved=8 << 20,
        exps=count,
        name="attention_backward",
    )


def act_back_kernel(
    me_ref, own, other, slope_own, slope_other, w0, w1, w2, w3, w4,
    du_own, du_other, sums, w, sems,
):
    copies = fetches(me_ref[0], (w0, w1, w2, w3, w4), wanted_down(w), sems)
    step = pl.program_id(0)

    @pl.when(step == 0)
    def _():
        start_all(copies)
        for group in copies:
            wait_group(group)

    rows = own.shape[0]
    piece = min(256, rows)
    w_part = w[pl.ds(pl.multiple_of(step * 512, 512), 512), :]
    total = jnp.zeros((1, 512), F32)
    for dy, slope, du in ((other, slope_other, du_other), (own, slope_own, du_own)):
        for r in range(0, rows, piece):
            grad = dot_nt(dy[r : r + piece], w_part) * slope[r : r + piece].astype(F32)
            rounded = grad.astype(BF16)
            du[r : r + piece] = rounded
            total += column_sum(rounded)
    sums[...] = jnp.broadcast_to(total, (8, 512))


def act_back(me, own, other, slope_own, slope_other, pieces):
    rows = own.shape[0]
    half = FF // 2
    columns = pl.BlockSpec((rows, 512), lambda j: (0, j))
    return call(
        act_back_kernel,
        [sds(rows, half), sds(rows, half), sds(8, half, dtype=F32)],
        me, own, other, slope_own, slope_other, *pieces,
        grid=(4,),
        in_specs=[SCALARS, fixed(rows, D), fixed(rows, D), columns, columns] + [ANYWHERE] * 5,
        out_specs=[columns, columns, pl.BlockSpec((8, 512), lambda j: (0, j))],
        scratch_shapes=[pltpu.VMEM((half, D), BF16), pltpu.SemaphoreType.DMA((4, 4))],
        flops=4 * rows * half * D,
        moved=16 << 20,
        name="act_back",
    )


def up_back_kernel(me_ref, du, w0, w1, w2, w3, w4, p_ref, w, sems):
    copies = fetches(me_ref[0], (w0, w1, w2, w3, w4), wanted_up(w), sems)
    start_all(copies)
    for group in copies:
        wait_group(group)
    p_ref[...] = dot_nt(du[...], w[...]).astype(BF16)


def up_back_other(me, du, pieces):
    rows, half = du.shape
    return call(
        up_back_kernel,
        sds(rows, D),
        me, du, *pieces,
        grid=(1,),
        in_specs=[SCALARS, fixed(rows, half)] + [ANYWHERE] * 5,
        out_specs=fixed(rows, D),
        scratch_shapes=[pltpu.VMEM((D, half), BF16), pltpu.SemaphoreType.DMA((4, 4))],
        flops=2 * rows * half * D,
        moved=7 << 20,
        name="up_back_other",
    )


def middle_back_kernel(
    me_ref, du, got, x1, dy, gain, w0, w1, w2, w3, w4, dx1_ref, db_ref, sums, w, sems
):
    copies = fetches(me_ref[0], (w0, w1, w2, w3, w4), wanted_up(w), sems)
    start_all(copies)
    normal, inverse = normalize(x1[...])
    for group in copies:
        wait_group(group)
    dh = dot_nt(du[...], w[...]) + got[...].astype(F32)
    top = dy[...].astype(F32)
    dx1 = top + norm_back(dh * gain[...], normal, inverse)
    dx1_ref[...] = dx1
    db = dx1.astype(BF16)
    db_ref[...] = db
    sums[0:1] = column_sum(dh * normal)
    sums[1:2] = column_sum(dh)
    sums[2:3] = column_sum(db)
    sums[3:4] = column_sum(top)
    sums[4:8] = jnp.zeros((4, D), F32)


def middle_back(me, du, got, x1, dy, gain, pieces):
    rows, half = du.shape
    return call(
        middle_back_kernel,
        [sds(rows, D, dtype=F32), sds(rows, D), sds(8, D, dtype=F32)],
        me, du, got, x1, dy, gain, *pieces,
        grid=(1,),
        in_specs=[SCALARS, fixed(rows, half)]
        + [fixed(rows, D)] * 3
        + [fixed(1, D)]
        + [ANYWHERE] * 5,
        out_specs=[fixed(rows, D), fixed(rows, D), fixed(8, D)],
        scratch_shapes=[pltpu.VMEM((D, half), BF16), pltpu.SemaphoreType.DMA((4, 4))],
        flops=2 * rows * half * D,
        moved=14 << 20,
        name="middle_back",
    )


def out_back_kernel(me_ref, own, other, w0, w1, w2, w3, w4, do_ref, w, sems):
    copies = fetches(me_ref[0], (w0, w1, w2, w3, w4), wanted_out(w), sems)
    start_all(copies)
    for group in copies:
        wait_group(group)
    do_ref[0] = dot_nt(own[...], w[...]).astype(BF16)
    do_ref[1] = dot_nt(other[...], w[...]).astype(BF16)


def out_back(me, own, other, pieces):
    rows = own.shape[0]
    half = D // 2
    return call(
        out_back_kernel,
        sds(2, rows, half),
        me, own, other, *pieces,
        grid=(1,),
        in_specs=[SCALARS, fixed(rows, D), fixed(rows, D)] + [ANYWHERE] * 5,
        out_specs=fixed(2, rows, half),
        scratch_shapes=[pltpu.VMEM((half, D), BF16), pltpu.SemaphoreType.DMA((2, 4))],
        flops=4 * rows * half * D,
        moved=4 << 20,
        name="out_back",
    )


def store_parts(step, parts_x, parts_y, send_x, send_y, keep_x, keep_y):
    def put(ref, pieces):
        row = 0
        for piece in pieces:
            ref[0, row : row + piece.shape[0]] = piece
            row += piece.shape[0]

    @pl.when(step < 2)
    def _():
        put(send_x, parts_x)

    @pl.when(step >= 2)
    def _():
        put(keep_x, parts_x)

    @pl.when(step % 2 == 0)
    def _():
        put(send_y, parts_y)

    @pl.when(step % 2 == 1)
    def _():
        put(keep_y, parts_y)


def part_outputs(rows):
    shapes = [kept(2, rows, 512)] * 4
    specs = [
        pl.BlockSpec((1, rows, 512), lambda i, order: (jnp.minimum(i, 1), 0, 0)),
        pl.BlockSpec((1, rows, 512), lambda i, order: (i // 2, 0, 0)),
        pl.BlockSpec((1, rows, 512), lambda i, order: (i // 3, 0, 0)),
        pl.BlockSpec((1, rows, 512), lambda i, order: (i // 3, 0, 0)),
    ]
    return shapes, specs


def down_grad_kernel(order, act_own, act_other, own, other, *outs):
    grad = (dot_tn(act_own[...], own[...]) + dot_tn(act_other[...], other[...])).astype(BF16)
    store_parts(
        pl.program_id(0),
        [grad[:256, :512], grad[:256, 512:]],
        [grad[256:, :512], grad[256:, 512:]],
        *outs,
    )


def down_grad(order, act_own, act_other, own, other):
    rows = own.shape[0]
    shapes, specs = part_outputs(512)
    columns = pl.BlockSpec((rows, 512), lambda i, order: (0, order[i]))
    full = pl.BlockSpec((rows, D), lambda i, order: (0, 0))
    return call(
        down_grad_kernel,
        shapes,
        order, act_own, act_other, own, other,
        grid_spec=pltpu.PrefetchScalarGridSpec(
            num_scalar_prefetch=1,
            grid=(4,),
            in_specs=[columns, columns, full, full],
            out_specs=specs,
        ),
        flops=4 * rows * (FF // 2) * D,
        moved=10 << 20,
        name="down_grad",
    )


def up_grad_kernel(order, h_own, h_other, du_own, du_other, *outs):
    grad = (dot_tn(h_own[...], du_own[...]) + dot_tn(h_other[...], du_other[...])).astype(BF16)
    store_parts(
        pl.program_id(0),
        [grad[:, :512], grad[:, 512:1024]],
        [grad[:, 1024:1536], grad[:, 1536:]],
        *outs,
    )


def up_grad(order, h_own, h_other, du_own, du_other):
    rows = h_own.shape[0]
    half = FF // 2
    shapes, specs = part_outputs(512)
    columns = pl.BlockSpec((rows, 256), lambda i, order: (0, order[i]))
    full = pl.BlockSpec((rows, half), lambda i, order: (0, 0))
    return call(
        up_grad_kernel,
        shapes,
        order, h_own, h_other, du_own, du_other,
        grid_spec=pltpu.PrefetchScalarGridSpec(
            num_scalar_prefetch=1,
            grid=(4,),
            in_specs=[columns, columns, full, full],
            out_specs=specs,
        ),
        flops=4 * rows * half * D,
        moved=14 << 20,
        name="up_grad",
    )


def qkv_grad_kernel(order, a_own, a_halo, *refs):
    o, db, dq, dko, dvo, dkh, dvh = (refs[2 * i : 2 * i + 2] for i in range(7))
    *parts, sums = refs[14:]

    def total(pairs):
        return sum(dot_tn(left[m], right[m][0]) for left, right in pairs for m in range(2)).astype(BF16)

    out_part = (dot_tn(o[0][0], db[0][...]) + dot_tn(o[1][0], db[1][...])).astype(BF16)
    first = [total([(a_own, dq)]), total([(a_own, dko), (a_halo, dkh)])]
    second = [total([(a_own, dvo), (a_halo, dvh)]), out_part[:, :512], out_part[:, 512:]]
    store_parts(pl.program_id(0), first, second, *parts)

    @pl.when(pl.program_id(0) == 0)
    def _():
        sums[0:1] = column_sum(dq[0][0]) + column_sum(dq[1][0])
        sums[1:2] = sum(column_sum(ref[0]) for ref in (*dvo, *dvh))
        sums[2:8] = jnp.zeros((6, sums.shape[1]), F32)


def qkv_grad(order, a_own, a_halo, *grads):
    rows, halo = a_own.shape[1], a_halo.shape[1]
    half = D // 2
    shapes, specs = part_outputs(512)
    full = lambda n: pl.BlockSpec((1, n, half), lambda i, order: (0, 0, 0))
    columns = lambda n: pl.BlockSpec((2, n, 256), lambda i, order: (0, 0, order[i]))
    top = pl.BlockSpec((rows, D), lambda i, order: (0, 0))
    heads = pl.BlockSpec((1, rows, 128), lambda i, order: (0, 0, order[i]))
    return call(
        qkv_grad_kernel,
        shapes + [sds(8, half, dtype=F32)],
        order, a_own, a_halo, *[ref for pair in grads for ref in pair],
        grid_spec=pltpu.PrefetchScalarGridSpec(
            num_scalar_prefetch=1,
            grid=(4,),
            in_specs=[columns(rows), columns(halo), heads, heads, top, top]
            + [full(rows)] * 6
            + [full(halo)] * 4,
            out_specs=specs + [pl.BlockSpec((8, half), lambda i, order: (0, 0))],
        ),
        flops=4 * D * half * (3 * rows + 2 * halo) + 4 * rows * D * half,
        moved=16 << 20,
        name="qkv_grad",
    )


def normed_back_kernel(hops, me_ref, *refs):
    wanted = (1, 2) if hops else (0, 1, 2)
    count = len(wanted)
    grads, a_ref, refs = refs[:count], refs[count], refs[count + 1 :]
    *outs, sums, w, sems = refs[5:]
    got = outs.pop(0) if len(outs) > max(hops, 1) else None
    copies = fetches(me_ref[0], refs[:5], wanted_qkv(w, wanted), sems)
    start_all(copies)
    for group in copies:
        wait_group(group)
    weighted = jnp.zeros((1, D), F32)
    plain = jnp.zeros((1, D), F32)
    rows = outs[0].shape[0] if got is not None else a_ref.shape[1] // max(hops, 1)
    for number in range(max(hops, 1)):
        r = slice(number * rows, (number + 1) * rows)
        da = sum(dot_nt(grad[0, r], w[i]) for i, grad in enumerate(grads))
        weighted += column_sum(da * a_ref[0, r].astype(F32))
        plain += column_sum(da)
        if got is None:
            outs[0][r] = da.astype(BF16)
        else:
            da = da + got[r].astype(F32)
            outs[number][...] = da.astype(outs[number].dtype)
    sums[0:1] = weighted
    sums[1:2] = plain
    sums[2:8] = jnp.zeros((6, D), F32)


def normed_back(me, which, hops, grads, a, pieces, got=None):
    length = a.shape[1]
    rows = length // max(hops, 1)
    half = D // 2
    count = len(grads)
    if got is None:
        outs, out_specs = [sds(length, D)], [fixed(length, D)]
    elif hops:
        outs, out_specs = [sds(rows, D)] * hops, [fixed(rows, D)] * hops
    else:
        outs, out_specs = [sds(rows, D, dtype=F32)], [fixed(rows, D)]
    return call(
        functools.partial(normed_back_kernel, hops),
        outs + [sds(8, D, dtype=F32)],
        me, *grads, a, *pieces, *([] if got is None else [got]),
        grid=(1,),
        in_specs=[SCALARS]
        + [fixed(1, length, half)] * count
        + [pl.BlockSpec((1, length, D), lambda i: (which, 0, 0))]
        + [ANYWHERE] * 5
        + ([] if got is None else [fixed(length, D)]),
        out_specs=out_specs + [fixed(8, D)],
        scratch_shapes=[pltpu.VMEM((count, D, half), BF16), pltpu.SemaphoreType.DMA((count, 4))],
        flops=2 * count * length * half * D,
        moved=8 << 20,
        name="normed_back",
    )


def first_back_kernel(word, da_ref, got, x_ref, dx1, gain, dx_ref, low_ref):
    da = da_ref[...] + got[...].astype(F32)
    normal, inverse = normalize(x_ref[...].astype(F32))
    dx = dx1[...] + norm_back(da * gain[...], normal, inverse)
    dx_ref[...] = dx
    low_ref[...] = dx.astype(BF16)


def first_back(word, da, got, x, dx1, gain):
    rows = da.shape[0]
    return call(
        first_back_kernel,
        [sds(rows, D, dtype=F32), sds(rows, D)],
        word, da, got, x, dx1, gain,
        grid=(1,),
        in_specs=[SCALARS] + [fixed(rows, D)] * 4 + [fixed(1, D)],
        out_specs=[fixed(rows, D), fixed(rows, D)],
        moved=10 << 20,
        name="first_back",
    )


def unpack_down_kernel(core_ref, kept, got, out):
    core = core_ref[0]
    for half, source in ((core, kept), (1 - core, got)):
        for rh in range(2):
            for j in range(2):
                at = (rh * 2 + j) * 256
                rows = pl.ds(pl.multiple_of(half * 512 + rh * 256, 256), 256)
                out[0, rows, j * 512 : (j + 1) * 512] = source[at : at + 256].astype(F32)


def unpack_up_kernel(core_ref, kept, got, out_up):
    core = core_ref[0]
    for half, source in ((core, kept), (1 - core, got)):
        for j in range(4):
            columns = pl.ds(pl.multiple_of(j * 1024 + half * 512, 512), 512)
            out_up[0, :, columns] = source[j * 256 : (j + 1) * 256].astype(F32)


def unpack_qkv_kernel(core_ref, kept_part, got, out, out_out):
    core = core_ref[0]
    for half, source in ((core, kept_part), (1 - core, got)):
        for g in range(3):
            row = (0, 256, 512)[g]
            for f in range(4):
                columns = pl.ds(pl.multiple_of((g * 4 + f) * 256 + half * 128, 128), 128)
                out[0, :, columns] = source[row : row + 256, f * 128 : (f + 1) * 128].astype(F32)
        rows = pl.ds(pl.multiple_of(half * 128, 128), 128)
        for j in range(2):
            out_out[0, rows, j * 512 : (j + 1) * 512] = source[
                768 + j * 128 : 768 + (j + 1) * 128
            ].astype(F32)


def unpack(kernel, core, pieces, shapes, name):
    return call(
        kernel,
        shapes,
        core, *pieces,
        in_specs=[SCALARS] + [INSIDE] * len(pieces),
        out_specs=jax.tree.map(lambda _: INSIDE, shapes),
        moved=10 << 20,
        name=name,
    )


def split_vector(values):
    pieces, offset = [], 0
    for length in (D, D, D, D, D, D, D, FF, D):
        pieces.append(values[offset : offset + length])
        offset += length
    return pieces


def shards(inputs, cotangent, segments, w_qkv, w_out, w_up, w_down, vectors):
    core = lax.axis_index("section")
    column = lax.axis_index("ctx")
    fs = lax.axis_index("fsdp")
    nf = lax.axis_size("fsdp")
    rows = inputs.shape[2]
    reach = (WIN - 1) // rows + 1
    halo = reach * rows
    first_core = core == 0
    me = fs.astype(jnp.int32).reshape(1)
    core_word = core.astype(jnp.int32).reshape(1)
    order = jnp.stack([fs ^ r for r in ROLL]).astype(jnp.int32)

    def pick(here, there):
        return jnp.where(first_core, here, there), jnp.where(first_core, there, here)

    mine = lambda values: lax.dynamic_index_in_dim(values, core, 0, keepdims=False)
    theirs = lambda values: lax.dynamic_index_in_dim(values, 1 - core, 0, keepdims=False)
    x_own, x_other = mine(inputs[:, 0]), theirs(inputs[:, 0])
    keep_a, send_a, keep_u, send_u, keep_d, send_d = pack_weights(
        tie(core_word, x_own), w_qkv, w_out, w_up, w_down
    )
    shard_a = pick(keep_a, swap(send_a))
    later = lambda value: tie(value, shard_a[0])

    both = later(jnp.concatenate(pick(vectors, swap(vectors))))
    near = flip(both, "fsdp", 1)
    low_x = (fs & 1) == 0
    pair = jnp.concatenate([jnp.where(low_x, both, near), jnp.where(low_x, near, both)], 1)
    far = flip(pair, "fsdp", 2)
    low_y = (fs & 2) == 0
    packed = jnp.concatenate([jnp.where(low_y, pair, far), jnp.where(low_y, far, pair)], 1)
    packed = packed.astype(F32)

    shard_u = pick(keep_u, swap(tie(send_u, far)))
    shard_d = pick(keep_d, swap(tie(send_d, far)))
    a0 = Gather(shard_a[0])
    u0 = Gather(shard_u[0], a0.near)
    d0 = Gather(shard_d[0], a0.far)
    a1 = Gather(shard_a[1], d0.near)
    u1 = Gather(shard_u[1], a1.near)
    d1 = Gather(shard_d[1], a1.far)
    weights = ((a0, u0, d0), (a1, u1, d1))

    top = later(cotangent[:, 0])
    top_own, top_other = mine(top), theirs(top)
    marks = later(segments[:, 0])
    starts = jnp.stack([mine(marks), theirs(marks)])
    position = column * rows + jnp.arange(rows, dtype=jnp.int32)
    lo = jnp.maximum(starts, position[None] - (WIN - 1)) - (column * rows - halo)
    lo_column, lo = lo[:, :, None], lo[:, None, :]

    nought = later(jnp.zeros((), jnp.int32))
    key_index = lax.broadcasted_iota(jnp.int32, (halo + rows, LANES), 0) + nought
    lane = lax.broadcasted_iota(jnp.int32, (halo + rows, LANES), 1)
    placed = jnp.where(lane % 2 == 0, key_index // 256 * 256, key_index % 256)
    ek = jnp.where(lane < 6, placed, jnp.where(lane < 9, 1, 0)).astype(BF16)
    local_heads = HEADS // 2
    per_group = local_heads // nf
    local = jnp.arange(local_heads) + nought
    head = (local // per_group) * (2 * per_group) + core * per_group + local % per_group
    slopes = jnp.exp2(-0.5 * (head.astype(F32) + 1.0)) * (4.0 / WIN)
    first, second, third = [values.astype(F32) for values in split3(slopes)]
    eq = jnp.concatenate(
        [
            jnp.stack([first, first, second, second, third, third], 1),
            jnp.zeros((local_heads, LANES - 6), F32),
        ],
        1,
    ).reshape(local_heads // 2, 2, LANES)

    def start_halo(own, *after):
        pieces, block = [], own
        for hop in range(reach):
            block = step_along(tie(block, *after) if hop == 1 else block, "ctx", 1)
            pieces.append(block)
        return pieces

    def finish_halo(pieces, *after):
        own = jnp.concatenate(tie(pieces, *after)[::-1], 0)
        return own, swap(own)

    def return_halo(hops):
        carried = []
        for piece in hops:
            if carried:
                piece = add_bf16(piece, carried[-1])
            carried.append(step_along(piece, "ctx", -1))
        return carried

    def my_half(values, groups):
        view = values.reshape(groups, 2, -1)
        return jnp.where(first_core, view[:, 0], view[:, 1]).reshape(1, -1)

    def widen(values, groups):
        view = values.reshape(groups, 1, -1)
        zero = jnp.zeros_like(view)
        return jnp.where(
            first_core, jnp.concatenate([view, zero], 1), jnp.concatenate([zero, view], 1)
        ).reshape(-1)

    line = Line()
    run = line.run

    def forward(layer, x_own, x_other, first_hops):
        g1, b1, bq, bv, bo, g2, b2, bu, bd = [
            values.reshape(1, -1) for values in split_vector(packed[layer])
        ]
        bq, bv, bu = my_half(bq, nf), my_half(bv, nf), my_half(bu, nf)
        ga, gu, gd = weights[layer]
        wa, wu, wd = ga.pieces, gu.pieces, gd.pieces
        a_own, q, ko, vo = run(
            make_qkv, me, x_own, x_other, g1, b1, bq, bv, wa, after=(ek, eq, lo, lo_column, bu)
        )
        halo_own, halo_other = finish_halo(first_hops, *([] if layer == 0 else [line.token]))
        a_halo, kh, vh = run(
            make_kv, me, halo_own, halo_other, rows, g1, b1, bv, wa
        )
        o_other, e_other = run(attend, me, 1, q, kh, ko, vh, vo, lo_column, ek, eq)
        part = run(out_other, me, o_other, wa, after=(gu.near,) if layer == 0 else ())
        o_own, e_own = run(attend, me, 0, q, kh, ko, vh, vo, lo_column, ek, eq)
        x1, h_own = run(
            middle, me, o_own, swap(part), x_own, bo, g2, b2, wa, after=(gu.near, gd.near)
        )
        o, e = (o_own, o_other), (e_own, e_other)
        h_other = swap(h_own)
        act_own, slope_own = run(up, me, h_own, bu, wu)
        act_other, slope_other = run(up, me, h_other, bu, wu)
        part = run(down_other, me, act_other, wd)
        y = run(last, me, act_own, swap(part), x1, bd, wd)
        stored = (
            x_own, a_own, a_halo, q, kh, ko, vh, vo, o, e, x1, h_own, h_other,
            act_own, slope_own, act_other, slope_other, g1, b1, g2,
        )
        return y, stored

    y0, stored0 = forward(0, x_own, x_other, start_halo(x_own, shard_a[0]))
    y0_other = swap(y0)
    y1, stored1 = forward(1, y0, y0_other, start_halo(y0, a1.near))
    y1_other = swap(y1)

    column_sums = Column()

    def step(block):
        column_sums.step(block, line.token)
        line.also = column_sums.sent

    def backward(layer, top_own, top_other, stored, before=None):
        (
            x_own, a_own, a_halo, q, kh, ko, vh, vo, o, e, x1, h_own, h_other,
            act_own, slope_own, act_other, slope_other, g1, b1, g2,
        ) = stored
        wa, wu, wd = (group.pieces for group in weights[layer])
        du_own, du_other, sums_up = run(
            act_back, me, top_own, top_other, slope_own, slope_other, wd
        )
        got = swap(run(up_back_other, me, du_other, wu))
        if before is not None:
            before[1].third(line.token)
            step(before[0].piece)
        down_part = Scatter(*run(down_grad, order, act_own, act_other, top_own, top_other))
        dx1, db_own, sums_middle = run(middle_back, me, du_own, got, x1, top_own, g2, wu)
        db_other = swap(db_own)
        up_part = Scatter(*run(up_grad, order, h_own, h_other, du_own, du_other))
        do = run(out_back, me, db_own, db_other, wa)
        if before is not None:
            step(before[1].piece)

        def early(m):
            return run(attend_back, me, m, q, kh, ko, vh, vo, o[m], do, e[m], lo, ek)

        def own(m, start):
            return run(attend_back, me, m, q, kh, ko, vh, vo, o[m], do, e[m], lo, ek, start)

        begun_other, dkh_other, dvh_other = early(1)
        part, sums_a = run(normed_back, me, 1, reach, (dkh_other, dvh_other), a_halo, wa)
        got = swap(part)
        down_part.second(line.token)
        line.also = (down_part.half,)
        begun_own, dkh_own, dvh_own = early(0)
        *hops, sums_b = run(normed_back, me, 0, reach, (dkh_own, dvh_own), a_halo, wa, got)
        carried = return_halo(hops)
        up_part.second(line.token)
        down_part.third(line.token)
        line.also = (up_part.half,)
        if before is not None:
            step(down_part.piece)
            line.also += (up_part.half,)
        dq_other, dko_other, dvo_other = own(1, begun_other)
        part, sums_c = run(normed_back, me, 1, 0, (dq_other, dko_other, dvo_other), a_own, wa)
        got = swap(part)
        dq_own, dko_own, dvo_own = own(0, begun_own)
        if before is not None:
            up_part.third(line.token)
            step(up_part.piece)
        *parts, sums_qkv = run(
            qkv_grad, order, a_own, a_halo, o, (db_own, db_other), (dq_own, dq_other),
            (dko_own, dko_other), (dvo_own, dvo_other), (dkh_own, dkh_other),
            (dvh_own, dvh_other),
        )
        qkv_part = Scatter(*parts)
        da, sums_d = run(normed_back, me, 0, 0, (dq_own, dko_own, dvo_own), a_own, wa, got)
        if before is None:
            up_part.third(line.token)
        else:
            step(None)
        qkv_part.second(line.token)
        dx, dx_low = run(
            first_back, me, da, carried[-1], x_own, dx1, g1, after=(qkv_part.half,)
        )
        if before is None:
            step(down_part.piece)
        else:
            qkv_part.third()
            step(qkv_part.piece)
            step(None)
            step(None)
            step(None)
        plain = sums_a[1] + sums_b[1] + sums_c[1] + sums_d[1]
        weighted = sums_a[0] + sums_b[0] + sums_c[0] + sums_d[0]
        vector = jnp.concatenate(
            [
                (weighted - b1[0] * plain) / g1[0], plain, widen(sums_qkv[0], nf),
                widen(sums_qkv[1], nf), sums_middle[2], sums_middle[0], sums_middle[1],
                widen(sums_up[0], nf), sums_middle[3],
            ]
        )
        return dx, dx_low, up_part, qkv_part, vector

    _, dx1, up1, qkv1, vector1 = backward(1, top_own, top_other, stored1)
    dx1_other = swap(dx1)
    dx0, _, _, _, vector0 = backward(0, dx1, dx1_other, stored0, (up1, qkv1))
    dx0_other = swap(dx0)
    down1_sum, up1_sum, qkv1_sum, down0_sum, up0_sum, qkv0_sum = column_sums.sums

    def by_micro(own, other):
        return jnp.where(first_core, jnp.stack([own, other]), jnp.stack([other, own]))

    activations = jnp.where(first_core, by_micro(y0, y0_other), by_micro(y1, y1_other))
    input_grad = jnp.where(
        first_core, by_micro(dx0, dx0_other), by_micro(dx1, dx1_other).astype(F32)
    )

    def exchange(first, second):
        kept, sent = pick(first, second)
        return kept, swap(sent)

    size = D // nf
    grad_down = unpack(
        unpack_down_kernel, core_word, exchange(down0_sum, down1_sum),
        sds(1, FF // nf, D, dtype=F32), "unpack_down",
    )
    grad_up = unpack(
        unpack_up_kernel, core_word, exchange(up0_sum, up1_sum),
        sds(1, size, FF, dtype=F32), "unpack_up",
    )
    grad_qkv, grad_out = unpack(
        unpack_qkv_kernel, core_word, exchange(qkv0_sum, qkv1_sum),
        [sds(1, size, 3 * D, dtype=F32), sds(1, size, D, dtype=F32)], "unpack_qkv",
    )
    summed = sum_all(jnp.stack([vector0, vector1]))
    length = summed.shape[1] // nf
    grad_vectors = lax.dynamic_slice(summed, (core, fs * length), (1, length))
    return (
        activations[None, :, None], input_grad[None, :, None],
        grad_qkv, grad_out, grad_up, grad_down, grad_vectors,
    )


def solution(mesh):
    placed = (
        P(None, "fsdp", "ctx", None),
        P(None, "fsdp", "ctx", None),
        P(None, "fsdp", "ctx"),
        P("section", "fsdp", None),
        P("section", "fsdp", None),
        P("section", "fsdp", None),
        P("section", "fsdp", None),
        P("section", "fsdp"),
    )
    return jax.shard_map(
        shards,
        mesh=mesh,
        in_specs=placed,
        out_specs=(
            P("section", None, "fsdp", "ctx", None),
            P("section", None, "fsdp", "ctx", None),
            P("section", "fsdp", None),
            P("section", "fsdp", None),
            P("section", "fsdp", None),
            P("section", "fsdp", None),
            P("section", "fsdp"),
        ),
        check_vma=False,
    )
```

```python
import functools
import math

import jax
import jax.numpy as jnp
from jax import lax
from jax.experimental import pallas as pl
from jax.experimental.pallas import tpu as pltpu
from jax.sharding import PartitionSpec as P

D = 1024
HEADS = 16
FF = 4096
WIN = 1024

EPSILON = 1e-05
F32 = jnp.float32
BF16 = jnp.bfloat16
LANES = 128
MASKED = -1e30


LEAST = 256
ROLL = (3, 1, 2, 0)


def flip(block, axis, bit):
    count = lax.axis_size(axis)
    return lax.ppermute(block, axis, [(i, i ^ bit) for i in range(count)])


def step_along(block, axis, distance):
    devices = range(lax.axis_size(axis))
    route = [(i - distance, i) for i in devices if i - distance in devices]
    return lax.ppermute(block, axis, route)


def swap(block):
    return flip(block, "section", 1)


def tie(value, *after):
    return lax.optimization_barrier((value, after))[0]


class Gather:
    def __init__(self, shard, *after, then=()):
        shard = tie(shard, *after) if after else shard
        half = shard.shape[0] // 2
        self.near = flip(shard, "fsdp", 1), flip(shard, "fsdp", 2)
        from_x, from_y = tie(self.near, *then) if then else self.near
        self.far = flip(from_x[:half], "fsdp", 2), flip(from_y[half:], "fsdp", 1)
        self.pieces = (shard, *self.near, *self.far)


def add_bf16(*terms):
    return sum(term.astype(F32) for term in terms).astype(BF16)


class Scatter:
    def __init__(self, send_x, send_y, keep_x, keep_y):
        self.near = flip(send_x, "fsdp", 1), flip(send_y, "fsdp", 2)
        self.keep = keep_x, keep_y

    def second(self, *after):
        (got_x, got_y), (keep_x, keep_y) = tie(self.near, *after), self.keep
        self.half = add_bf16(keep_x[0], got_x[0]), add_bf16(keep_y[0], got_y[0])
        self.far = flip(self.half[0], "fsdp", 2), flip(self.half[1], "fsdp", 1)

    def third(self, *after):
        far_x, far_y = tie(self.far, *after)
        (got_x, got_y), (keep_x, keep_y) = self.near, self.keep
        self.piece = jnp.concatenate(
            [add_bf16(keep_x[1], got_x[1], far_x), add_bf16(keep_y[1], got_y[1], far_y)]
        )


class Column:
    def __init__(self):
        self.line = lax.axis_size("ctx") == 4
        me = lax.axis_index("ctx")
        self.inner = (me == 1) | (me == 2)
        self.block = self.half = self.total = self.outer_got = self.inner_got = None
        self.sums = []
        self.sent = ()

    def step(self, block, *after):
        if not self.line:
            if block is not None:
                self.sums.append(lax.psum(block, "ctx"))
            return
        outer_got, inner_got, block = tie((self.outer_got, self.inner_got, block), *after)
        half = total = None
        if self.block is not None:
            half = add_bf16(self.block, outer_got[: self.block.shape[0]])
        if self.half is not None:
            total = add_bf16(self.half, inner_got)
        if self.total is not None:
            outer_sum = outer_got[: self.total.shape[0]]
            self.sums.append(jnp.where(self.inner, self.total, outer_sum))
        self.block, self.half, self.total = block, half, total
        self.sent = ()
        if block is not None or total is not None:
            sent = total if block is None else block
            if block is not None and total is not None:
                rows = max(total.shape[0], block.shape[0])
                fill = lambda part: jnp.pad(part, ((0, rows - part.shape[0]), (0, 0)))
                sent = jnp.where(self.inner, fill(total), fill(block))
            self.outer_got = flip(sent, "ctx", 1)
            self.sent += (sent,)
        if half is not None:
            self.inner_got = lax.ppermute(half, "ctx", [(1, 2), (2, 1)])
            self.sent += (half,)


class Line:
    def __init__(self):
        self.token = ()
        self.also = ()

    def run(self, kernel, word, *args, after=()):
        word = tie(word, self.token, self.also, after)
        self.also = ()
        out = kernel(word, *args)
        self.token = out[0] if isinstance(out, (list, tuple)) else out
        return out


def sum_all(block):
    for axis in ("section", "fsdp"):
        bit = 1
        while bit < lax.axis_size(axis):
            block = block + flip(block, axis, bit)
            bit *= 2
    return lax.psum(block, "ctx")


def call(kernel, out_shape, *operands, limit=32, flops=0, moved=0, exps=0, name=None, **rest):
    return pl.pallas_call(
        kernel,
        out_shape=out_shape,
        compiler_params=pltpu.CompilerParams(vmem_limit_bytes=limit * 1024 * 1024),
        cost_estimate=pl.CostEstimate(flops=flops, bytes_accessed=moved, transcendentals=exps),
        name=name,
        **rest,
    )(*operands)


def sds(*shape, dtype=BF16):
    return jax.ShapeDtypeStruct(shape, dtype)


def kept(*shape, dtype=BF16):
    return pltpu.HBM(shape, dtype)


ANYWHERE = pl.BlockSpec(memory_space=pltpu.HBM)
SCALARS = pl.BlockSpec(memory_space=pltpu.SMEM)
INSIDE = pl.BlockSpec(memory_space=pltpu.VMEM)


def fixed(*shape):
    return pl.BlockSpec(shape, lambda *_: (0,) * len(shape))


def fetches(me, pieces, wanted, sems):
    half = pieces[0].shape[0] // 2
    copies = []
    for number, (row, count, place) in enumerate(wanted):
        group = []
        for r in range(4):
            if r < 3:
                source = pieces[r].at[row : row + count]
            elif row < half:
                source = pieces[3].at[row : row + count]
            else:
                source = pieces[4].at[row - half : row - half + count]
            group.append(pltpu.make_async_copy(source, place(me ^ r), sems.at[number, r]))
        copies.append(group)
    return copies


def start_all(copies):
    for group in copies:
        for copy in group:
            copy.start()


def wait_group(group):
    for copy in group:
        copy.wait()


def part(a, size):
    return pl.ds(pl.multiple_of(a * size, size), size)


def wanted_qkv(w, which=(0, 1, 2)):
    return [
        (g * LEAST, LEAST, lambda a, i=i: w.at[i, part(a, LEAST)]) for i, g in enumerate(which)
    ]


def wanted_out(w):
    return [
        (3 * LEAST + j * 128, 128, lambda a, j=j: w.at[part(a, 128), j * 512 : (j + 1) * 512])
        for j in range(2)
    ]


def wanted_up(w):
    return [
        (j * LEAST, LEAST, lambda a, j=j: w.at[part(a, LEAST), j * 512 : (j + 1) * 512])
        for j in range(4)
    ]


def wanted_down(w):
    def place(a, rh, j):
        return w.at[pl.ds(pl.multiple_of(a * 512 + rh * 256, 256), 256), j * 512 : (j + 1) * 512]

    return [
        (
            (rh * 2 + j) * LEAST,
            LEAST,
            lambda a, rh=rh, j=j: place(a, rh, j),
        )
        for j in range(2)
        for rh in range(2)
    ]


def dot_nn(left, right):
    return lax.dot_general(left, right, (((1,), (0,)), ((), ())), preferred_element_type=F32)


def dot_nt(left, right):
    return lax.dot_general(left, right, (((1,), (1,)), ((), ())), preferred_element_type=F32)


def dot_tn(left, right):
    return lax.dot_general(left, right, (((0,), (0,)), ((), ())), preferred_element_type=F32)


def mean_last(values):
    return jnp.mean(values, axis=-1, keepdims=True)


def normalize(values):
    centred = values - mean_last(values)
    inverse = lax.rsqrt(mean_last(centred * centred) + EPSILON)
    return centred * inverse, inverse


def norm_back(grad_norm, normal, inverse):
    return inverse * (grad_norm - mean_last(grad_norm) - normal * mean_last(grad_norm * normal))


def column_sum(values):
    return jnp.sum(values.astype(F32), axis=0, keepdims=True)


def pack_kernel(
    core_ref, qkv, out, up, down, keep_a, send_a, keep_u, send_u, keep_d, send_d, sems
):
    core = core_ref[0]
    number = 0
    copies = []
    for target_a, target_u, target_d, half in (
        (send_a, send_u, send_d, 1 - core), (keep_a, keep_u, keep_d, core)
    ):
        for g in range(3):
            for f in range(4):
                columns = pl.ds(pl.multiple_of((g * 4 + f) * 256 + half * 128, 128), 128)
                copies.append(
                    (
                        qkv.at[0, :, columns],
                        target_a.at[g * LEAST : (g + 1) * LEAST, f * 128 : (f + 1) * 128],
                    )
                )
        for j in range(2):
            rows = pl.ds(pl.multiple_of(half * 128, 128), 128)
            copies.append(
                (
                    out.at[0, rows, j * 512 : (j + 1) * 512],
                    target_a.at[3 * LEAST + j * 128 : 3 * LEAST + (j + 1) * 128],
                )
            )
        for j in range(4):
            columns = pl.ds(pl.multiple_of(j * 1024 + half * 512, 512), 512)
            copies.append((up.at[0, :, columns], target_u.at[j * LEAST : (j + 1) * LEAST]))
        for rh in range(2):
            for j in range(2):
                rows = pl.ds(pl.multiple_of(half * 512 + rh * 256, 256), 256)
                at = (rh * 2 + j) * LEAST
                copies.append(
                    (down.at[0, rows, j * 512 : (j + 1) * 512], target_d.at[at : at + LEAST])
                )
    started = []
    for number, (source, target) in enumerate(copies):
        copy = pltpu.make_async_copy(source, target, sems.at[number])
        copy.start()
        started.append(copy)
    for copy in started:
        copy.wait()


def pack_weights(core, qkv, out, up, down):
    return call(
        pack_kernel,
        [kept(4 * LEAST, 512)] * 6,
        core, qkv, out, up, down,
        in_specs=[SCALARS] + [ANYWHERE] * 4,
        out_specs=[ANYWHERE] * 6,
        scratch_shapes=[pltpu.SemaphoreType.DMA((44,))],
        moved=12 << 20,
        limit=16,
        name="pack_weights",
    )


def qkv_kernel(
    me_ref, own_ref, other_ref, gain, bias, bq, bv, w0, w1, w2, w3, w4,
    a_ref, q_ref, k_ref, v_ref, w, sems,
):
    copies = fetches(me_ref[0], (w0, w1, w2, w3, w4), wanted_qkv(w), sems)
    start_all(copies)
    scale = BF16(1.0 / math.sqrt(D // HEADS))
    for m, x_ref in enumerate((own_ref, other_ref)):
        normed = (normalize(x_ref[...].astype(F32))[0] * gain[...] + bias[...]).astype(BF16)
        a_ref[m] = normed
        if m == 0:
            for group in copies:
                wait_group(group)
        q_ref[m] = (dot_nn(normed, w[0]) + bq[...]).astype(BF16) * scale
        k_ref[m] = dot_nn(normed, w[1]).astype(BF16)
        v_ref[m] = (dot_nn(normed, w[2]) + bv[...]).astype(BF16)


def make_qkv(me, own, other, gain, bias, bq, bv, pieces):
    rows = own.shape[0]
    half = D // 2
    return call(
        qkv_kernel,
        [kept(2, rows, D)] + [kept(2, rows, half)] * 3,
        me, own, other, gain, bias, bq, bv, *pieces,
        grid=(1,),
        in_specs=[SCALARS, fixed(rows, D), fixed(rows, D)]
        + [fixed(1, D), fixed(1, D), fixed(1, half), fixed(1, half)]
        + [ANYWHERE] * 5,
        out_specs=[fixed(2, rows, D)] + [fixed(2, rows, half)] * 3,
        scratch_shapes=[pltpu.VMEM((3, D, half), BF16), pltpu.SemaphoreType.DMA((3, 4))],
        flops=4 * rows * D * 3 * half,
        moved=14 << 20,
        name="project_qkv",
    )


def kv_kernel(me_ref, own_ref, other_ref, gain, bias, bv, w0, w1, w2, w3, w4, *rest):
    a_ref, k_ref, v_ref, w, sems = rest[-5:]
    copies = fetches(me_ref[0], (w0, w1, w2, w3, w4), wanted_qkv(w, (1, 2)), sems)
    start_all(copies)
    for m, x_ref in enumerate((own_ref, other_ref)):
        normed = (normalize(x_ref[...].astype(F32))[0] * gain[...] + bias[...]).astype(BF16)
        a_ref[m] = normed
        if m == 0:
            for group in copies:
                wait_group(group)
        k_ref[m] = dot_nn(normed, w[0]).astype(BF16)
        v_ref[m] = (dot_nn(normed, w[1]) + bv[...]).astype(BF16)


def make_kv(me, own, other, hops, at, earlier, gain, bias, bv, pieces):
    rows = own.shape[0]
    halo = hops * rows
    half = D // 2
    row = lambda width: pl.BlockSpec((2, rows, width), lambda i: (0, at, 0))
    first = 11
    return call(
        kv_kernel,
        [kept(2, halo, D), kept(2, halo, half), kept(2, halo, half)],
        me, own, other, gain, bias, bv, *pieces, *earlier,
        grid=(1,),
        in_specs=[SCALARS, fixed(rows, D), fixed(rows, D), fixed(1, D), fixed(1, D), fixed(1, half)]
        + [ANYWHERE] * 5
        + [ANYWHERE] * len(earlier),
        out_specs=[row(D), row(half), row(half)],
        input_output_aliases={first + i: i for i in range(len(earlier))},
        scratch_shapes=[pltpu.VMEM((2, D, half), BF16), pltpu.SemaphoreType.DMA((2, 4))],
        flops=2 * 2 * rows * D * 2 * half,
        moved=8 << 20,
        name="project_earlier",
    )


def out_kernel(me_ref, o_ref, w0, w1, w2, w3, w4, p_ref, w, sems):
    copies = fetches(me_ref[0], (w0, w1, w2, w3, w4), wanted_out(w), sems)
    start_all(copies)
    for group in copies:
        wait_group(group)
    p_ref[...] = dot_nn(o_ref[0], w[...]).astype(BF16)


def out_other(me, o, pieces):
    _, rows, half = o.shape
    return call(
        out_kernel,
        sds(rows, D),
        me, o, *pieces,
        grid=(1,),
        in_specs=[SCALARS, fixed(1, rows, half)] + [ANYWHERE] * 5,
        out_specs=fixed(rows, D),
        scratch_shapes=[pltpu.VMEM((half, D), BF16), pltpu.SemaphoreType.DMA((2, 4))],
        flops=2 * rows * half * D,
        moved=3 << 20,
        name="out_other",
    )


def middle_kernel(
    me_ref, o_ref, got, x_ref, bo, gain, bias, w0, w1, w2, w3, w4, x1_ref, h_ref, w, sems
):
    copies = fetches(me_ref[0], (w0, w1, w2, w3, w4), wanted_out(w), sems)
    start_all(copies)
    base = x_ref[...].astype(F32) + got[...].astype(F32) + bo[...]
    for group in copies:
        wait_group(group)
    x1 = base + dot_nn(o_ref[0], w[...])
    x1_ref[...] = x1
    h_ref[...] = (normalize(x1)[0] * gain[...] + bias[...]).astype(BF16)


def middle(me, o, got, x, bo, gain, bias, pieces):
    _, rows, half = o.shape
    return call(
        middle_kernel,
        [sds(rows, D, dtype=F32), sds(rows, D)],
        me, o, got, x, bo, gain, bias, *pieces,
        grid=(1,),
        in_specs=[SCALARS, fixed(1, rows, half)]
        + [fixed(rows, D)] * 2
        + [fixed(1, D)] * 3
        + [ANYWHERE] * 5,
        out_specs=[fixed(rows, D)] * 2,
        scratch_shapes=[pltpu.VMEM((half, D), BF16), pltpu.SemaphoreType.DMA((2, 4))],
        flops=2 * rows * half * D,
        moved=8 << 20,
        name="middle",
    )


def gelu_and_slope(u):
    c = math.sqrt(2.0 / math.pi)
    square = u * u
    half = 0.5 + 0.5 * jnp.tanh(u * (c + (c * 0.044715) * square))
    value = u * half
    slope = half + value * (1.0 - half) * (2.0 * c + (6.0 * c * 0.044715) * square)
    return value, slope


def up_kernel(me_ref, h_ref, bu, w0, w1, w2, w3, w4, act_ref, slope_ref, w, sems):
    copies = fetches(me_ref[0], (w0, w1, w2, w3, w4), wanted_up(w), sems)
    step = pl.program_id(0)

    @pl.when(step == 0)
    def _():
        start_all(copies)

    for j in range(4):

        @pl.when(step == j)
        def _(j=j):
            wait_group(copies[j])
            columns = slice(j * 512, (j + 1) * 512)
            rows = h_ref.shape[0]
            piece = min(256, rows)
            for r in range(0, rows, piece):
                u = dot_nn(h_ref[r : r + piece], w[:, columns]) + bu[:, columns]
                value, slope = gelu_and_slope(u)
                act_ref[r : r + piece] = value.astype(BF16)
                slope_ref[r : r + piece] = slope.astype(BF16)


def up(me, h, bu, pieces):
    rows = h.shape[0]
    half = FF // 2
    out = pl.BlockSpec((rows, 512), lambda j: (0, j))
    return call(
        up_kernel,
        [sds(rows, half), kept(rows, half)],
        me, h, bu, *pieces,
        grid=(4,),
        in_specs=[SCALARS, fixed(rows, D), fixed(1, half)] + [ANYWHERE] * 5,
        out_specs=[out, out],
        scratch_shapes=[pltpu.VMEM((D, half), BF16), pltpu.SemaphoreType.DMA((4, 4))],
        flops=2 * rows * half * D,
        moved=9 << 20,
        exps=rows * half,
        name="up",
    )


def down_kernel(me_ref, act, w0, w1, w2, w3, w4, p_ref, w, sems):
    copies = fetches(me_ref[0], (w0, w1, w2, w3, w4), wanted_down(w), sems)
    start_all(copies)
    for j in range(2):
        wait_group(copies[2 * j])
        wait_group(copies[2 * j + 1])
        columns = slice(j * 512, (j + 1) * 512)
        p_ref[:, columns] = dot_nn(act[...], w[:, columns]).astype(BF16)


def down_other(me, act, pieces):
    rows, half = act.shape
    return call(
        down_kernel,
        sds(rows, D),
        me, act, *pieces,
        grid=(1,),
        in_specs=[SCALARS, fixed(rows, half)] + [ANYWHERE] * 5,
        out_specs=fixed(rows, D),
        scratch_shapes=[pltpu.VMEM((half, D), BF16), pltpu.SemaphoreType.DMA((4, 4))],
        flops=2 * rows * half * D,
        moved=7 << 20,
        name="down_other",
    )


def last_kernel(me_ref, act, got, x1, bd, w0, w1, w2, w3, w4, y_ref, w, sems):
    copies = fetches(me_ref[0], (w0, w1, w2, w3, w4), wanted_down(w), sems)
    start_all(copies)
    for j in range(2):
        wait_group(copies[2 * j])
        wait_group(copies[2 * j + 1])
        columns = slice(j * 512, (j + 1) * 512)
        base = x1[:, columns] + got[:, columns].astype(F32) + bd[:, columns]
        y_ref[:, columns] = (base + dot_nn(act[...], w[:, columns])).astype(BF16)


def last(me, act, got, x1, bd, pieces):
    rows, half = act.shape
    return call(
        last_kernel,
        sds(rows, D),
        me, act, got, x1, bd, *pieces,
        grid=(1,),
        in_specs=[SCALARS, fixed(rows, half), fixed(rows, D), fixed(rows, D), fixed(1, D)]
        + [ANYWHERE] * 5,
        out_specs=fixed(rows, D),
        scratch_shapes=[pltpu.VMEM((half, D), BF16), pltpu.SemaphoreType.DMA((4, 4))],
        flops=2 * rows * half * D,
        moved=10 << 20,
        name="down_own",
    )


def lanes_of(rows, low):
    lane = lax.broadcasted_iota(jnp.int32, (rows, LANES), 1)
    return lane < LANES // 2 if low else lane >= LANES // 2


def split3(values):
    first = values.astype(BF16)
    rest = values - first.astype(F32)
    second = rest.astype(BF16)
    third = (rest - second.astype(F32)).astype(BF16)
    return first, second, third


def forward_kernel(
    rows, halo, block,
    word, q_ref, kh_ref, ko_ref, vh_ref, vo_ref, lo_ref, ek_ref, eq_ref, o_ref, e_ref,
):
    lane = lax.broadcasted_iota(jnp.int32, (block, LANES), 1)
    for q0 in range(0, rows, block):
        k0 = max(0, halo + q0 - WIN) // block * block
        k1 = halo + q0 + block
        q = q_ref[0, q0 : q0 + block, :]
        lo = lo_ref[0, q0 : q0 + block, :]
        outs = []
        for t in range(2):
            keep = lanes_of(block, t == 0)
            eq = jnp.broadcast_to(eq_ref[0, t : t + 1, :], (block, LANES))
            qcat = jnp.concatenate([q, eq.astype(BF16)], axis=1)
            tiles = []
            for kb in range(k0, k1, block):
                k = kh_ref[0, kb : kb + block, :] if kb < halo else ko_ref[0, kb - halo : kb - halo + block, :]
                kcat = jnp.concatenate(
                    [jnp.where(keep, k, jnp.zeros_like(k)), ek_ref[kb : kb + block, :]], axis=1
                )
                s = dot_nt(qcat, kcat)
                kidx = lax.broadcasted_iota(jnp.int32, (block, block), 1) + kb
                allowed = kidx >= lo
                if kb + block == k1:
                    qidx = lax.broadcasted_iota(jnp.int32, (block, block), 0) + (halo + q0)
                    allowed = allowed & (kidx <= qidx)
                tiles.append(jnp.where(allowed, s, MASKED))
            top = functools.reduce(jnp.maximum, tiles)
            m = jnp.max(top, axis=1, keepdims=True)
            ps = [jnp.exp(s - m) for s in tiles]
            total = jnp.sum(functools.reduce(jnp.add, ps), axis=1, keepdims=True)
            early = (halo - k0) // block
            pcat = [p.astype(BF16) for p in ps]
            o = dot_nn(jnp.concatenate(pcat[early:], axis=1), vo_ref[0, : q0 + block, :])
            if early > 0:
                o += dot_nn(jnp.concatenate(pcat[:early], axis=1), vh_ref[0, k0:halo, :])
            outs.append(o / total)
            first, second, third = split3(-(m + jnp.log(total)))
            e = jnp.where(lane == 6, first.astype(F32), eq)
            e = jnp.where(lane == 7, second.astype(F32), e)
            e = jnp.where(lane == 8, third.astype(F32), e)
            e_ref[0, t, q0 : q0 + block, :] = e.astype(BF16)
        o_ref[0, q0 : q0 + block, :] = jnp.where(lanes_of(block, True), outs[0], outs[1]).astype(
            BF16
        )


def attend(word, which, q, kh, ko, vh, vo, lo, ek, eq):
    _, rows, width = q.shape
    halo = kh.shape[1]
    pairs = width // LANES
    block = min(256, rows)
    spec = lambda n: pl.BlockSpec((1, n, LANES), lambda p: (which, 0, p))
    count = pairs * 2 * rows * (WIN + block)
    return call(
        functools.partial(forward_kernel, rows, halo, block),
        [sds(1, rows, width), kept(1, 2 * pairs, rows, LANES)],
        word, q, kh, ko, vh, vo, lo, ek, eq,
        grid=(pairs,),
        in_specs=[
            SCALARS,
            spec(rows), spec(halo), spec(rows), spec(halo), spec(rows),
            pl.BlockSpec((1, rows, 1), lambda p: (which, 0, 0)),
            fixed(halo + rows, LANES),
            pl.BlockSpec((1, 2, LANES), lambda p: (p, 0, 0)),
        ],
        out_specs=[
            pl.BlockSpec((1, rows, LANES), lambda p: (0, 0, p)),
            pl.BlockSpec((1, 2, rows, LANES), lambda p: (0, p, 0, 0)),
        ],
        flops=count * 1024,
        moved=6 << 20,
        exps=count,
        name="attention_forward",
    )


def backward_kernel(
    rows, halo, block, begin, end, final,
    word, q_ref, kh_ref, ko_ref, vh_ref, vo_ref, o_ref, do_ref, e_ref, lo_ref, ek_ref, *refs,
):
    acc_ref = refs[-1]
    refs = list(refs[:-1])
    start_ref = refs.pop(0) if begin > 0 else None
    dq_ref = refs.pop(0)
    dkh_ref, dvh_ref = (refs.pop(0), refs.pop(0)) if begin == 0 else (None, None)
    dko_ref, dvo_ref = (refs.pop(0), refs.pop(0)) if final else (None, None)
    q = q_ref[0]
    do = do_ref[0]
    lo = lo_ref[0]
    lane = lax.broadcasted_iota(jnp.int32, (rows, LANES), 1)
    ones = jnp.where(lax.broadcasted_iota(jnp.int32, (block, LANES), 1) < 3, 1.0, 0.0).astype(BF16)
    product = do.astype(F32) * o_ref[0].astype(F32)
    qcats, docats, qts, dots = [], [], [], []
    for t in range(2):
        keep = lanes_of(rows, t == 0)
        delta = jnp.sum(jnp.where(keep, product, 0.0), axis=1, keepdims=True)
        first, second, third = split3(-delta)
        ed = jnp.where(lane == 0, first.astype(F32), 0.0)
        ed = jnp.where(lane == 1, second.astype(F32), ed)
        ed = jnp.where(lane == 2, third.astype(F32), ed)
        qcats.append(jnp.concatenate([q, e_ref[0, t]], axis=1))
        docats.append(jnp.concatenate([do, ed.astype(BF16)], axis=1))
        qts.append(jnp.where(keep, q, jnp.zeros_like(q)))
        dots.append(jnp.where(keep, do, jnp.zeros_like(do)))
    acc_ref[...] = jnp.zeros_like(acc_ref) if start_ref is None else start_ref[0]
    for kb in range(begin, end, block):
        if kb < halo:
            k_in, v_in, dk_out, dv_out, at = kh_ref, vh_ref, dkh_ref, dvh_ref, kb
        else:
            k_in, v_in, dk_out, dv_out, at = ko_ref, vo_ref, dko_ref, dvo_ref, kb - halo
        qlo = max(0, kb - halo)
        qhi = min(rows, -(-(kb + block - 1 + WIN - halo) // block) * block)
        if qhi <= qlo:
            dk_out[0, at : at + block, :] = jnp.zeros((block, LANES), BF16)
            dv_out[0, at : at + block, :] = jnp.zeros((block, LANES), BF16)
            continue
        k = k_in[0, at : at + block, :]
        v = v_in[0, at : at + block, :]
        ek = ek_ref[kb : kb + block, :]
        kidx = lax.broadcasted_iota(jnp.int32, (block, qhi - qlo), 0) + kb
        allowed = kidx >= lo[:, qlo:qhi]
        if kb + block > halo + qlo:
            qidx = lax.broadcasted_iota(jnp.int32, (block, qhi - qlo), 1) + (halo + qlo)
            allowed = allowed & (kidx <= qidx)
        pts, dss, kts = [], [], []
        for t in range(2):
            keep = lanes_of(block, t == 0)
            kt = jnp.where(keep, k, jnp.zeros_like(k))
            vt = jnp.where(keep, v, jnp.zeros_like(v))
            st = dot_nt(jnp.concatenate([kt, ek], axis=1), qcats[t][qlo:qhi])
            pt = jnp.exp(jnp.where(allowed, st, MASKED))
            dpt = dot_nt(jnp.concatenate([vt, ones], axis=1), docats[t][qlo:qhi])
            pts.append(pt.astype(BF16))
            dss.append((pt * dpt).astype(BF16))
            kts.append(kt)
        dv = dot_nn(jnp.concatenate(pts, axis=1), jnp.concatenate([d[qlo:qhi] for d in dots], axis=0))
        dk = dot_nn(jnp.concatenate(dss, axis=1), jnp.concatenate([d[qlo:qhi] for d in qts], axis=0))
        dv_out[0, at : at + block, :] = dv.astype(BF16)
        dk_out[0, at : at + block, :] = dk.astype(BF16)
        acc_ref[:, qlo:qhi] += dot_tn(jnp.concatenate(kts, axis=0), jnp.concatenate(dss, axis=0))
    if final:
        scale = 1.0 / math.sqrt(LANES // 2)
        dq_ref[0] = (acc_ref[...].T * scale).astype(BF16)
    else:
        dq_ref[0] = acc_ref[...]


def attend_back(word, which, q, kh, ko, vh, vo, o, do, e, lo, ek, start=None):
    _, rows, width = q.shape
    halo = kh.shape[1]
    pairs = width // LANES
    block = min(256, rows)
    begin, end, final = (0, halo, False) if start is None else (halo, halo + rows, True)
    spec = lambda n: pl.BlockSpec((1, n, LANES), lambda p: (which, 0, p))
    only = lambda n: pl.BlockSpec((1, n, LANES), lambda p: (0, 0, p))
    sums = pl.BlockSpec((1, LANES, rows), lambda p: (0, p, 0))
    count = pairs * 2 * rows * (WIN + block) * (end - begin) // (halo + rows)
    if final:
        shapes, specs = [sds(1, rows, width)] * 3, [only(rows)] * 3
    else:
        shapes = [sds(1, width, rows, dtype=F32)] + [sds(1, halo, width)] * 2
        specs = [sums, only(halo), only(halo)]
    return call(
        functools.partial(backward_kernel, rows, halo, block, begin, end, final),
        shapes,
        word, *[pltpu.with_memory_space_constraint(x, pltpu.HBM) for x in (q, kh, ko, vh, vo)],
        o, do, pltpu.with_memory_space_constraint(e, pltpu.HBM), lo, ek,
        *([] if start is None else [start]),
        grid=(pairs,),
        in_specs=[
            SCALARS,
            spec(rows), spec(halo), spec(rows), spec(halo), spec(rows), only(rows), spec(rows),
            pl.BlockSpec((1, 2, rows, LANES), lambda p: (0, p, 0, 0)),
            pl.BlockSpec((1, 1, rows), lambda p: (which, 0, 0)),
            fixed(halo + rows, LANES),
        ]
        + ([] if start is None else [sums]),
        out_specs=specs,
        scratch_shapes=[pltpu.VMEM((LANES, rows), F32)],
        flops=count * 2304,
        moved=8 << 20,
        exps=count,
        name="attention_backward",
    )


def act_back_kernel(
    me_ref, own, other, slope_own, slope_other, w0, w1, w2, w3, w4,
    du_own, du_other, sums, w, sems,
):
    copies = fetches(me_ref[0], (w0, w1, w2, w3, w4), wanted_down(w), sems)
    step = pl.program_id(0)

    @pl.when(step == 0)
    def _():
        start_all(copies)
        for group in copies:
            wait_group(group)

    rows = own.shape[0]
    piece = min(256, rows)
    w_part = w[pl.ds(pl.multiple_of(step * 512, 512), 512), :]
    total = jnp.zeros((1, 512), F32)
    for dy, slope, du in ((other, slope_other, du_other), (own, slope_own, du_own)):
        for r in range(0, rows, piece):
            grad = dot_nt(dy[r : r + piece], w_part) * slope[r : r + piece].astype(F32)
            rounded = grad.astype(BF16)
            du[r : r + piece] = rounded
            total += column_sum(rounded)
    sums[...] = jnp.broadcast_to(total, (8, 512))


def act_back(me, own, other, slope_own, slope_other, pieces):
    rows = own.shape[0]
    half = FF // 2
    columns = pl.BlockSpec((rows, 512), lambda j: (0, j))
    return call(
        act_back_kernel,
        [sds(rows, half), sds(rows, half), sds(8, half, dtype=F32)],
        me, own, other, slope_own, slope_other, *pieces,
        grid=(4,),
        in_specs=[SCALARS, fixed(rows, D), fixed(rows, D), columns, columns] + [ANYWHERE] * 5,
        out_specs=[columns, columns, pl.BlockSpec((8, 512), lambda j: (0, j))],
        scratch_shapes=[pltpu.VMEM((half, D), BF16), pltpu.SemaphoreType.DMA((4, 4))],
        flops=4 * rows * half * D,
        moved=16 << 20,
        name="act_back",
    )


def up_back_kernel(me_ref, du, w0, w1, w2, w3, w4, p_ref, w, sems):
    copies = fetches(me_ref[0], (w0, w1, w2, w3, w4), wanted_up(w), sems)
    start_all(copies)
    for group in copies:
        wait_group(group)
    p_ref[...] = dot_nt(du[...], w[...]).astype(BF16)


def up_back_other(me, du, pieces):
    rows, half = du.shape
    return call(
        up_back_kernel,
        sds(rows, D),
        me, du, *pieces,
        grid=(1,),
        in_specs=[SCALARS, fixed(rows, half)] + [ANYWHERE] * 5,
        out_specs=fixed(rows, D),
        scratch_shapes=[pltpu.VMEM((D, half), BF16), pltpu.SemaphoreType.DMA((4, 4))],
        flops=2 * rows * half * D,
        moved=7 << 20,
        name="up_back_other",
    )


def middle_back_kernel(
    me_ref, du, got, x1, dy, gain, w0, w1, w2, w3, w4, dx1_ref, db_ref, sums, w, sems
):
    copies = fetches(me_ref[0], (w0, w1, w2, w3, w4), wanted_up(w), sems)
    start_all(copies)
    normal, inverse = normalize(x1[...])
    for group in copies:
        wait_group(group)
    dh = dot_nt(du[...], w[...]) + got[...].astype(F32)
    top = dy[...].astype(F32)
    dx1 = top + norm_back(dh * gain[...], normal, inverse)
    dx1_ref[...] = dx1
    db = dx1.astype(BF16)
    db_ref[...] = db
    sums[0:1] = column_sum(dh * normal)
    sums[1:2] = column_sum(dh)
    sums[2:3] = column_sum(db)
    sums[3:4] = column_sum(top)
    sums[4:8] = jnp.zeros((4, D), F32)


def middle_back(me, du, got, x1, dy, gain, pieces):
    rows, half = du.shape
    return call(
        middle_back_kernel,
        [sds(rows, D, dtype=F32), sds(rows, D), sds(8, D, dtype=F32)],
        me, du, got, x1, dy, gain, *pieces,
        grid=(1,),
        in_specs=[SCALARS, fixed(rows, half)]
        + [fixed(rows, D)] * 3
        + [fixed(1, D)]
        + [ANYWHERE] * 5,
        out_specs=[fixed(rows, D), fixed(rows, D), fixed(8, D)],
        scratch_shapes=[pltpu.VMEM((D, half), BF16), pltpu.SemaphoreType.DMA((4, 4))],
        flops=2 * rows * half * D,
        moved=14 << 20,
        name="middle_back",
    )


def out_back_kernel(me_ref, own, other, w0, w1, w2, w3, w4, do_ref, w, sems):
    copies = fetches(me_ref[0], (w0, w1, w2, w3, w4), wanted_out(w), sems)
    start_all(copies)
    for group in copies:
        wait_group(group)
    do_ref[0] = dot_nt(own[...], w[...]).astype(BF16)
    do_ref[1] = dot_nt(other[...], w[...]).astype(BF16)


def out_back(me, own, other, pieces):
    rows = own.shape[0]
    half = D // 2
    return call(
        out_back_kernel,
        sds(2, rows, half),
        me, own, other, *pieces,
        grid=(1,),
        in_specs=[SCALARS, fixed(rows, D), fixed(rows, D)] + [ANYWHERE] * 5,
        out_specs=fixed(2, rows, half),
        scratch_shapes=[pltpu.VMEM((half, D), BF16), pltpu.SemaphoreType.DMA((2, 4))],
        flops=4 * rows * half * D,
        moved=4 << 20,
        name="out_back",
    )


def store_parts(step, parts_x, parts_y, send_x, send_y, keep_x, keep_y):
    def put(ref, pieces):
        row = 0
        for piece in pieces:
            ref[0, row : row + piece.shape[0]] = piece
            row += piece.shape[0]

    @pl.when(step < 2)
    def _():
        put(send_x, parts_x)

    @pl.when(step >= 2)
    def _():
        put(keep_x, parts_x)

    @pl.when(step % 2 == 0)
    def _():
        put(send_y, parts_y)

    @pl.when(step % 2 == 1)
    def _():
        put(keep_y, parts_y)


def part_outputs(rows):
    shapes = [kept(2, rows, 512)] * 4
    specs = [
        pl.BlockSpec((1, rows, 512), lambda i, order: (jnp.minimum(i, 1), 0, 0)),
        pl.BlockSpec((1, rows, 512), lambda i, order: (i // 2, 0, 0)),
        pl.BlockSpec((1, rows, 512), lambda i, order: (i // 3, 0, 0)),
        pl.BlockSpec((1, rows, 512), lambda i, order: (i // 3, 0, 0)),
    ]
    return shapes, specs


def down_grad_kernel(order, act_own, act_other, own, other, *outs):
    grad = (dot_tn(act_own[...], own[...]) + dot_tn(act_other[...], other[...])).astype(BF16)
    store_parts(
        pl.program_id(0),
        [grad[:256, :512], grad[:256, 512:]],
        [grad[256:, :512], grad[256:, 512:]],
        *outs,
    )


def down_grad(order, act_own, act_other, own, other):
    rows = own.shape[0]
    shapes, specs = part_outputs(512)
    columns = pl.BlockSpec((rows, 512), lambda i, order: (0, order[i]))
    full = pl.BlockSpec((rows, D), lambda i, order: (0, 0))
    return call(
        down_grad_kernel,
        shapes,
        order, act_own, act_other, own, other,
        grid_spec=pltpu.PrefetchScalarGridSpec(
            num_scalar_prefetch=1,
            grid=(4,),
            in_specs=[columns, columns, full, full],
            out_specs=specs,
        ),
        flops=4 * rows * (FF // 2) * D,
        moved=10 << 20,
        name="down_grad",
    )


def up_grad_kernel(
    order, h_own, h_other, du_own, du_other, o_own, o_other, db_own, db_other, *outs
):
    grad = (dot_tn(h_own[...], du_own[...]) + dot_tn(h_other[...], du_other[...])).astype(BF16)
    out_part = (dot_tn(o_own[0], db_own[...]) + dot_tn(o_other[0], db_other[...])).astype(BF16)
    store_parts(
        pl.program_id(0),
        [grad[:, :512], grad[:, 512:1024], out_part[:, :512]],
        [grad[:, 1024:1536], grad[:, 1536:], out_part[:, 512:]],
        *outs,
    )


def up_grad(order, h_own, h_other, du_own, du_other, o_own, o_other, db_own, db_other):
    rows = h_own.shape[0]
    half = FF // 2
    shapes, specs = part_outputs(640)
    columns = pl.BlockSpec((rows, 256), lambda i, order: (0, order[i]))
    full = lambda width: pl.BlockSpec((rows, width), lambda i, order: (0, 0))
    heads = pl.BlockSpec((1, rows, 128), lambda i, order: (0, 0, order[i]))
    return call(
        up_grad_kernel,
        shapes,
        order, h_own, h_other, du_own, du_other, o_own, o_other, db_own, db_other,
        grid_spec=pltpu.PrefetchScalarGridSpec(
            num_scalar_prefetch=1,
            grid=(4,),
            in_specs=[columns, columns, full(half), full(half), heads, heads, full(D), full(D)],
            out_specs=specs,
        ),
        flops=4 * rows * half * D + 2 * rows * D * D,
        moved=14 << 20,
        name="up_grad",
    )


def qkv_grad_kernel(order, a_own, a_halo, *refs):
    dq, dko, dvo, dkh, dvh = (refs[2 * i : 2 * i + 2] for i in range(5))
    *parts, sums = refs[10:]

    def total(pairs):
        return sum(dot_tn(left[m], right[m][0]) for left, right in pairs for m in range(2)).astype(BF16)

    k_part = total([(a_own, dko), (a_halo, dkh)])
    first = [total([(a_own, dq)]), k_part[:128]]
    second = [k_part[128:], total([(a_own, dvo), (a_halo, dvh)])]
    store_parts(pl.program_id(0), first, second, *parts)

    @pl.when(pl.program_id(0) == 0)
    def _():
        sums[0:1] = column_sum(dq[0][0]) + column_sum(dq[1][0])
        sums[1:2] = sum(column_sum(ref[0]) for ref in (*dvo, *dvh))
        sums[2:8] = jnp.zeros((6, sums.shape[1]), F32)


def qkv_grad(order, a_own, a_halo, *grads):
    rows, halo = a_own.shape[1], a_halo.shape[1]
    half = D // 2
    shapes, specs = part_outputs(384)
    full = lambda n: pl.BlockSpec((1, n, half), lambda i, order: (0, 0, 0))
    columns = lambda n: pl.BlockSpec((2, n, 256), lambda i, order: (0, 0, order[i]))
    return call(
        qkv_grad_kernel,
        shapes + [sds(8, half, dtype=F32)],
        order, a_own, a_halo, *[ref for pair in grads for ref in pair],
        grid_spec=pltpu.PrefetchScalarGridSpec(
            num_scalar_prefetch=1,
            grid=(4,),
            in_specs=[columns(rows), columns(halo)]
            + [full(rows)] * 6
            + [full(halo)] * 4,
            out_specs=specs + [pl.BlockSpec((8, half), lambda i, order: (0, 0))],
        ),
        flops=4 * D * half * (3 * rows + 2 * halo),
        moved=16 << 20,
        name="qkv_grad",
    )


def normed_back_kernel(hops, me_ref, *refs):
    wanted = (1, 2) if hops else (0, 1, 2)
    count = len(wanted)
    grads, a_ref, refs = refs[:count], refs[count], refs[count + 1 :]
    *outs, sums, w, sems = refs[5:]
    got = outs.pop(0) if len(outs) > max(hops, 1) else None
    copies = fetches(me_ref[0], refs[:5], wanted_qkv(w, wanted), sems)
    start_all(copies)
    for group in copies:
        wait_group(group)
    weighted = jnp.zeros((1, D), F32)
    plain = jnp.zeros((1, D), F32)
    rows = outs[0].shape[0] if got is not None else a_ref.shape[1] // max(hops, 1)
    for number in range(max(hops, 1)):
        r = slice(number * rows, (number + 1) * rows)
        da = sum(dot_nt(grad[0, r], w[i]) for i, grad in enumerate(grads))
        weighted += column_sum(da * a_ref[0, r].astype(F32))
        plain += column_sum(da)
        if got is None:
            outs[0][r] = da.astype(BF16)
        else:
            da = da + got[r].astype(F32)
            outs[number][...] = da.astype(outs[number].dtype)
    sums[0:1] = weighted
    sums[1:2] = plain
    sums[2:8] = jnp.zeros((6, D), F32)


def normed_back(me, which, hops, grads, a, pieces, got=None):
    length = a.shape[1]
    rows = length // max(hops, 1)
    half = D // 2
    count = len(grads)
    if got is None:
        outs, out_specs = [sds(length, D)], [fixed(length, D)]
    elif hops:
        outs, out_specs = [sds(rows, D)] * hops, [fixed(rows, D)] * hops
    else:
        outs, out_specs = [sds(rows, D, dtype=F32)], [fixed(rows, D)]
    return call(
        functools.partial(normed_back_kernel, hops),
        outs + [sds(8, D, dtype=F32)],
        me, *grads, a, *pieces, *([] if got is None else [got]),
        grid=(1,),
        in_specs=[SCALARS]
        + [fixed(1, length, half)] * count
        + [pl.BlockSpec((1, length, D), lambda i: (which, 0, 0))]
        + [ANYWHERE] * 5
        + ([] if got is None else [fixed(length, D)]),
        out_specs=out_specs + [fixed(8, D)],
        scratch_shapes=[pltpu.VMEM((count, D, half), BF16), pltpu.SemaphoreType.DMA((count, 4))],
        flops=2 * count * length * half * D,
        moved=8 << 20,
        name="normed_back",
    )


def first_back_kernel(word, da_ref, got, x_ref, dx1, gain, dx_ref, low_ref):
    da = da_ref[...] + got[...].astype(F32)
    normal, inverse = normalize(x_ref[...].astype(F32))
    dx = dx1[...] + norm_back(da * gain[...], normal, inverse)
    dx_ref[...] = dx
    low_ref[...] = dx.astype(BF16)


def first_back(word, da, got, x, dx1, gain):
    rows = da.shape[0]
    return call(
        first_back_kernel,
        [sds(rows, D, dtype=F32), sds(rows, D)],
        word, da, got, x, dx1, gain,
        grid=(1,),
        in_specs=[SCALARS] + [fixed(rows, D)] * 4 + [fixed(1, D)],
        out_specs=[fixed(rows, D), fixed(rows, D)],
        moved=10 << 20,
        name="first_back",
    )


def unpack_down_kernel(core_ref, kept, got, out):
    core = core_ref[0]
    for half, source in ((core, kept), (1 - core, got)):
        for rh in range(2):
            for j in range(2):
                at = (rh * 2 + j) * 256
                rows = pl.ds(pl.multiple_of(half * 512 + rh * 256, 256), 256)
                out[0, rows, j * 512 : (j + 1) * 512] = source[at : at + 256].astype(F32)


def unpack_up_kernel(core_ref, kept_part, got, out_up, out_out):
    core = core_ref[0]
    for half, source in ((core, kept_part), (1 - core, got)):
        for j in range(4):
            at = (j // 2) * 640 + (j % 2) * 256
            columns = pl.ds(pl.multiple_of(j * 1024 + half * 512, 512), 512)
            out_up[0, :, columns] = source[at : at + 256].astype(F32)
        rows = pl.ds(pl.multiple_of(half * 128, 128), 128)
        for j in range(2):
            at = j * 640 + 512
            out_out[0, rows, j * 512 : (j + 1) * 512] = source[at : at + 128].astype(F32)


def unpack_qkv_kernel(core_ref, kept_part, got, out):
    core = core_ref[0]
    for half, source in ((core, kept_part), (1 - core, got)):
        for g in range(3):
            for f in range(4):
                columns = pl.ds(pl.multiple_of((g * 4 + f) * 256 + half * 128, 128), 128)
                out[0, :, columns] = source[
                    g * 256 : (g + 1) * 256, f * 128 : (f + 1) * 128
                ].astype(F32)


def unpack(kernel, core, pieces, shapes, name):
    return call(
        kernel,
        shapes,
        core, *pieces,
        in_specs=[SCALARS] + [INSIDE] * len(pieces),
        out_specs=jax.tree.map(lambda _: INSIDE, shapes),
        moved=10 << 20,
        name=name,
    )


def split_vector(values):
    pieces, offset = [], 0
    for length in (D, D, D, D, D, D, D, FF, D):
        pieces.append(values[offset : offset + length])
        offset += length
    return pieces


def shards(inputs, cotangent, segments, w_qkv, w_out, w_up, w_down, vectors):
    core = lax.axis_index("section")
    column = lax.axis_index("ctx")
    fs = lax.axis_index("fsdp")
    nf = lax.axis_size("fsdp")
    rows = inputs.shape[2]
    reach = (WIN - 1) // rows + 1
    halo = reach * rows
    first_core = core == 0
    me = fs.astype(jnp.int32).reshape(1)
    core_word = core.astype(jnp.int32).reshape(1)
    order = jnp.stack([fs ^ r for r in ROLL]).astype(jnp.int32)

    def pick(here, there):
        return jnp.where(first_core, here, there), jnp.where(first_core, there, here)

    mine = lambda values: lax.dynamic_index_in_dim(values, core, 0, keepdims=False)
    theirs = lambda values: lax.dynamic_index_in_dim(values, 1 - core, 0, keepdims=False)
    x_own, x_other = mine(inputs[:, 0]), theirs(inputs[:, 0])
    keep_a, send_a, keep_u, send_u, keep_d, send_d = pack_weights(
        tie(core_word, x_own), w_qkv, w_out, w_up, w_down
    )
    shard_a = pick(keep_a, swap(send_a))
    later = lambda value: tie(value, shard_a[0])

    shard_u = pick(keep_u, swap(later(send_u)))
    shard_d = pick(keep_d, swap(later(send_d)))
    both = tie(jnp.concatenate(pick(vectors, swap(vectors))), shard_u, shard_d)
    near = flip(both, "fsdp", 1)
    low_x = (fs & 1) == 0
    pair = jnp.concatenate([jnp.where(low_x, both, near), jnp.where(low_x, near, both)], 1)
    far = flip(pair, "fsdp", 2)
    low_y = (fs & 2) == 0
    packed = jnp.concatenate([jnp.where(low_y, pair, far), jnp.where(low_y, far, pair)], 1)
    packed = packed.astype(F32)

    a0 = Gather(shard_a[0])
    u0 = Gather(shard_u[0], a0.far)
    d0 = Gather(shard_d[0], u0.near)
    a1 = Gather(shard_a[1], d0.near)
    u1 = Gather(shard_u[1], a1.far)
    d1 = Gather(shard_d[1], u1.near)
    weights = ((a0, u0, d0), (a1, u1, d1))

    top = later(cotangent[:, 0])
    top_own, top_other = mine(top), theirs(top)
    marks = later(segments[:, 0])
    starts = jnp.stack([mine(marks), theirs(marks)])
    position = column * rows + jnp.arange(rows, dtype=jnp.int32)
    lo = jnp.maximum(starts, position[None] - (WIN - 1)) - (column * rows - halo)
    lo_column, lo = lo[:, :, None], lo[:, None, :]

    nought = later(jnp.zeros((), jnp.int32))
    key_index = lax.broadcasted_iota(jnp.int32, (halo + rows, LANES), 0) + nought
    lane = lax.broadcasted_iota(jnp.int32, (halo + rows, LANES), 1)
    placed = jnp.where(lane % 2 == 0, key_index // 256 * 256, key_index % 256)
    ek = jnp.where(lane < 6, placed, jnp.where(lane < 9, 1, 0)).astype(BF16)
    local_heads = HEADS // 2
    per_group = local_heads // nf
    local = jnp.arange(local_heads) + nought
    head = (local // per_group) * (2 * per_group) + core * per_group + local % per_group
    slopes = jnp.exp2(-0.5 * (head.astype(F32) + 1.0)) * (4.0 / WIN)
    first, second, third = [values.astype(F32) for values in split3(slopes)]
    eq = jnp.concatenate(
        [
            jnp.stack([first, first, second, second, third, third], 1),
            jnp.zeros((local_heads, LANES - 6), F32),
        ],
        1,
    ).reshape(local_heads // 2, 2, LANES)

    def start_halo(own, *after):
        pieces, block = [], own
        for hop in range(reach):
            block = step_along(tie(block, *after) if hop == 1 else block, "ctx", 1)
            pieces.append(block)
        return pieces

    def finish_return(first, hops, *after):
        carried, sent = first, first
        for hop, piece in enumerate(hops[1:]):
            sent = add_bf16(piece, tie(carried, *after) if hop == 0 else carried)
            carried = step_along(sent, "ctx", -1)
        return carried, sent

    def my_half(values, groups):
        view = values.reshape(groups, 2, -1)
        return jnp.where(first_core, view[:, 0], view[:, 1]).reshape(1, -1)

    def widen(values, groups):
        view = values.reshape(groups, 1, -1)
        zero = jnp.zeros_like(view)
        return jnp.where(
            first_core, jnp.concatenate([view, zero], 1), jnp.concatenate([zero, view], 1)
        ).reshape(-1)

    line = Line()
    run = line.run

    def forward(layer, x_own, x_other, first_hops):
        g1, b1, bq, bv, bo, g2, b2, bu, bd = [
            values.reshape(1, -1) for values in split_vector(packed[layer])
        ]
        bq, bv, bu = my_half(bq, nf), my_half(bv, nf), my_half(bu, nf)
        ga, gu, gd = weights[layer]
        wa, wu, wd = ga.pieces, gu.pieces, gd.pieces
        a_own, q, ko, vo = run(
            make_qkv, me, x_own, x_other, g1, b1, bq, bv, wa,
            after=(ek, eq, lo, lo_column, bu, first_hops if layer == 0 else ()),
        )
        earlier = ()
        for hop, block in enumerate(first_hops):
            block = tie(block, line.token if hop == 0 else ())
            earlier = run(
                make_kv, me, block, swap(block), reach, reach - 1 - hop, earlier, g1, b1, bv, wa,
                after=first_hops if hop == 0 else (),
            )
        a_halo, kh, vh = earlier
        o_other, e_other = run(
            attend, me, 1, q, kh, ko, vh, vo, lo_column, ek, eq, after=(gu.near,)
        )
        part = run(out_other, me, o_other, wa)
        o_own, e_own = run(attend, me, 0, q, kh, ko, vh, vo, lo_column, ek, eq)
        x1, h_own = run(
            middle, me, o_own, swap(part), x_own, bo, g2, b2, wa, after=(gu.far,)
        )
        o, e = (o_own, o_other), (e_own, e_other)
        h_other = swap(h_own)
        act_own, slope_own = run(up, me, h_own, bu, wu, after=(gd.near,))
        act_other, slope_other = run(up, me, h_other, bu, wu)
        part = run(down_other, me, act_other, wd)
        y = run(last, me, act_own, swap(part), x1, bd, wd)
        stored = (
            x_own, a_own, a_halo, q, kh, ko, vh, vo, o, e, x1, h_own, h_other,
            act_own, slope_own, act_other, slope_other, g1, b1, g2,
        )
        return y, stored

    y0, stored0 = forward(0, x_own, x_other, start_halo(x_own, shard_a[0]))
    y0_other = swap(y0)
    y1, stored1 = forward(1, y0, y0_other, start_halo(y0, a1.near))
    y1_other = swap(y1)

    column_sums = Column()

    def step(block, *after):
        column_sums.step(block, line.token, *after)
        line.also += column_sums.sent

    def backward(layer, top_own, top_other, stored, before=()):
        last_layer = layer == 0
        (
            x_own, a_own, a_halo, q, kh, ko, vh, vo, o, e, x1, h_own, h_other,
            act_own, slope_own, act_other, slope_other, g1, b1, g2,
        ) = stored
        wa, wu, wd = (group.pieces for group in weights[layer])
        du_own, du_other, sums_up = run(
            act_back, me, top_own, top_other, slope_own, slope_other, wd
        )
        got = swap(run(up_back_other, me, du_other, wu))
        down_part = Scatter(*run(down_grad, order, act_own, act_other, top_own, top_other))
        if last_layer:
            before[1].third(line.token)
        dx1, db_own, sums_middle = run(middle_back, me, du_own, got, x1, top_own, g2, wu)
        db_other = swap(db_own)
        do = run(out_back, me, db_own, db_other, wa)
        up_part = Scatter(
            *run(up_grad, order, h_own, h_other, du_own, du_other, *o, db_own, db_other)
        )
        if last_layer:
            step(before[0].piece)

        def early(m):
            return run(attend_back, me, m, q, kh, ko, vh, vo, o[m], do, e[m], lo, ek)

        def own(m, start):
            return run(attend_back, me, m, q, kh, ko, vh, vo, o[m], do, e[m], lo, ek, start)

        begun_other, dkh_other, dvh_other = early(1)
        down_part.second(line.token)
        line.also += (down_part.half,)
        if last_layer:
            step(before[1].piece)
        part, sums_a = run(normed_back, me, 1, reach, (dkh_other, dvh_other), a_halo, wa)
        got = swap(part)
        begun_own, dkh_own, dvh_own = early(0)
        down_part.third(line.token)
        line.also = (down_part.piece,)
        *hops, sums_b = run(normed_back, me, 0, reach, (dkh_own, dvh_own), a_halo, wa, got)
        first = step_along(hops[0], "ctx", -1)
        carried = sent = first
        if last_layer:
            step(down_part.piece, hops)
        else:
            carried, sent = finish_return(first, hops)
        dq_other, dko_other, dvo_other = own(1, begun_other)
        part, sums_c = run(normed_back, me, 1, 0, (dq_other, dko_other, dvo_other), a_own, wa)
        got = swap(part)
        up_part.second(line.token)
        line.also += (up_part.half,)
        dq_own, dko_own, dvo_own = own(0, begun_own)
        *parts, sums_qkv = run(
            qkv_grad, order, a_own, a_halo, (dq_own, dq_other), (dko_own, dko_other),
            (dvo_own, dvo_other), (dkh_own, dkh_other), (dvh_own, dvh_other),
            after=(column_sums.outer_got, column_sums.inner_got) if last_layer else (sent,),
        )
        qkv_part = Scatter(*parts)
        up_part.third(line.token)
        line.also = (up_part.piece,)
        if last_layer:
            step(up_part.piece)
        da, sums_d = run(
            normed_back, me, 0, 0, (dq_own, dko_own, dvo_own), a_own, wa, got,
            after=() if last_layer else (carried,),
        )
        qkv_part.second(line.token)
        line.also += (qkv_part.half,)
        if last_layer:
            carried, sent = finish_return(first, hops, line.token)
            line.also += (sent,)
            qkv_part.third()
            step(qkv_part.piece)
        dx, dx_low = run(first_back, me, da, carried, x_own, dx1, g1)
        if last_layer:
            step(None)
        else:
            step(down_part.piece)
        plain = sums_a[1] + sums_b[1] + sums_c[1] + sums_d[1]
        weighted = sums_a[0] + sums_b[0] + sums_c[0] + sums_d[0]
        vector = jnp.concatenate(
            [
                (weighted - b1[0] * plain) / g1[0], plain, widen(sums_qkv[0], nf),
                widen(sums_qkv[1], nf), sums_middle[2], sums_middle[0], sums_middle[1],
                widen(sums_up[0], nf), sums_middle[3],
            ]
        )
        return dx, dx_low, (up_part, qkv_part), vector

    _, dx1, parts1, vector1 = backward(1, top_own, top_other, stored1)
    dx1_other = swap(dx1)
    dx0, _, _, vector0 = backward(0, dx1, dx1_other, stored0, parts1)
    dx0_other = swap(dx0)
    def by_micro(own, other):
        return jnp.where(first_core, jnp.stack([own, other]), jnp.stack([other, own]))

    activations = jnp.where(first_core, by_micro(y0, y0_other), by_micro(y1, y1_other))
    input_grad = jnp.where(
        first_core, by_micro(dx0, dx0_other), by_micro(dx1, dx1_other).astype(F32)
    )

    def exchange(first, second):
        kept, sent = pick(first, second)
        return kept, swap(sent)

    step(None, activations, input_grad)
    size = D // nf
    down1_sum, up1_sum, qkv1_sum, down0_sum, up0_sum, *_ = column_sums.sums
    grad_down = unpack(
        unpack_down_kernel, core_word, exchange(down0_sum, down1_sum),
        sds(1, FF // nf, D, dtype=F32), "unpack_down",
    )
    grad_up, grad_out = unpack(
        unpack_up_kernel, core_word, exchange(up0_sum, up1_sum),
        [sds(1, size, FF, dtype=F32), sds(1, size, D, dtype=F32)], "unpack_up",
    )
    summed = sum_all(jnp.stack([vector0, vector1]))
    step(None, grad_down, grad_up)
    qkv0_sum = column_sums.sums[-1]
    grad_qkv = unpack(
        unpack_qkv_kernel, core_word, exchange(qkv0_sum, qkv1_sum),
        sds(1, size, 3 * D, dtype=F32), "unpack_qkv",
    )
    length = summed.shape[1] // nf
    grad_vectors = lax.dynamic_slice(summed, (core, fs * length), (1, length))
    return (
        activations[None, :, None], input_grad[None, :, None],
        grad_qkv, grad_out, grad_up, grad_down, grad_vectors,
    )


def solution(mesh):
    placed = (
        P(None, "fsdp", "ctx", None),
        P(None, "fsdp", "ctx", None),
        P(None, "fsdp", "ctx"),
        P("section", "fsdp", None),
        P("section", "fsdp", None),
        P("section", "fsdp", None),
        P("section", "fsdp", None),
        P("section", "fsdp"),
    )
    return jax.shard_map(
        shards,
        mesh=mesh,
        in_specs=placed,
        out_specs=(
            P("section", None, "fsdp", "ctx", None),
            P("section", None, "fsdp", "ctx", None),
            P("section", "fsdp", None),
            P("section", "fsdp", None),
            P("section", "fsdp", None),
            P("section", "fsdp", None),
            P("section", "fsdp"),
        ),
        check_vma=False,
    )
```

```python
import functools
import math

import jax
import jax.numpy as jnp
from jax import lax
from jax.experimental import pallas as pl
from jax.experimental.pallas import tpu as pltpu
from jax.sharding import PartitionSpec as P

D = 1024
HEADS = 16
FF = 4096
WIN = 1024

EPSILON = 1e-05
F32 = jnp.float32
BF16 = jnp.bfloat16
LANES = 128
MASKED = -1e30


LEAST = 256
ROLL = (3, 1, 2, 0)


def flip(block, axis, bit):
    count = lax.axis_size(axis)
    return lax.ppermute(block, axis, [(i, i ^ bit) for i in range(count)])


def step_along(block, axis, distance):
    devices = range(lax.axis_size(axis))
    route = [(i - distance, i) for i in devices if i - distance in devices]
    return lax.ppermute(block, axis, route)


def swap(block):
    return flip(block, "section", 1)


def tie(value, *after):
    return lax.optimization_barrier((value, after))[0]


class Gather:
    def __init__(self, shard, *after, then=()):
        shard = tie(shard, *after) if after else shard
        half = shard.shape[0] // 2
        self.near = flip(shard, "fsdp", 1), flip(shard, "fsdp", 2)
        from_x, from_y = tie(self.near, *then) if then else self.near
        self.far = flip(from_x[:half], "fsdp", 2), flip(from_y[half:], "fsdp", 1)
        self.pieces = (shard, *self.near, *self.far)


def add_bf16(*terms):
    return sum(term.astype(F32) for term in terms).astype(BF16)


class Scatter:
    def __init__(self, send_x, send_y, keep_x, keep_y):
        self.near = flip(send_x, "fsdp", 1), flip(send_y, "fsdp", 2)
        self.keep = keep_x, keep_y

    def second(self, *after):
        (got_x, got_y), (keep_x, keep_y) = tie(self.near, *after), self.keep
        self.half = add_bf16(keep_x[0], got_x[0]), add_bf16(keep_y[0], got_y[0])
        self.far = flip(self.half[0], "fsdp", 2), flip(self.half[1], "fsdp", 1)

    def third(self, *after):
        far_x, far_y = tie(self.far, *after)
        (got_x, got_y), (keep_x, keep_y) = self.near, self.keep
        self.piece = jnp.concatenate(
            [add_bf16(keep_x[1], got_x[1], far_x), add_bf16(keep_y[1], got_y[1], far_y)]
        )


class Column:
    def __init__(self):
        self.line = lax.axis_size("ctx") == 4
        me = lax.axis_index("ctx")
        self.inner = (me == 1) | (me == 2)
        self.block = self.half = self.total = self.outer_got = self.inner_got = None
        self.sums = []
        self.sent = ()

    def step(self, block, *after):
        if not self.line:
            if block is not None:
                self.sums.append(lax.psum(block, "ctx"))
            return
        outer_got, inner_got, block = tie((self.outer_got, self.inner_got, block), *after)
        half = total = None
        if self.block is not None:
            half = add_bf16(self.block, outer_got[: self.block.shape[0]])
        if self.half is not None:
            total = add_bf16(self.half, inner_got)
        if self.total is not None:
            outer_sum = outer_got[: self.total.shape[0]]
            self.sums.append(jnp.where(self.inner, self.total, outer_sum))
        self.block, self.half, self.total = block, half, total
        self.sent = ()
        if block is not None or total is not None:
            sent = total if block is None else block
            if block is not None and total is not None:
                rows = max(total.shape[0], block.shape[0])
                fill = lambda part: jnp.pad(part, ((0, rows - part.shape[0]), (0, 0)))
                sent = jnp.where(self.inner, fill(total), fill(block))
            self.outer_got = flip(sent, "ctx", 1)
            self.sent += (sent,)
        if half is not None:
            self.inner_got = lax.ppermute(half, "ctx", [(1, 2), (2, 1)])
            self.sent += (half,)


class Line:
    def __init__(self):
        self.token = ()
        self.also = ()

    def run(self, kernel, word, *args, after=()):
        word = tie(word, self.token, self.also, after)
        self.also = ()
        out = kernel(word, *args)
        self.token = out[0] if isinstance(out, (list, tuple)) else out
        return out


def sums_over_all(block):
    stages = [block]
    for axis in ("section", "fsdp", "ctx"):
        bit = 1
        while bit < lax.axis_size(axis):
            stages.append(stages[-1] + flip(stages[-1], axis, bit))
            bit *= 2
    return stages


def streamed(*arrays):
    return [pltpu.with_memory_space_constraint(array, pltpu.HBM) for array in arrays]


def call(kernel, out_shape, *operands, limit=32, flops=0, moved=0, exps=0, name=None, **rest):
    return pl.pallas_call(
        kernel,
        out_shape=out_shape,
        compiler_params=pltpu.CompilerParams(vmem_limit_bytes=limit * 1024 * 1024),
        cost_estimate=pl.CostEstimate(flops=flops, bytes_accessed=moved, transcendentals=exps),
        name=name,
        **rest,
    )(*operands)


def sds(*shape, dtype=BF16):
    return jax.ShapeDtypeStruct(shape, dtype)


def kept(*shape, dtype=BF16):
    return pltpu.HBM(shape, dtype)


ANYWHERE = pl.BlockSpec(memory_space=pltpu.HBM)
SCALARS = pl.BlockSpec(memory_space=pltpu.SMEM)
INSIDE = pl.BlockSpec(memory_space=pltpu.VMEM)


def fixed(*shape):
    return pl.BlockSpec(shape, lambda *_: (0,) * len(shape))


def fetches(me, pieces, wanted, sems):
    half = pieces[0].shape[0] // 2
    copies = []
    for number, (row, count, place) in enumerate(wanted):
        group = []
        for r in range(4):
            if r < 3:
                source = pieces[r].at[row : row + count]
            elif row < half:
                source = pieces[3].at[row : row + count]
            else:
                source = pieces[4].at[row - half : row - half + count]
            group.append(pltpu.make_async_copy(source, place(me ^ r), sems.at[number, r]))
        copies.append(group)
    return copies


def start_all(copies):
    for group in copies:
        for copy in group:
            copy.start()


def wait_group(group):
    for copy in group:
        copy.wait()


def part(a, size):
    return pl.ds(pl.multiple_of(a * size, size), size)


def wanted_qkv(w, which=(0, 1, 2)):
    return [
        (g * LEAST, LEAST, lambda a, i=i: w.at[i, part(a, LEAST)]) for i, g in enumerate(which)
    ]


def wanted_out(w):
    return [
        (3 * LEAST + j * 128, 128, lambda a, j=j: w.at[part(a, 128), j * 512 : (j + 1) * 512])
        for j in range(2)
    ]


def wanted_up(w):
    return [
        (j * LEAST, LEAST, lambda a, j=j: w.at[part(a, LEAST), j * 512 : (j + 1) * 512])
        for j in range(4)
    ]


def wanted_down(w):
    def place(a, rh, j):
        return w.at[pl.ds(pl.multiple_of(a * 512 + rh * 256, 256), 256), j * 512 : (j + 1) * 512]

    return [
        (
            (rh * 2 + j) * LEAST,
            LEAST,
            lambda a, rh=rh, j=j: place(a, rh, j),
        )
        for j in range(2)
        for rh in range(2)
    ]


def dot_nn(left, right):
    return lax.dot_general(left, right, (((1,), (0,)), ((), ())), preferred_element_type=F32)


def dot_nt(left, right):
    return lax.dot_general(left, right, (((1,), (1,)), ((), ())), preferred_element_type=F32)


def dot_tn(left, right):
    return lax.dot_general(left, right, (((0,), (0,)), ((), ())), preferred_element_type=F32)


def mean_last(values):
    return jnp.mean(values, axis=-1, keepdims=True)


def normalize(values):
    centred = values - mean_last(values)
    inverse = lax.rsqrt(mean_last(centred * centred) + EPSILON)
    return centred * inverse, inverse


def norm_back(grad_norm, normal, inverse):
    return inverse * (grad_norm - mean_last(grad_norm) - normal * mean_last(grad_norm * normal))


def column_sum(values):
    return jnp.sum(values.astype(F32), axis=0, keepdims=True)


def pack_kernel(
    core_ref, qkv, out, up, down, keep_a, send_a, keep_u, send_u, keep_d, send_d, sems
):
    core = core_ref[0]
    number = 0
    copies = []
    for target_a, target_u, target_d, half in (
        (send_a, send_u, send_d, 1 - core), (keep_a, keep_u, keep_d, core)
    ):
        for g in range(3):
            for f in range(4):
                columns = pl.ds(pl.multiple_of((g * 4 + f) * 256 + half * 128, 128), 128)
                copies.append(
                    (
                        qkv.at[0, :, columns],
                        target_a.at[g * LEAST : (g + 1) * LEAST, f * 128 : (f + 1) * 128],
                    )
                )
        for j in range(2):
            rows = pl.ds(pl.multiple_of(half * 128, 128), 128)
            copies.append(
                (
                    out.at[0, rows, j * 512 : (j + 1) * 512],
                    target_a.at[3 * LEAST + j * 128 : 3 * LEAST + (j + 1) * 128],
                )
            )
        for j in range(4):
            columns = pl.ds(pl.multiple_of(j * 1024 + half * 512, 512), 512)
            copies.append((up.at[0, :, columns], target_u.at[j * LEAST : (j + 1) * LEAST]))
        for rh in range(2):
            for j in range(2):
                rows = pl.ds(pl.multiple_of(half * 512 + rh * 256, 256), 256)
                at = (rh * 2 + j) * LEAST
                copies.append(
                    (down.at[0, rows, j * 512 : (j + 1) * 512], target_d.at[at : at + LEAST])
                )
    started = []
    for number, (source, target) in enumerate(copies):
        copy = pltpu.make_async_copy(source, target, sems.at[number])
        copy.start()
        started.append(copy)
    for copy in started:
        copy.wait()


def pack_weights(core, qkv, out, up, down):
    return call(
        pack_kernel,
        [kept(4 * LEAST, 512)] * 6,
        core, qkv, out, up, down,
        in_specs=[SCALARS] + [ANYWHERE] * 4,
        out_specs=[ANYWHERE] * 6,
        scratch_shapes=[pltpu.SemaphoreType.DMA((44,))],
        moved=12 << 20,
        limit=16,
        name="pack_weights",
    )


def qkv_kernel(
    me_ref, own_ref, other_ref, gain, bias, bq, bv, w0, w1, w2, w3, w4,
    a_ref, q_ref, k_ref, v_ref, w, sems,
):
    copies = fetches(me_ref[0], (w0, w1, w2, w3, w4), wanted_qkv(w), sems)
    start_all(copies)
    scale = BF16(1.0 / math.sqrt(D // HEADS))
    for m, x_ref in enumerate((own_ref, other_ref)):
        normed = (normalize(x_ref[...].astype(F32))[0] * gain[...] + bias[...]).astype(BF16)
        a_ref[m] = normed
        if m == 0:
            for group in copies:
                wait_group(group)
        q_ref[m] = (dot_nn(normed, w[0]) + bq[...]).astype(BF16) * scale
        k_ref[m] = dot_nn(normed, w[1]).astype(BF16)
        v_ref[m] = (dot_nn(normed, w[2]) + bv[...]).astype(BF16)


def make_qkv(me, own, other, gain, bias, bq, bv, pieces):
    rows = own.shape[0]
    half = D // 2
    return call(
        qkv_kernel,
        [kept(2, rows, D)] + [kept(2, rows, half)] * 3,
        me, own, other, gain, bias, bq, bv, *pieces,
        grid=(1,),
        in_specs=[SCALARS, fixed(rows, D), fixed(rows, D)]
        + [fixed(1, D), fixed(1, D), fixed(1, half), fixed(1, half)]
        + [ANYWHERE] * 5,
        out_specs=[fixed(2, rows, D)] + [fixed(2, rows, half)] * 3,
        scratch_shapes=[pltpu.VMEM((3, D, half), BF16), pltpu.SemaphoreType.DMA((3, 4))],
        flops=4 * rows * D * 3 * half,
        moved=14 << 20,
        name="project_qkv",
    )


def kv_kernel(me_ref, own_ref, other_ref, gain, bias, bv, w0, w1, w2, w3, w4, *rest):
    a_ref, k_ref, v_ref, w, sems = rest[-5:]
    copies = fetches(me_ref[0], (w0, w1, w2, w3, w4), wanted_qkv(w, (1, 2)), sems)
    start_all(copies)
    for m, x_ref in enumerate((own_ref, other_ref)):
        normed = (normalize(x_ref[...].astype(F32))[0] * gain[...] + bias[...]).astype(BF16)
        a_ref[m] = normed
        if m == 0:
            for group in copies:
                wait_group(group)
        k_ref[m] = dot_nn(normed, w[0]).astype(BF16)
        v_ref[m] = (dot_nn(normed, w[1]) + bv[...]).astype(BF16)


def make_kv(me, own, other, hops, at, earlier, gain, bias, bv, pieces):
    rows = own.shape[0]
    halo = hops * rows
    half = D // 2
    row = lambda width: pl.BlockSpec((2, rows, width), lambda i: (0, at, 0))
    first = 11
    return call(
        kv_kernel,
        [kept(2, halo, D), kept(2, halo, half), kept(2, halo, half)],
        me, own, other, gain, bias, bv, *pieces, *earlier,
        grid=(1,),
        in_specs=[SCALARS, fixed(rows, D), fixed(rows, D), fixed(1, D), fixed(1, D), fixed(1, half)]
        + [ANYWHERE] * 5
        + [ANYWHERE] * len(earlier),
        out_specs=[row(D), row(half), row(half)],
        input_output_aliases={first + i: i for i in range(len(earlier))},
        scratch_shapes=[pltpu.VMEM((2, D, half), BF16), pltpu.SemaphoreType.DMA((2, 4))],
        flops=2 * 2 * rows * D * 2 * half,
        moved=8 << 20,
        name="project_earlier",
    )


def out_kernel(me_ref, o_ref, w0, w1, w2, w3, w4, p_ref, w, sems):
    copies = fetches(me_ref[0], (w0, w1, w2, w3, w4), wanted_out(w), sems)
    start_all(copies)
    for group in copies:
        wait_group(group)
    p_ref[...] = dot_nn(o_ref[0], w[...]).astype(BF16)


def out_other(me, o, pieces):
    _, rows, half = o.shape
    return call(
        out_kernel,
        sds(rows, D),
        me, o, *pieces,
        grid=(1,),
        in_specs=[SCALARS, fixed(1, rows, half)] + [ANYWHERE] * 5,
        out_specs=fixed(rows, D),
        scratch_shapes=[pltpu.VMEM((half, D), BF16), pltpu.SemaphoreType.DMA((2, 4))],
        flops=2 * rows * half * D,
        moved=3 << 20,
        name="out_other",
    )


def middle_kernel(
    me_ref, o_ref, got, x_ref, bo, gain, bias, w0, w1, w2, w3, w4, x1_ref, h_ref, w, sems
):
    copies = fetches(me_ref[0], (w0, w1, w2, w3, w4), wanted_out(w), sems)
    start_all(copies)
    base = x_ref[...].astype(F32) + got[...].astype(F32) + bo[...]
    for group in copies:
        wait_group(group)
    x1 = base + dot_nn(o_ref[0], w[...])
    x1_ref[...] = x1
    h_ref[...] = (normalize(x1)[0] * gain[...] + bias[...]).astype(BF16)


def middle(me, o, got, x, bo, gain, bias, pieces):
    _, rows, half = o.shape
    return call(
        middle_kernel,
        [sds(rows, D, dtype=F32), sds(rows, D)],
        me, o, got, x, bo, gain, bias, *pieces,
        grid=(1,),
        in_specs=[SCALARS, fixed(1, rows, half)]
        + [fixed(rows, D)] * 2
        + [fixed(1, D)] * 3
        + [ANYWHERE] * 5,
        out_specs=[fixed(rows, D)] * 2,
        scratch_shapes=[pltpu.VMEM((half, D), BF16), pltpu.SemaphoreType.DMA((2, 4))],
        flops=2 * rows * half * D,
        moved=8 << 20,
        name="middle",
    )


def gelu_and_slope(u):
    c = math.sqrt(2.0 / math.pi)
    square = u * u
    half = 0.5 + 0.5 * jnp.tanh(u * (c + (c * 0.044715) * square))
    value = u * half
    slope = half + value * (1.0 - half) * (2.0 * c + (6.0 * c * 0.044715) * square)
    return value, slope


def up_kernel(me_ref, h_ref, bu, w0, w1, w2, w3, w4, act_ref, slope_ref, w, sems):
    copies = fetches(me_ref[0], (w0, w1, w2, w3, w4), wanted_up(w), sems)
    step = pl.program_id(0)

    @pl.when(step == 0)
    def _():
        start_all(copies)

    for j in range(4):

        @pl.when(step == j)
        def _(j=j):
            wait_group(copies[j])
            columns = slice(j * 512, (j + 1) * 512)
            rows = h_ref.shape[0]
            piece = min(256, rows)
            for r in range(0, rows, piece):
                u = dot_nn(h_ref[r : r + piece], w[:, columns]) + bu[:, columns]
                value, slope = gelu_and_slope(u)
                act_ref[r : r + piece] = value.astype(BF16)
                slope_ref[r : r + piece] = slope.astype(BF16)


def up(me, h, bu, pieces):
    rows = h.shape[0]
    half = FF // 2
    out = pl.BlockSpec((rows, 512), lambda j: (0, j))
    return call(
        up_kernel,
        [sds(rows, half), kept(rows, half)],
        me, h, bu, *pieces,
        grid=(4,),
        in_specs=[SCALARS, fixed(rows, D), fixed(1, half)] + [ANYWHERE] * 5,
        out_specs=[out, out],
        scratch_shapes=[pltpu.VMEM((D, half), BF16), pltpu.SemaphoreType.DMA((4, 4))],
        flops=2 * rows * half * D,
        moved=9 << 20,
        exps=rows * half,
        name="up",
    )


def down_kernel(me_ref, act, w0, w1, w2, w3, w4, p_ref, w, sems):
    copies = fetches(me_ref[0], (w0, w1, w2, w3, w4), wanted_down(w), sems)
    start_all(copies)
    for j in range(2):
        wait_group(copies[2 * j])
        wait_group(copies[2 * j + 1])
        columns = slice(j * 512, (j + 1) * 512)
        p_ref[:, columns] = dot_nn(act[...], w[:, columns]).astype(BF16)


def down_other(me, act, pieces):
    rows, half = act.shape
    return call(
        down_kernel,
        sds(rows, D),
        me, act, *pieces,
        grid=(1,),
        in_specs=[SCALARS, fixed(rows, half)] + [ANYWHERE] * 5,
        out_specs=fixed(rows, D),
        scratch_shapes=[pltpu.VMEM((half, D), BF16), pltpu.SemaphoreType.DMA((4, 4))],
        flops=2 * rows * half * D,
        moved=7 << 20,
        name="down_other",
    )


def last_kernel(me_ref, act, got, x1, bd, w0, w1, w2, w3, w4, y_ref, w, sems):
    copies = fetches(me_ref[0], (w0, w1, w2, w3, w4), wanted_down(w), sems)
    start_all(copies)
    for j in range(2):
        wait_group(copies[2 * j])
        wait_group(copies[2 * j + 1])
        columns = slice(j * 512, (j + 1) * 512)
        base = x1[:, columns] + got[:, columns].astype(F32) + bd[:, columns]
        y_ref[:, columns] = (base + dot_nn(act[...], w[:, columns])).astype(BF16)


def last(me, act, got, x1, bd, pieces):
    rows, half = act.shape
    return call(
        last_kernel,
        sds(rows, D),
        me, act, got, x1, bd, *pieces,
        grid=(1,),
        in_specs=[SCALARS, fixed(rows, half), fixed(rows, D), fixed(rows, D), fixed(1, D)]
        + [ANYWHERE] * 5,
        out_specs=fixed(rows, D),
        scratch_shapes=[pltpu.VMEM((half, D), BF16), pltpu.SemaphoreType.DMA((4, 4))],
        flops=2 * rows * half * D,
        moved=10 << 20,
        name="down_own",
    )


def lanes_of(rows, low):
    lane = lax.broadcasted_iota(jnp.int32, (rows, LANES), 1)
    return lane < LANES // 2 if low else lane >= LANES // 2


def split3(values):
    first = values.astype(BF16)
    rest = values - first.astype(F32)
    second = rest.astype(BF16)
    third = (rest - second.astype(F32)).astype(BF16)
    return first, second, third


def forward_kernel(
    rows, halo, block,
    word, q_ref, kh_ref, ko_ref, vh_ref, vo_ref, lo_ref, ek_ref, eq_ref, o_ref, e_ref,
):
    lane = lax.broadcasted_iota(jnp.int32, (block, LANES), 1)
    for q0 in range(0, rows, block):
        k0 = max(0, halo + q0 - WIN) // block * block
        k1 = halo + q0 + block
        q = q_ref[0, q0 : q0 + block, :]
        lo = lo_ref[0, q0 : q0 + block, :]
        outs = []
        for t in range(2):
            keep = lanes_of(block, t == 0)
            eq = jnp.broadcast_to(eq_ref[0, t : t + 1, :], (block, LANES))
            qcat = jnp.concatenate([q, eq.astype(BF16)], axis=1)
            tiles = []
            for kb in range(k0, k1, block):
                k = kh_ref[0, kb : kb + block, :] if kb < halo else ko_ref[0, kb - halo : kb - halo + block, :]
                kcat = jnp.concatenate(
                    [jnp.where(keep, k, jnp.zeros_like(k)), ek_ref[kb : kb + block, :]], axis=1
                )
                s = dot_nt(qcat, kcat)
                kidx = lax.broadcasted_iota(jnp.int32, (block, block), 1) + kb
                allowed = kidx >= lo
                if kb + block == k1:
                    qidx = lax.broadcasted_iota(jnp.int32, (block, block), 0) + (halo + q0)
                    allowed = allowed & (kidx <= qidx)
                tiles.append(jnp.where(allowed, s, MASKED))
            top = functools.reduce(jnp.maximum, tiles)
            m = jnp.max(top, axis=1, keepdims=True)
            product = None
            for kb, s in zip(range(k0, k1, block), tiles):
                if kb < halo:
                    v = vh_ref[0, kb : kb + block, :]
                else:
                    v = vo_ref[0, kb - halo : kb - halo + block, :]
                part = dot_nn(
                    jnp.exp(s - m).astype(BF16), jnp.concatenate([v, jnp.ones_like(v)], axis=1)
                )
                product = part if product is None else product + part
            total = product[:, LANES : LANES + 1]
            outs.append(product[:, :LANES] / total)
            first, second, third = split3(-(m + jnp.log(total)))
            e = jnp.where(lane == 6, first.astype(F32), eq)
            e = jnp.where(lane == 7, second.astype(F32), e)
            e = jnp.where(lane == 8, third.astype(F32), e)
            e_ref[0, t, q0 : q0 + block, :] = e.astype(BF16)
        o_ref[0, q0 : q0 + block, :] = jnp.where(lanes_of(block, True), outs[0], outs[1]).astype(
            BF16
        )


def attend(word, which, q, kh, ko, vh, vo, lo, ek, eq):
    _, rows, width = q.shape
    halo = kh.shape[1]
    pairs = width // LANES
    block = min(256, rows)
    spec = lambda n: pl.BlockSpec((1, n, LANES), lambda p: (which, 0, p))
    count = pairs * 2 * rows * (WIN + block)
    return call(
        functools.partial(forward_kernel, rows, halo, block),
        [sds(1, rows, width), kept(1, 2 * pairs, rows, LANES)],
        word, *streamed(q, kh, ko, vh, vo), lo, ek, eq,
        grid=(pairs,),
        in_specs=[
            SCALARS,
            spec(rows), spec(halo), spec(rows), spec(halo), spec(rows),
            pl.BlockSpec((1, rows, 1), lambda p: (which, 0, 0)),
            fixed(halo + rows, LANES),
            pl.BlockSpec((1, 2, LANES), lambda p: (p, 0, 0)),
        ],
        out_specs=[
            pl.BlockSpec((1, rows, LANES), lambda p: (0, 0, p)),
            pl.BlockSpec((1, 2, rows, LANES), lambda p: (0, p, 0, 0)),
        ],
        flops=count * 1024,
        moved=6 << 20,
        exps=count,
        name="attention_forward",
    )


def backward_kernel(
    rows, halo, block, begin, end, final,
    word, q_ref, kh_ref, ko_ref, vh_ref, vo_ref, o_ref, do_ref, e_ref, lo_ref, ek_ref, *refs,
):
    acc_ref = refs[-1]
    refs = list(refs[:-1])
    start_ref = refs.pop(0) if begin > 0 else None
    dq_ref = refs.pop(0)
    dkh_ref, dvh_ref = (refs.pop(0), refs.pop(0)) if begin == 0 else (None, None)
    dko_ref, dvo_ref = (refs.pop(0), refs.pop(0)) if final else (None, None)
    q = q_ref[0]
    do = do_ref[0]
    lo = lo_ref[0]
    lane = lax.broadcasted_iota(jnp.int32, (rows, LANES), 1)
    ones = jnp.where(lax.broadcasted_iota(jnp.int32, (block, LANES), 1) < 3, 1.0, 0.0).astype(BF16)
    product = do.astype(F32) * o_ref[0].astype(F32)
    qcats, docats, qts, dots = [], [], [], []
    for t in range(2):
        keep = lanes_of(rows, t == 0)
        delta = jnp.sum(jnp.where(keep, product, 0.0), axis=1, keepdims=True)
        first, second, third = split3(-delta)
        ed = jnp.where(lane == 0, first.astype(F32), 0.0)
        ed = jnp.where(lane == 1, second.astype(F32), ed)
        ed = jnp.where(lane == 2, third.astype(F32), ed)
        qcats.append(jnp.concatenate([q, e_ref[0, t]], axis=1))
        docats.append(jnp.concatenate([do, ed.astype(BF16)], axis=1))
        qts.append(jnp.where(keep, q, jnp.zeros_like(q)))
        dots.append(jnp.where(keep, do, jnp.zeros_like(do)))
    acc_ref[...] = jnp.zeros_like(acc_ref) if start_ref is None else start_ref[0]
    for kb in range(begin, end, block):
        if kb < halo:
            k_in, v_in, dk_out, dv_out, at = kh_ref, vh_ref, dkh_ref, dvh_ref, kb
        else:
            k_in, v_in, dk_out, dv_out, at = ko_ref, vo_ref, dko_ref, dvo_ref, kb - halo
        qlo = max(0, kb - halo)
        qhi = min(rows, -(-(kb + block - 1 + WIN - halo) // block) * block)
        if qhi <= qlo:
            dk_out[0, at : at + block, :] = jnp.zeros((block, LANES), BF16)
            dv_out[0, at : at + block, :] = jnp.zeros((block, LANES), BF16)
            continue
        k = k_in[0, at : at + block, :]
        v = v_in[0, at : at + block, :]
        ek = ek_ref[kb : kb + block, :]
        kidx = lax.broadcasted_iota(jnp.int32, (block, qhi - qlo), 0) + kb
        allowed = kidx >= lo[:, qlo:qhi]
        if kb + block > halo + qlo:
            qidx = lax.broadcasted_iota(jnp.int32, (block, qhi - qlo), 1) + (halo + qlo)
            allowed = allowed & (kidx <= qidx)
        pts, dss, kts = [], [], []
        for t in range(2):
            keep = lanes_of(block, t == 0)
            kt = jnp.where(keep, k, jnp.zeros_like(k))
            vt = jnp.where(keep, v, jnp.zeros_like(v))
            st = dot_nt(jnp.concatenate([kt, ek], axis=1), qcats[t][qlo:qhi])
            pt = jnp.exp(jnp.where(allowed, st, MASKED))
            dpt = dot_nt(jnp.concatenate([vt, ones], axis=1), docats[t][qlo:qhi])
            pts.append(pt.astype(BF16))
            dss.append((pt * dpt).astype(BF16))
            kts.append(kt)
        dv = dot_nn(jnp.concatenate(pts, axis=1), jnp.concatenate([d[qlo:qhi] for d in dots], axis=0))
        dk = dot_nn(jnp.concatenate(dss, axis=1), jnp.concatenate([d[qlo:qhi] for d in qts], axis=0))
        dv_out[0, at : at + block, :] = dv.astype(BF16)
        dk_out[0, at : at + block, :] = dk.astype(BF16)
        acc_ref[:, qlo:qhi] += dot_tn(jnp.concatenate(kts, axis=0), jnp.concatenate(dss, axis=0))
    if final:
        scale = 1.0 / math.sqrt(LANES // 2)
        dq_ref[0] = (acc_ref[...].T * scale).astype(BF16)
    else:
        dq_ref[0] = acc_ref[...]


def attend_back(word, which, q, kh, ko, vh, vo, o, do, e, lo, ek, start=None):
    _, rows, width = q.shape
    halo = kh.shape[1]
    pairs = width // LANES
    block = min(256, rows)
    begin, end, final = (0, halo, False) if start is None else (halo, halo + rows, True)
    spec = lambda n: pl.BlockSpec((1, n, LANES), lambda p: (which, 0, p))
    only = lambda n: pl.BlockSpec((1, n, LANES), lambda p: (0, 0, p))
    sums = pl.BlockSpec((1, LANES, rows), lambda p: (0, p, 0))
    count = pairs * 2 * rows * (WIN + block) * (end - begin) // (halo + rows)
    if final:
        shapes, specs = [sds(1, rows, width)] * 3, [only(rows)] * 3
    else:
        shapes = [sds(1, width, rows, dtype=F32)] + [sds(1, halo, width)] * 2
        specs = [sums, only(halo), only(halo)]
    return call(
        functools.partial(backward_kernel, rows, halo, block, begin, end, final),
        shapes,
        word, *streamed(q, kh, ko, vh, vo), o, do, *streamed(e), lo, ek,
        *([] if start is None else [start]),
        grid=(pairs,),
        in_specs=[
            SCALARS,
            spec(rows), spec(halo), spec(rows), spec(halo), spec(rows), only(rows), spec(rows),
            pl.BlockSpec((1, 2, rows, LANES), lambda p: (0, p, 0, 0)),
            pl.BlockSpec((1, 1, rows), lambda p: (which, 0, 0)),
            fixed(halo + rows, LANES),
        ]
        + ([] if start is None else [sums]),
        out_specs=specs,
        scratch_shapes=[pltpu.VMEM((LANES, rows), F32)],
        flops=count * 2304,
        moved=8 << 20,
        exps=count,
        name="attention_backward",
    )


def act_back_kernel(
    me_ref, own, other, slope_own, slope_other, w0, w1, w2, w3, w4,
    du_own, du_other, sums, w, sems,
):
    copies = fetches(me_ref[0], (w0, w1, w2, w3, w4), wanted_down(w), sems)
    step = pl.program_id(0)

    @pl.when(step == 0)
    def _():
        start_all(copies)
        for group in copies:
            wait_group(group)

    rows = own.shape[0]
    piece = min(256, rows)
    w_part = w[pl.ds(pl.multiple_of(step * 512, 512), 512), :]
    total = jnp.zeros((1, 512), F32)
    for dy, slope, du in ((other, slope_other, du_other), (own, slope_own, du_own)):
        for r in range(0, rows, piece):
            grad = dot_nt(dy[r : r + piece], w_part) * slope[r : r + piece].astype(F32)
            rounded = grad.astype(BF16)
            du[r : r + piece] = rounded
            total += column_sum(rounded)
    sums[...] = jnp.broadcast_to(total, (8, 512))


def act_back(me, own, other, slope_own, slope_other, pieces):
    rows = own.shape[0]
    half = FF // 2
    columns = pl.BlockSpec((rows, 512), lambda j: (0, j))
    return call(
        act_back_kernel,
        [sds(rows, half), sds(rows, half), sds(8, half, dtype=F32)],
        me, own, other, *streamed(slope_own, slope_other), *pieces,
        grid=(4,),
        in_specs=[SCALARS, fixed(rows, D), fixed(rows, D), columns, columns] + [ANYWHERE] * 5,
        out_specs=[columns, columns, pl.BlockSpec((8, 512), lambda j: (0, j))],
        scratch_shapes=[pltpu.VMEM((half, D), BF16), pltpu.SemaphoreType.DMA((4, 4))],
        flops=4 * rows * half * D,
        moved=16 << 20,
        name="act_back",
    )


def up_back_kernel(me_ref, du, w0, w1, w2, w3, w4, p_ref, w, sems):
    copies = fetches(me_ref[0], (w0, w1, w2, w3, w4), wanted_up(w), sems)
    start_all(copies)
    for group in copies:
        wait_group(group)
    p_ref[...] = dot_nt(du[...], w[...]).astype(BF16)


def up_back_other(me, du, pieces):
    rows, half = du.shape
    return call(
        up_back_kernel,
        sds(rows, D),
        me, du, *pieces,
        grid=(1,),
        in_specs=[SCALARS, fixed(rows, half)] + [ANYWHERE] * 5,
        out_specs=fixed(rows, D),
        scratch_shapes=[pltpu.VMEM((D, half), BF16), pltpu.SemaphoreType.DMA((4, 4))],
        flops=2 * rows * half * D,
        moved=7 << 20,
        name="up_back_other",
    )


def middle_back_kernel(
    me_ref, du, got, x1, dy, gain, w0, w1, w2, w3, w4, dx1_ref, db_ref, sums, w, sems
):
    copies = fetches(me_ref[0], (w0, w1, w2, w3, w4), wanted_up(w), sems)
    start_all(copies)
    normal, inverse = normalize(x1[...])
    for group in copies:
        wait_group(group)
    dh = dot_nt(du[...], w[...]) + got[...].astype(F32)
    top = dy[...].astype(F32)
    dx1 = top + norm_back(dh * gain[...], normal, inverse)
    dx1_ref[...] = dx1
    db = dx1.astype(BF16)
    db_ref[...] = db
    sums[0:1] = column_sum(dh * normal)
    sums[1:2] = column_sum(dh)
    sums[2:3] = column_sum(db)
    sums[3:4] = column_sum(top)
    sums[4:8] = jnp.zeros((4, D), F32)


def middle_back(me, du, got, x1, dy, gain, pieces):
    rows, half = du.shape
    return call(
        middle_back_kernel,
        [sds(rows, D, dtype=F32), sds(rows, D), sds(8, D, dtype=F32)],
        me, du, got, x1, dy, gain, *pieces,
        grid=(1,),
        in_specs=[SCALARS, fixed(rows, half)]
        + [fixed(rows, D)] * 3
        + [fixed(1, D)]
        + [ANYWHERE] * 5,
        out_specs=[fixed(rows, D), fixed(rows, D), fixed(8, D)],
        scratch_shapes=[pltpu.VMEM((D, half), BF16), pltpu.SemaphoreType.DMA((4, 4))],
        flops=2 * rows * half * D,
        moved=14 << 20,
        name="middle_back",
    )


def out_back_kernel(me_ref, own, other, w0, w1, w2, w3, w4, do_ref, w, sems):
    copies = fetches(me_ref[0], (w0, w1, w2, w3, w4), wanted_out(w), sems)
    start_all(copies)
    for group in copies:
        wait_group(group)
    do_ref[0] = dot_nt(own[...], w[...]).astype(BF16)
    do_ref[1] = dot_nt(other[...], w[...]).astype(BF16)


def out_back(me, own, other, pieces):
    rows = own.shape[0]
    half = D // 2
    return call(
        out_back_kernel,
        sds(2, rows, half),
        me, own, other, *pieces,
        grid=(1,),
        in_specs=[SCALARS, fixed(rows, D), fixed(rows, D)] + [ANYWHERE] * 5,
        out_specs=fixed(2, rows, half),
        scratch_shapes=[pltpu.VMEM((half, D), BF16), pltpu.SemaphoreType.DMA((2, 4))],
        flops=4 * rows * half * D,
        moved=4 << 20,
        name="out_back",
    )


def store_parts(step, parts_x, parts_y, send_x, send_y, keep_x, keep_y):
    def put(ref, pieces):
        row = 0
        for piece in pieces:
            ref[0, row : row + piece.shape[0]] = piece
            row += piece.shape[0]

    @pl.when(step < 2)
    def _():
        put(send_x, parts_x)

    @pl.when(step >= 2)
    def _():
        put(keep_x, parts_x)

    @pl.when(step % 2 == 0)
    def _():
        put(send_y, parts_y)

    @pl.when(step % 2 == 1)
    def _():
        put(keep_y, parts_y)


def part_outputs(rows):
    shapes = [kept(2, rows, 512)] * 4
    specs = [
        pl.BlockSpec((1, rows, 512), lambda i, order: (jnp.minimum(i, 1), 0, 0)),
        pl.BlockSpec((1, rows, 512), lambda i, order: (i // 2, 0, 0)),
        pl.BlockSpec((1, rows, 512), lambda i, order: (i // 3, 0, 0)),
        pl.BlockSpec((1, rows, 512), lambda i, order: (i // 3, 0, 0)),
    ]
    return shapes, specs


def down_grad_kernel(order, act_own, act_other, own, other, *outs):
    grad = (dot_tn(act_own[...], own[...]) + dot_tn(act_other[...], other[...])).astype(BF16)
    store_parts(
        pl.program_id(0),
        [grad[:256, :512], grad[:256, 512:]],
        [grad[256:, :512], grad[256:, 512:]],
        *outs,
    )


def down_grad(order, act_own, act_other, own, other):
    rows = own.shape[0]
    shapes, specs = part_outputs(512)
    columns = pl.BlockSpec((rows, 512), lambda i, order: (0, order[i]))
    full = pl.BlockSpec((rows, D), lambda i, order: (0, 0))
    return call(
        down_grad_kernel,
        shapes,
        order, *streamed(act_own, act_other), own, other,
        grid_spec=pltpu.PrefetchScalarGridSpec(
            num_scalar_prefetch=1,
            grid=(4,),
            in_specs=[columns, columns, full, full],
            out_specs=specs,
        ),
        flops=4 * rows * (FF // 2) * D,
        moved=10 << 20,
        name="down_grad",
    )


def up_grad_kernel(
    order, h_own, h_other, du_own, du_other, o_own, o_other, db_own, db_other, *outs
):
    grad = (dot_tn(h_own[...], du_own[...]) + dot_tn(h_other[...], du_other[...])).astype(BF16)
    out_part = (dot_tn(o_own[0], db_own[...]) + dot_tn(o_other[0], db_other[...])).astype(BF16)
    store_parts(
        pl.program_id(0),
        [grad[:, :512], grad[:, 512:1024], out_part[:, :512]],
        [grad[:, 1024:1536], grad[:, 1536:], out_part[:, 512:]],
        *outs,
    )


def up_grad(order, h_own, h_other, du_own, du_other, o_own, o_other, db_own, db_other):
    rows = h_own.shape[0]
    half = FF // 2
    shapes, specs = part_outputs(640)
    columns = pl.BlockSpec((rows, 256), lambda i, order: (0, order[i]))
    full = lambda width: pl.BlockSpec((rows, width), lambda i, order: (0, 0))
    heads = pl.BlockSpec((1, rows, 128), lambda i, order: (0, 0, order[i]))
    return call(
        up_grad_kernel,
        shapes,
        order, h_own, h_other, du_own, du_other, o_own, o_other, db_own, db_other,
        grid_spec=pltpu.PrefetchScalarGridSpec(
            num_scalar_prefetch=1,
            grid=(4,),
            in_specs=[columns, columns, full(half), full(half), heads, heads, full(D), full(D)],
            out_specs=specs,
        ),
        flops=4 * rows * half * D + 2 * rows * D * D,
        moved=14 << 20,
        name="up_grad",
    )


def qkv_grad_kernel(order, a_own, a_halo, *refs):
    dq, dko, dvo, dkh, dvh = (refs[2 * i : 2 * i + 2] for i in range(5))
    *parts, sums = refs[10:]

    def total(pairs):
        return sum(dot_tn(left[m], right[m][0]) for left, right in pairs for m in range(2)).astype(BF16)

    k_part = total([(a_own, dko), (a_halo, dkh)])
    first = [total([(a_own, dq)]), k_part[:128]]
    second = [k_part[128:], total([(a_own, dvo), (a_halo, dvh)])]
    store_parts(pl.program_id(0), first, second, *parts)

    @pl.when(pl.program_id(0) == 0)
    def _():
        sums[0:1] = column_sum(dq[0][0]) + column_sum(dq[1][0])
        sums[1:2] = sum(column_sum(ref[0]) for ref in (*dvo, *dvh))
        sums[2:8] = jnp.zeros((6, sums.shape[1]), F32)


def qkv_grad(order, a_own, a_halo, *grads):
    rows, halo = a_own.shape[1], a_halo.shape[1]
    half = D // 2
    shapes, specs = part_outputs(384)
    full = lambda n: pl.BlockSpec((1, n, half), lambda i, order: (0, 0, 0))
    columns = lambda n: pl.BlockSpec((2, n, 256), lambda i, order: (0, 0, order[i]))
    return call(
        qkv_grad_kernel,
        shapes + [sds(8, half, dtype=F32)],
        order, a_own, a_halo, *[ref for pair in grads for ref in pair],
        grid_spec=pltpu.PrefetchScalarGridSpec(
            num_scalar_prefetch=1,
            grid=(4,),
            in_specs=[columns(rows), columns(halo)]
            + [full(rows)] * 6
            + [full(halo)] * 4,
            out_specs=specs + [pl.BlockSpec((8, half), lambda i, order: (0, 0))],
        ),
        flops=4 * D * half * (3 * rows + 2 * halo),
        moved=16 << 20,
        name="qkv_grad",
    )


def normed_back_kernel(hops, me_ref, *refs):
    wanted = (1, 2) if hops else (0, 1, 2)
    count = len(wanted)
    grads, a_ref, refs = refs[:count], refs[count], refs[count + 1 :]
    *outs, sums, w, sems = refs[5:]
    got = outs.pop(0) if len(outs) > max(hops, 1) else None
    copies = fetches(me_ref[0], refs[:5], wanted_qkv(w, wanted), sems)
    start_all(copies)
    for group in copies:
        wait_group(group)
    weighted = jnp.zeros((1, D), F32)
    plain = jnp.zeros((1, D), F32)
    rows = outs[0].shape[0] if got is not None else a_ref.shape[1] // max(hops, 1)
    for number in range(max(hops, 1)):
        r = slice(number * rows, (number + 1) * rows)
        da = sum(dot_nt(grad[0, r], w[i]) for i, grad in enumerate(grads))
        weighted += column_sum(da * a_ref[0, r].astype(F32))
        plain += column_sum(da)
        if got is None:
            outs[0][r] = da.astype(BF16)
        else:
            da = da + got[r].astype(F32)
            outs[number][...] = da.astype(outs[number].dtype)
    sums[0:1] = weighted
    sums[1:2] = plain
    sums[2:8] = jnp.zeros((6, D), F32)


def normed_back(me, which, hops, grads, a, pieces, got=None):
    length = a.shape[1]
    rows = length // max(hops, 1)
    half = D // 2
    count = len(grads)
    if got is None:
        outs, out_specs = [sds(length, D)], [fixed(length, D)]
    elif hops:
        outs, out_specs = [sds(rows, D)] * hops, [fixed(rows, D)] * hops
    else:
        outs, out_specs = [sds(rows, D, dtype=F32)], [fixed(rows, D)]
    return call(
        functools.partial(normed_back_kernel, hops),
        outs + [sds(8, D, dtype=F32)],
        me, *grads, a, *pieces, *([] if got is None else [got]),
        grid=(1,),
        in_specs=[SCALARS]
        + [fixed(1, length, half)] * count
        + [pl.BlockSpec((1, length, D), lambda i: (which, 0, 0))]
        + [ANYWHERE] * 5
        + ([] if got is None else [fixed(length, D)]),
        out_specs=out_specs + [fixed(8, D)],
        scratch_shapes=[pltpu.VMEM((count, D, half), BF16), pltpu.SemaphoreType.DMA((count, 4))],
        flops=2 * count * length * half * D,
        moved=8 << 20,
        name="normed_back",
    )


def first_back_kernel(word, da_ref, got, x_ref, dx1, gain, dx_ref, low_ref):
    da = da_ref[...] + got[...].astype(F32)
    normal, inverse = normalize(x_ref[...].astype(F32))
    dx = dx1[...] + norm_back(da * gain[...], normal, inverse)
    dx_ref[...] = dx
    low_ref[...] = dx.astype(BF16)


def first_back(word, da, got, x, dx1, gain):
    rows = da.shape[0]
    return call(
        first_back_kernel,
        [sds(rows, D, dtype=F32), sds(rows, D)],
        word, da, got, x, dx1, gain,
        grid=(1,),
        in_specs=[SCALARS] + [fixed(rows, D)] * 4 + [fixed(1, D)],
        out_specs=[fixed(rows, D), fixed(rows, D)],
        moved=10 << 20,
        name="first_back",
    )


def unpack_down_kernel(core_ref, kept, got, out):
    core = core_ref[0]
    for half, source in ((core, kept), (1 - core, got)):
        for rh in range(2):
            for j in range(2):
                at = (rh * 2 + j) * 256
                rows = pl.ds(pl.multiple_of(half * 512 + rh * 256, 256), 256)
                out[0, rows, j * 512 : (j + 1) * 512] = source[at : at + 256].astype(F32)


def unpack_up_kernel(core_ref, kept_part, got, out_up, out_out):
    core = core_ref[0]
    for half, source in ((core, kept_part), (1 - core, got)):
        for j in range(4):
            at = (j // 2) * 640 + (j % 2) * 256
            columns = pl.ds(pl.multiple_of(j * 1024 + half * 512, 512), 512)
            out_up[0, :, columns] = source[at : at + 256].astype(F32)
        rows = pl.ds(pl.multiple_of(half * 128, 128), 128)
        for j in range(2):
            at = j * 640 + 512
            out_out[0, rows, j * 512 : (j + 1) * 512] = source[at : at + 128].astype(F32)


def unpack_qkv_kernel(core_ref, kept_part, got, out):
    core = core_ref[0]
    for half, source in ((core, kept_part), (1 - core, got)):
        for g in range(3):
            for f in range(4):
                columns = pl.ds(pl.multiple_of((g * 4 + f) * 256 + half * 128, 128), 128)
                out[0, :, columns] = source[
                    g * 256 : (g + 1) * 256, f * 128 : (f + 1) * 128
                ].astype(F32)


def unpack(kernel, core, pieces, shapes, name):
    return call(
        kernel,
        shapes,
        core, *pieces,
        in_specs=[SCALARS] + [INSIDE] * len(pieces),
        out_specs=jax.tree.map(lambda _: INSIDE, shapes),
        moved=10 << 20,
        name=name,
    )


def split_vector(values):
    pieces, offset = [], 0
    for length in (D, D, D, D, D, D, D, FF, D):
        pieces.append(values[offset : offset + length])
        offset += length
    return pieces


def shards(inputs, cotangent, segments, w_qkv, w_out, w_up, w_down, vectors):
    core = lax.axis_index("section")
    column = lax.axis_index("ctx")
    fs = lax.axis_index("fsdp")
    nf = lax.axis_size("fsdp")
    rows = inputs.shape[2]
    reach = (WIN - 1) // rows + 1
    halo = reach * rows
    first_core = core == 0
    me = fs.astype(jnp.int32).reshape(1)
    core_word = core.astype(jnp.int32).reshape(1)
    order = jnp.stack([fs ^ r for r in ROLL]).astype(jnp.int32)

    def pick(here, there):
        return jnp.where(first_core, here, there), jnp.where(first_core, there, here)

    mine = lambda values: lax.dynamic_index_in_dim(values, core, 0, keepdims=False)
    theirs = lambda values: lax.dynamic_index_in_dim(values, 1 - core, 0, keepdims=False)
    x_own, x_other = mine(inputs[:, 0]), theirs(inputs[:, 0])
    keep_a, send_a, keep_u, send_u, keep_d, send_d = pack_weights(
        tie(core_word, x_own), w_qkv, w_out, w_up, w_down
    )
    shard_a = pick(keep_a, swap(send_a))
    later = lambda value: tie(value, shard_a[0])

    shard_u = pick(keep_u, swap(later(send_u)))
    shard_d = pick(keep_d, swap(later(send_d)))
    both = tie(jnp.concatenate(pick(vectors, swap(vectors))), shard_u, shard_d)
    near = flip(both, "fsdp", 1)
    low_x = (fs & 1) == 0
    pair = jnp.concatenate([jnp.where(low_x, both, near), jnp.where(low_x, near, both)], 1)
    far = flip(pair, "fsdp", 2)
    low_y = (fs & 2) == 0
    packed = jnp.concatenate([jnp.where(low_y, pair, far), jnp.where(low_y, far, pair)], 1)
    packed = packed.astype(F32)

    a0 = Gather(shard_a[0])
    u0 = Gather(shard_u[0], a0.far)
    d0 = Gather(shard_d[0], a0.far)
    a1 = Gather(shard_a[1], d0.near)
    u1 = Gather(shard_u[1], a1.far)
    d1 = Gather(shard_d[1], a1.far)
    weights = ((a0, u0, d0), (a1, u1, d1))

    top = later(cotangent[:, 0])
    top_own, top_other = mine(top), theirs(top)
    marks = later(segments[:, 0])
    starts = jnp.stack([mine(marks), theirs(marks)])
    position = column * rows + jnp.arange(rows, dtype=jnp.int32)
    lo = jnp.maximum(starts, position[None] - (WIN - 1)) - (column * rows - halo)
    lo_column, lo = lo[:, :, None], lo[:, None, :]

    nought = later(jnp.zeros((), jnp.int32))
    key_index = lax.broadcasted_iota(jnp.int32, (halo + rows, LANES), 0) + nought
    lane = lax.broadcasted_iota(jnp.int32, (halo + rows, LANES), 1)
    placed = jnp.where(lane % 2 == 0, key_index // 256 * 256, key_index % 256)
    ek = jnp.where(lane < 6, placed, jnp.where(lane < 9, 1, 0)).astype(BF16)
    local_heads = HEADS // 2
    per_group = local_heads // nf
    local = jnp.arange(local_heads) + nought
    head = (local // per_group) * (2 * per_group) + core * per_group + local % per_group
    slopes = jnp.exp2(-0.5 * (head.astype(F32) + 1.0)) * (4.0 / WIN)
    first, second, third = [values.astype(F32) for values in split3(slopes)]
    eq = jnp.concatenate(
        [
            jnp.stack([first, first, second, second, third, third], 1),
            jnp.zeros((local_heads, LANES - 6), F32),
        ],
        1,
    ).reshape(local_heads // 2, 2, LANES)

    def start_halo(own, *after):
        pieces, block = [], own
        for hop in range(reach):
            block = step_along(tie(block, *after) if hop == 1 else block, "ctx", 1)
            pieces.append(block)
        return pieces

    def finish_return(first, hops, *after):
        carried, sent = first, first
        for hop, piece in enumerate(hops[1:]):
            sent = add_bf16(piece, tie(carried, *after) if hop == 0 else carried)
            carried = step_along(sent, "ctx", -1)
        return carried, sent

    def my_half(values, groups):
        view = values.reshape(groups, 2, -1)
        return jnp.where(first_core, view[:, 0], view[:, 1]).reshape(1, -1)

    def widen(values, groups):
        view = values.reshape(groups, 1, -1)
        zero = jnp.zeros_like(view)
        return jnp.where(
            first_core, jnp.concatenate([view, zero], 1), jnp.concatenate([zero, view], 1)
        ).reshape(-1)

    line = Line()
    run = line.run

    def forward(layer, x_own, x_other, first_hops):
        g1, b1, bq, bv, bo, g2, b2, bu, bd = [
            values.reshape(1, -1) for values in split_vector(packed[layer])
        ]
        bq, bv, bu = my_half(bq, nf), my_half(bv, nf), my_half(bu, nf)
        ga, gu, gd = weights[layer]
        wa, wu, wd = ga.pieces, gu.pieces, gd.pieces
        a_own, q, ko, vo = run(
            make_qkv, me, x_own, x_other, g1, b1, bq, bv, wa,
            after=(ek, eq, lo, lo_column, bu, first_hops if layer == 0 else ()),
        )
        earlier = ()
        for hop, block in enumerate(first_hops):
            block = tie(block, line.token if hop == 0 else ())
            earlier = run(
                make_kv, me, block, swap(block), reach, reach - 1 - hop, earlier, g1, b1, bv, wa,
                after=first_hops if hop == 0 else (),
            )
        a_halo, kh, vh = earlier
        o_other, e_other = run(
            attend, me, 1, q, kh, ko, vh, vo, lo_column, ek, eq, after=(gu.near,)
        )
        part = run(out_other, me, o_other, wa)
        o_own, e_own = run(
            attend, me, 0, q, kh, ko, vh, vo, lo_column, ek, eq, after=(gd.near,)
        )
        x1, h_own = run(
            middle, me, o_own, swap(part), x_own, bo, g2, b2, wa, after=(gu.far,)
        )
        o, e = (o_own, o_other), (e_own, e_other)
        h_other = swap(h_own)
        act_own, slope_own = run(up, me, h_own, bu, wu)
        act_other, slope_other = run(up, me, h_other, bu, wu)
        part = run(down_other, me, act_other, wd)
        y = run(last, me, act_own, swap(part), x1, bd, wd)
        stored = (
            x_own, a_own, a_halo, q, kh, ko, vh, vo, o, e, x1, h_own, h_other,
            act_own, slope_own, act_other, slope_other, g1, b1, g2,
        )
        return y, stored

    y0, stored0 = forward(0, x_own, x_other, start_halo(x_own, shard_a[0]))
    y0_other = swap(y0)
    y1, stored1 = forward(1, y0, y0_other, start_halo(y0, a1.near))
    y1_other = swap(y1)

    column_sums = Column()

    def step(block, *after):
        column_sums.step(block, line.token, *after)
        line.also += column_sums.sent

    def backward(layer, top_own, top_other, stored, before=()):
        last_layer = layer == 0
        (
            x_own, a_own, a_halo, q, kh, ko, vh, vo, o, e, x1, h_own, h_other,
            act_own, slope_own, act_other, slope_other, g1, b1, g2,
        ) = stored
        wa, wu, wd = (group.pieces for group in weights[layer])
        du_own, du_other, sums_up = run(
            act_back, me, top_own, top_other, slope_own, slope_other, wd
        )
        got = swap(run(up_back_other, me, du_other, wu))
        down_part = Scatter(*run(down_grad, order, act_own, act_other, top_own, top_other))
        if last_layer:
            before[1].third(line.token)
        dx1, db_own, sums_middle = run(middle_back, me, du_own, got, x1, top_own, g2, wu)
        db_other = swap(db_own)
        do = run(out_back, me, db_own, db_other, wa)
        up_part = Scatter(
            *run(up_grad, order, h_own, h_other, du_own, du_other, *o, db_own, db_other)
        )
        if last_layer:
            step(before[0].piece)

        def early(m):
            return run(attend_back, me, m, q, kh, ko, vh, vo, o[m], do, e[m], lo, ek)

        def own(m, start):
            return run(attend_back, me, m, q, kh, ko, vh, vo, o[m], do, e[m], lo, ek, start)

        begun_other, dkh_other, dvh_other = early(1)
        down_part.second(line.token)
        line.also += (down_part.half,)
        if last_layer:
            step(before[1].piece)
        part, sums_a = run(normed_back, me, 1, reach, (dkh_other, dvh_other), a_halo, wa)
        got = swap(part)
        begun_own, dkh_own, dvh_own = early(0)
        down_part.third(line.token)
        line.also = (down_part.piece,)
        *hops, sums_b = run(normed_back, me, 0, reach, (dkh_own, dvh_own), a_halo, wa, got)
        first = step_along(hops[0], "ctx", -1)
        carried = sent = first
        if last_layer:
            step(down_part.piece, hops)
        else:
            carried, sent = finish_return(first, hops)
        dq_other, dko_other, dvo_other = own(1, begun_other)
        part, sums_c = run(normed_back, me, 1, 0, (dq_other, dko_other, dvo_other), a_own, wa)
        got = swap(part)
        up_part.second(line.token)
        line.also += (up_part.half,)
        dq_own, dko_own, dvo_own = own(0, begun_own)
        *parts, sums_qkv = run(
            qkv_grad, order, a_own, a_halo, (dq_own, dq_other), (dko_own, dko_other),
            (dvo_own, dvo_other), (dkh_own, dkh_other), (dvh_own, dvh_other),
            after=(column_sums.outer_got, column_sums.inner_got) if last_layer else (sent,),
        )
        qkv_part = Scatter(*parts)
        up_part.third(line.token)
        line.also = (up_part.piece,)
        if last_layer:
            step(up_part.piece)
        da, sums_d = run(
            normed_back, me, 0, 0, (dq_own, dko_own, dvo_own), a_own, wa, got,
            after=() if last_layer else (carried,),
        )
        qkv_part.second(line.token)
        line.also += (qkv_part.half,)
        if last_layer:
            carried, sent = finish_return(first, hops, line.token)
            line.also += (sent,)
            qkv_part.third()
            step(qkv_part.piece)
        dx, dx_low = run(first_back, me, da, carried, x_own, dx1, g1)
        if not last_layer:
            step(down_part.piece)
        plain = sums_a[1] + sums_b[1] + sums_c[1] + sums_d[1]
        weighted = sums_a[0] + sums_b[0] + sums_c[0] + sums_d[0]
        vector = jnp.concatenate(
            [
                (weighted - b1[0] * plain) / g1[0], plain, widen(sums_qkv[0], nf),
                widen(sums_qkv[1], nf), sums_middle[2], sums_middle[0], sums_middle[1],
                widen(sums_up[0], nf), sums_middle[3],
            ]
        )
        return dx, dx_low, (up_part, qkv_part), vector

    _, dx1, parts1, vector1 = backward(1, top_own, top_other, stored1)
    dx1_other = swap(dx1)
    dx0, _, _, vector0 = backward(0, dx1, dx1_other, stored0, parts1)
    dx0_other = swap(dx0)
    stages = sums_over_all(jnp.stack([vector0, vector1]))
    step(None, stages[2])
    def by_micro(own, other):
        return jnp.where(first_core, jnp.stack([own, other]), jnp.stack([other, own]))

    activations = jnp.where(first_core, by_micro(y0, y0_other), by_micro(y1, y1_other))
    input_grad = jnp.where(
        first_core, by_micro(dx0, dx0_other), by_micro(dx1, dx1_other).astype(F32)
    )

    def exchange(first, second):
        kept, sent = pick(first, second)
        return kept, swap(sent)

    waiting = column_sums.outer_got, column_sums.inner_got
    waiting, activations, input_grad = lax.optimization_barrier((waiting, activations, input_grad))
    column_sums.outer_got, column_sums.inner_got = waiting
    step(None, stages[4])
    size = D // nf
    down1_sum, up1_sum, qkv1_sum, down0_sum, up0_sum, *_ = column_sums.sums
    grad_down = unpack(
        unpack_down_kernel, core_word, exchange(down0_sum, down1_sum),
        sds(1, FF // nf, D, dtype=F32), "unpack_down",
    )
    grad_up, grad_out = unpack(
        unpack_up_kernel, core_word, exchange(up0_sum, up1_sum),
        [sds(1, size, FF, dtype=F32), sds(1, size, D, dtype=F32)], "unpack_up",
    )
    waiting = column_sums.outer_got
    waiting, grad_down, grad_up, grad_out = lax.optimization_barrier(
        (waiting, grad_down, grad_up, grad_out)
    )
    column_sums.outer_got = waiting
    step(None, stages[-1])
    qkv0_sum = column_sums.sums[-1]
    grad_qkv = unpack(
        unpack_qkv_kernel, core_word, exchange(qkv0_sum, qkv1_sum),
        sds(1, size, 3 * D, dtype=F32), "unpack_qkv",
    )
    summed = stages[-1]
    length = summed.shape[1] // nf
    grad_vectors = lax.dynamic_slice(summed, (core, fs * length), (1, length))
    return (
        activations[None, :, None], input_grad[None, :, None],
        grad_qkv, grad_out, grad_up, grad_down, grad_vectors,
    )


def solution(mesh):
    placed = (
        P(None, "fsdp", "ctx", None),
        P(None, "fsdp", "ctx", None),
        P(None, "fsdp", "ctx"),
        P("section", "fsdp", None),
        P("section", "fsdp", None),
        P("section", "fsdp", None),
        P("section", "fsdp", None),
        P("section", "fsdp"),
    )
    return jax.shard_map(
        shards,
        mesh=mesh,
        in_specs=placed,
        out_specs=(
            P("section", None, "fsdp", "ctx", None),
            P("section", None, "fsdp", "ctx", None),
            P("section", "fsdp", None),
            P("section", "fsdp", None),
            P("section", "fsdp", None),
            P("section", "fsdp", None),
            P("section", "fsdp"),
        ),
        check_vma=False,
    )
```

```python
import functools
import math

import jax
import jax.numpy as jnp
from jax import lax
from jax.experimental import pallas as pl
from jax.experimental.pallas import tpu as pltpu
from jax.sharding import PartitionSpec as P

D = 1024
HEADS = 16
FF = 4096
WIN = 1024

EPSILON = 1e-05
F32 = jnp.float32
BF16 = jnp.bfloat16
LANES = 128
MASKED = -1e30


LEAST = 256
ROLL = (3, 1, 2, 0)


def flip(block, axis, bit):
    count = lax.axis_size(axis)
    return lax.ppermute(block, axis, [(i, i ^ bit) for i in range(count)])


def step_along(block, axis, distance):
    devices = range(lax.axis_size(axis))
    route = [(i - distance, i) for i in devices if i - distance in devices]
    return lax.ppermute(block, axis, route)


def swap(block):
    return flip(block, "section", 1)


def tie(value, *after):
    return lax.optimization_barrier((value, after))[0]


class Gather:
    def __init__(self, shard, *after, then=()):
        shard = tie(shard, *after) if after else shard
        half = shard.shape[0] // 2
        self.near = flip(shard, "fsdp", 1), flip(shard, "fsdp", 2)
        from_x, from_y = tie(self.near, *then) if then else self.near
        self.far = flip(from_x[:half], "fsdp", 2), flip(from_y[half:], "fsdp", 1)
        self.pieces = (shard, *self.near, *self.far)


def add_bf16(*terms):
    return sum(term.astype(F32) for term in terms).astype(BF16)


class Scatter:
    def __init__(self, send_x, send_y, keep_x, keep_y):
        self.near = flip(send_x, "fsdp", 1), flip(send_y, "fsdp", 2)
        self.keep = keep_x, keep_y

    def second(self, *after):
        (got_x, got_y), (keep_x, keep_y) = tie(self.near, *after), self.keep
        self.half = add_bf16(keep_x[0], got_x[0]), add_bf16(keep_y[0], got_y[0])
        self.far = flip(self.half[0], "fsdp", 2), flip(self.half[1], "fsdp", 1)

    def third(self, *after):
        far_x, far_y = tie(self.far, *after)
        (got_x, got_y), (keep_x, keep_y) = self.near, self.keep
        self.piece = jnp.concatenate(
            [add_bf16(keep_x[1], got_x[1], far_x), add_bf16(keep_y[1], got_y[1], far_y)]
        )


class Column:
    def __init__(self):
        self.line = lax.axis_size("ctx") == 4
        me = lax.axis_index("ctx")
        self.inner = (me == 1) | (me == 2)
        self.block = self.half = self.total = self.outer_got = self.inner_got = None
        self.sums = []
        self.sent = ()

    def step(self, block, *after):
        if not self.line:
            if block is not None:
                self.sums.append(lax.psum(block, "ctx"))
            return
        outer_got, inner_got, block = tie((self.outer_got, self.inner_got, block), *after)
        half = total = None
        if self.block is not None:
            half = add_bf16(self.block, outer_got[: self.block.shape[0]])
        if self.half is not None:
            total = add_bf16(self.half, inner_got)
        if self.total is not None:
            outer_sum = outer_got[: self.total.shape[0]]
            self.sums.append(jnp.where(self.inner, self.total, outer_sum))
        self.block, self.half, self.total = block, half, total
        self.sent = ()
        if block is not None or total is not None:
            sent = total if block is None else block
            if block is not None and total is not None:
                rows = max(total.shape[0], block.shape[0])
                fill = lambda part: jnp.pad(part, ((0, rows - part.shape[0]), (0, 0)))
                sent = jnp.where(self.inner, fill(total), fill(block))
            self.outer_got = flip(sent, "ctx", 1)
            self.sent += (sent,)
        if half is not None:
            self.inner_got = lax.ppermute(half, "ctx", [(1, 2), (2, 1)])
            self.sent += (half,)


class Line:
    def __init__(self):
        self.token = ()
        self.also = ()

    def run(self, kernel, word, *args, after=()):
        word = tie(word, self.token, self.also, after)
        self.also = ()
        out = kernel(word, *args)
        self.token = out[0] if isinstance(out, (list, tuple)) else out
        return out


def sums_over_all(block):
    stages = [block]
    for axis in ("section", "fsdp", "ctx"):
        bit = 1
        while bit < lax.axis_size(axis):
            stages.append(stages[-1] + flip(stages[-1], axis, bit))
            bit *= 2
    return stages


def streamed(*arrays):
    return [pltpu.with_memory_space_constraint(array, pltpu.HBM) for array in arrays]


def call(kernel, out_shape, *operands, limit=28, flops=0, moved=0, exps=0, name=None, **rest):
    return pl.pallas_call(
        kernel,
        out_shape=out_shape,
        compiler_params=pltpu.CompilerParams(vmem_limit_bytes=limit * 1024 * 1024),
        cost_estimate=pl.CostEstimate(flops=flops, bytes_accessed=moved, transcendentals=exps),
        name=name,
        **rest,
    )(*operands)


def sds(*shape, dtype=BF16):
    return jax.ShapeDtypeStruct(shape, dtype)


def kept(*shape, dtype=BF16):
    return pltpu.HBM(shape, dtype)


ANYWHERE = pl.BlockSpec(memory_space=pltpu.HBM)
SCALARS = pl.BlockSpec(memory_space=pltpu.SMEM)
INSIDE = pl.BlockSpec(memory_space=pltpu.VMEM)


def fixed(*shape):
    return pl.BlockSpec(shape, lambda *_: (0,) * len(shape))


def fetches(me, pieces, wanted, sems):
    half = pieces[0].shape[0] // 2
    copies = []
    for number, (row, count, place) in enumerate(wanted):
        group = []
        for r in range(4):
            if r < 3:
                source = pieces[r].at[row : row + count]
            elif row < half:
                source = pieces[3].at[row : row + count]
            else:
                source = pieces[4].at[row - half : row - half + count]
            group.append(pltpu.make_async_copy(source, place(me ^ r), sems.at[number, r]))
        copies.append(group)
    return copies


def start_all(copies):
    for group in copies:
        for copy in group:
            copy.start()


def wait_group(group):
    for copy in group:
        copy.wait()


def part(a, size):
    return pl.ds(pl.multiple_of(a * size, size), size)


def wanted_qkv(w, which=(0, 1, 2)):
    return [
        (g * LEAST, LEAST, lambda a, i=i: w.at[i, part(a, LEAST)]) for i, g in enumerate(which)
    ]


def wanted_out(w):
    return [
        (3 * LEAST + j * 128, 128, lambda a, j=j: w.at[part(a, 128), j * 512 : (j + 1) * 512])
        for j in range(2)
    ]


def wanted_up(w):
    return [
        (j * LEAST, LEAST, lambda a, j=j: w.at[part(a, LEAST), j * 512 : (j + 1) * 512])
        for j in range(4)
    ]


def wanted_down(w):
    def place(a, rh, j):
        return w.at[pl.ds(pl.multiple_of(a * 512 + rh * 256, 256), 256), j * 512 : (j + 1) * 512]

    return [
        (
            (rh * 2 + j) * LEAST,
            LEAST,
            lambda a, rh=rh, j=j: place(a, rh, j),
        )
        for j in range(2)
        for rh in range(2)
    ]


def dot_nn(left, right):
    return lax.dot_general(left, right, (((1,), (0,)), ((), ())), preferred_element_type=F32)


def dot_nt(left, right):
    return lax.dot_general(left, right, (((1,), (1,)), ((), ())), preferred_element_type=F32)


def dot_tn(left, right):
    return lax.dot_general(left, right, (((0,), (0,)), ((), ())), preferred_element_type=F32)


def mean_last(values):
    return jnp.mean(values, axis=-1, keepdims=True)


def normalize(values):
    centred = values - mean_last(values)
    inverse = lax.rsqrt(mean_last(centred * centred) + EPSILON)
    return centred * inverse, inverse


def norm_back(grad_norm, normal, inverse):
    return inverse * (grad_norm - mean_last(grad_norm) - normal * mean_last(grad_norm * normal))


def column_sum(values):
    return jnp.sum(values.astype(F32), axis=0, keepdims=True)


def pack_kernel(
    core_ref, qkv, out, up, down, keep_a, send_a, keep_u, send_u, keep_d, send_d, sems
):
    core = core_ref[0]
    number = 0
    copies = []
    for target_a, target_u, target_d, half in (
        (send_a, send_u, send_d, 1 - core), (keep_a, keep_u, keep_d, core)
    ):
        for g in range(3):
            for f in range(4):
                columns = pl.ds(pl.multiple_of((g * 4 + f) * 256 + half * 128, 128), 128)
                copies.append(
                    (
                        qkv.at[0, :, columns],
                        target_a.at[g * LEAST : (g + 1) * LEAST, f * 128 : (f + 1) * 128],
                    )
                )
        for j in range(2):
            rows = pl.ds(pl.multiple_of(half * 128, 128), 128)
            copies.append(
                (
                    out.at[0, rows, j * 512 : (j + 1) * 512],
                    target_a.at[3 * LEAST + j * 128 : 3 * LEAST + (j + 1) * 128],
                )
            )
        for j in range(4):
            columns = pl.ds(pl.multiple_of(j * 1024 + half * 512, 512), 512)
            copies.append((up.at[0, :, columns], target_u.at[j * LEAST : (j + 1) * LEAST]))
        for rh in range(2):
            for j in range(2):
                rows = pl.ds(pl.multiple_of(half * 512 + rh * 256, 256), 256)
                at = (rh * 2 + j) * LEAST
                copies.append(
                    (down.at[0, rows, j * 512 : (j + 1) * 512], target_d.at[at : at + LEAST])
                )
    started = []
    for number, (source, target) in enumerate(copies):
        copy = pltpu.make_async_copy(source, target, sems.at[number])
        copy.start()
        started.append(copy)
    for copy in started:
        copy.wait()


def pack_weights(core, qkv, out, up, down):
    return call(
        pack_kernel,
        [kept(4 * LEAST, 512)] * 6,
        core, qkv, out, up, down,
        in_specs=[SCALARS] + [ANYWHERE] * 4,
        out_specs=[ANYWHERE] * 6,
        scratch_shapes=[pltpu.SemaphoreType.DMA((44,))],
        moved=12 << 20,
        limit=16,
        name="pack_weights",
    )


def qkv_kernel(
    me_ref, own_ref, other_ref, gain, bias, bq, bv, w0, w1, w2, w3, w4,
    a_ref, q_ref, k_ref, v_ref, w, sems,
):
    copies = fetches(me_ref[0], (w0, w1, w2, w3, w4), wanted_qkv(w), sems)
    start_all(copies)
    scale = BF16(1.0 / math.sqrt(D // HEADS))
    for m, x_ref in enumerate((own_ref, other_ref)):
        normed = (normalize(x_ref[...].astype(F32))[0] * gain[...] + bias[...]).astype(BF16)
        a_ref[m] = normed
        if m == 0:
            for group in copies:
                wait_group(group)
        q_ref[m] = (dot_nn(normed, w[0]) + bq[...]).astype(BF16) * scale
        k_ref[m] = dot_nn(normed, w[1]).astype(BF16)
        v_ref[m] = (dot_nn(normed, w[2]) + bv[...]).astype(BF16)


def make_qkv(me, own, other, gain, bias, bq, bv, pieces):
    rows = own.shape[0]
    half = D // 2
    return call(
        qkv_kernel,
        [kept(2, rows, D)] + [kept(2, rows, half)] * 3,
        me, own, other, gain, bias, bq, bv, *pieces,
        grid=(1,),
        in_specs=[SCALARS, fixed(rows, D), fixed(rows, D)]
        + [fixed(1, D), fixed(1, D), fixed(1, half), fixed(1, half)]
        + [ANYWHERE] * 5,
        out_specs=[fixed(2, rows, D)] + [fixed(2, rows, half)] * 3,
        scratch_shapes=[pltpu.VMEM((3, D, half), BF16), pltpu.SemaphoreType.DMA((3, 4))],
        flops=4 * rows * D * 3 * half,
        moved=14 << 20,
        name="project_qkv",
    )


def kv_kernel(me_ref, own_ref, other_ref, gain, bias, bv, w0, w1, w2, w3, w4, *rest):
    a_ref, k_ref, v_ref, w, sems = rest[-5:]
    copies = fetches(me_ref[0], (w0, w1, w2, w3, w4), wanted_qkv(w, (1, 2)), sems)
    start_all(copies)
    for m, x_ref in enumerate((own_ref, other_ref)):
        normed = (normalize(x_ref[...].astype(F32))[0] * gain[...] + bias[...]).astype(BF16)
        a_ref[m] = normed
        if m == 0:
            for group in copies:
                wait_group(group)
        k_ref[m] = dot_nn(normed, w[0]).astype(BF16)
        v_ref[m] = (dot_nn(normed, w[1]) + bv[...]).astype(BF16)


def make_kv(me, own, other, hops, at, earlier, gain, bias, bv, pieces):
    rows = own.shape[0]
    halo = hops * rows
    half = D // 2
    row = lambda width: pl.BlockSpec((2, rows, width), lambda i: (0, at, 0))
    first = 11
    return call(
        kv_kernel,
        [kept(2, halo, D), kept(2, halo, half), kept(2, halo, half)],
        me, own, other, gain, bias, bv, *pieces, *earlier,
        grid=(1,),
        in_specs=[SCALARS, fixed(rows, D), fixed(rows, D), fixed(1, D), fixed(1, D), fixed(1, half)]
        + [ANYWHERE] * 5
        + [ANYWHERE] * len(earlier),
        out_specs=[row(D), row(half), row(half)],
        input_output_aliases={first + i: i for i in range(len(earlier))},
        scratch_shapes=[pltpu.VMEM((2, D, half), BF16), pltpu.SemaphoreType.DMA((2, 4))],
        flops=2 * 2 * rows * D * 2 * half,
        moved=8 << 20,
        name="project_earlier",
    )


def out_kernel(me_ref, o_ref, w0, w1, w2, w3, w4, p_ref, w, sems):
    copies = fetches(me_ref[0], (w0, w1, w2, w3, w4), wanted_out(w), sems)
    start_all(copies)
    for group in copies:
        wait_group(group)
    p_ref[...] = dot_nn(o_ref[0], w[...]).astype(BF16)


def out_other(me, o, pieces):
    _, rows, half = o.shape
    return call(
        out_kernel,
        sds(rows, D),
        me, o, *pieces,
        grid=(1,),
        in_specs=[SCALARS, fixed(1, rows, half)] + [ANYWHERE] * 5,
        out_specs=fixed(rows, D),
        scratch_shapes=[pltpu.VMEM((half, D), BF16), pltpu.SemaphoreType.DMA((2, 4))],
        flops=2 * rows * half * D,
        moved=3 << 20,
        name="out_other",
    )


def middle_kernel(
    me_ref, o_ref, got, x_ref, bo, gain, bias, w0, w1, w2, w3, w4, x1_ref, h_ref, w, sems
):
    copies = fetches(me_ref[0], (w0, w1, w2, w3, w4), wanted_out(w), sems)
    start_all(copies)
    base = x_ref[...].astype(F32) + got[...].astype(F32) + bo[...]
    for group in copies:
        wait_group(group)
    x1 = base + dot_nn(o_ref[0], w[...])
    x1_ref[...] = x1
    h_ref[...] = (normalize(x1)[0] * gain[...] + bias[...]).astype(BF16)


def middle(me, o, got, x, bo, gain, bias, pieces):
    _, rows, half = o.shape
    return call(
        middle_kernel,
        [sds(rows, D, dtype=F32), sds(rows, D)],
        me, o, got, x, bo, gain, bias, *pieces,
        grid=(1,),
        in_specs=[SCALARS, fixed(1, rows, half)]
        + [fixed(rows, D)] * 2
        + [fixed(1, D)] * 3
        + [ANYWHERE] * 5,
        out_specs=[fixed(rows, D)] * 2,
        scratch_shapes=[pltpu.VMEM((half, D), BF16), pltpu.SemaphoreType.DMA((2, 4))],
        flops=2 * rows * half * D,
        moved=8 << 20,
        name="middle",
    )


def gelu_and_slope(u):
    c = math.sqrt(2.0 / math.pi)
    square = u * u
    half = 0.5 + 0.5 * jnp.tanh(u * (c + (c * 0.044715) * square))
    value = u * half
    slope = half + value * (1.0 - half) * (2.0 * c + (6.0 * c * 0.044715) * square)
    return value, slope


def up_kernel(me_ref, h_ref, bu, w0, w1, w2, w3, w4, act_ref, slope_ref, w, sems):
    copies = fetches(me_ref[0], (w0, w1, w2, w3, w4), wanted_up(w), sems)
    step = pl.program_id(0)

    @pl.when(step == 0)
    def _():
        start_all(copies)

    for j in range(4):

        @pl.when(step == j)
        def _(j=j):
            wait_group(copies[j])
            columns = slice(j * 512, (j + 1) * 512)
            rows = h_ref.shape[0]
            piece = min(256, rows)
            for r in range(0, rows, piece):
                u = dot_nn(h_ref[r : r + piece], w[:, columns]) + bu[:, columns]
                value, slope = gelu_and_slope(u)
                act_ref[r : r + piece] = value.astype(BF16)
                slope_ref[r : r + piece] = slope.astype(BF16)


def up(me, h, bu, pieces):
    rows = h.shape[0]
    half = FF // 2
    out = pl.BlockSpec((rows, 512), lambda j: (0, j))
    return call(
        up_kernel,
        [sds(rows, half), kept(rows, half)],
        me, h, bu, *pieces,
        grid=(4,),
        in_specs=[SCALARS, fixed(rows, D), fixed(1, half)] + [ANYWHERE] * 5,
        out_specs=[out, out],
        scratch_shapes=[pltpu.VMEM((D, half), BF16), pltpu.SemaphoreType.DMA((4, 4))],
        flops=2 * rows * half * D,
        moved=9 << 20,
        exps=rows * half,
        name="up",
    )


def down_kernel(me_ref, act, w0, w1, w2, w3, w4, p_ref, w, sems):
    copies = fetches(me_ref[0], (w0, w1, w2, w3, w4), wanted_down(w), sems)
    start_all(copies)
    for j in range(2):
        wait_group(copies[2 * j])
        wait_group(copies[2 * j + 1])
        columns = slice(j * 512, (j + 1) * 512)
        p_ref[:, columns] = dot_nn(act[...], w[:, columns]).astype(BF16)


def down_other(me, act, pieces):
    rows, half = act.shape
    return call(
        down_kernel,
        sds(rows, D),
        me, act, *pieces,
        grid=(1,),
        in_specs=[SCALARS, fixed(rows, half)] + [ANYWHERE] * 5,
        out_specs=fixed(rows, D),
        scratch_shapes=[pltpu.VMEM((half, D), BF16), pltpu.SemaphoreType.DMA((4, 4))],
        flops=2 * rows * half * D,
        moved=7 << 20,
        name="down_other",
    )


def last_kernel(me_ref, act, got, x1, bd, w0, w1, w2, w3, w4, y_ref, w, sems):
    copies = fetches(me_ref[0], (w0, w1, w2, w3, w4), wanted_down(w), sems)
    start_all(copies)
    for j in range(2):
        wait_group(copies[2 * j])
        wait_group(copies[2 * j + 1])
        columns = slice(j * 512, (j + 1) * 512)
        base = x1[:, columns] + got[:, columns].astype(F32) + bd[:, columns]
        y_ref[:, columns] = (base + dot_nn(act[...], w[:, columns])).astype(BF16)


def last(me, act, got, x1, bd, pieces):
    rows, half = act.shape
    return call(
        last_kernel,
        sds(rows, D),
        me, act, got, x1, bd, *pieces,
        grid=(1,),
        in_specs=[SCALARS, fixed(rows, half), fixed(rows, D), fixed(rows, D), fixed(1, D)]
        + [ANYWHERE] * 5,
        out_specs=fixed(rows, D),
        scratch_shapes=[pltpu.VMEM((half, D), BF16), pltpu.SemaphoreType.DMA((4, 4))],
        flops=2 * rows * half * D,
        moved=10 << 20,
        name="down_own",
    )


def lanes_of(rows, low):
    lane = lax.broadcasted_iota(jnp.int32, (rows, LANES), 1)
    return lane < LANES // 2 if low else lane >= LANES // 2


def split3(values):
    first = values.astype(BF16)
    rest = values - first.astype(F32)
    second = rest.astype(BF16)
    third = (rest - second.astype(F32)).astype(BF16)
    return first, second, third


def forward_kernel(
    rows, halo, block,
    word, q_ref, kh_ref, ko_ref, vh_ref, vo_ref, lo_ref, ek_ref, eq_ref, o_ref, e_ref,
):
    lane = lax.broadcasted_iota(jnp.int32, (block, LANES), 1)
    for q0 in range(0, rows, block):
        k0 = max(0, halo + q0 - WIN) // block * block
        k1 = halo + q0 + block
        q = q_ref[0, q0 : q0 + block, :]
        lo = lo_ref[0, q0 : q0 + block, :]
        outs = []
        for t in range(2):
            keep = lanes_of(block, t == 0)
            eq = jnp.broadcast_to(eq_ref[0, t : t + 1, :], (block, LANES))
            qcat = jnp.concatenate([q, eq.astype(BF16)], axis=1)
            tiles = []
            for kb in range(k0, k1, block):
                k = kh_ref[0, kb : kb + block, :] if kb < halo else ko_ref[0, kb - halo : kb - halo + block, :]
                kcat = jnp.concatenate(
                    [jnp.where(keep, k, jnp.zeros_like(k)), ek_ref[kb : kb + block, :]], axis=1
                )
                s = dot_nt(qcat, kcat)
                kidx = lax.broadcasted_iota(jnp.int32, (block, block), 1) + kb
                allowed = kidx >= lo
                if kb + block == k1:
                    qidx = lax.broadcasted_iota(jnp.int32, (block, block), 0) + (halo + q0)
                    allowed = allowed & (kidx <= qidx)
                tiles.append(jnp.where(allowed, s, MASKED))
            top = functools.reduce(jnp.maximum, tiles)
            m = jnp.max(top, axis=1, keepdims=True)
            product = None
            for kb, s in zip(range(k0, k1, block), tiles):
                if kb < halo:
                    v = vh_ref[0, kb : kb + block, :]
                else:
                    v = vo_ref[0, kb - halo : kb - halo + block, :]
                part = dot_nn(
                    jnp.exp(s - m).astype(BF16), jnp.concatenate([v, jnp.ones_like(v)], axis=1)
                )
                product = part if product is None else product + part
            total = product[:, LANES : LANES + 1]
            outs.append(product[:, :LANES] / total)
            first, second, third = split3(-(m + jnp.log(total)))
            e = jnp.where(lane == 6, first.astype(F32), eq)
            e = jnp.where(lane == 7, second.astype(F32), e)
            e = jnp.where(lane == 8, third.astype(F32), e)
            e_ref[0, t, q0 : q0 + block, :] = e.astype(BF16)
        o_ref[0, q0 : q0 + block, :] = jnp.where(lanes_of(block, True), outs[0], outs[1]).astype(
            BF16
        )


def attend(word, which, q, kh, ko, vh, vo, lo, ek, eq):
    _, rows, width = q.shape
    halo = kh.shape[1]
    pairs = width // LANES
    block = min(256, rows)
    spec = lambda n: pl.BlockSpec((1, n, LANES), lambda p: (which, 0, p))
    count = pairs * 2 * rows * (WIN + block)
    return call(
        functools.partial(forward_kernel, rows, halo, block),
        [sds(1, rows, width), kept(1, 2 * pairs, rows, LANES)],
        word, *streamed(q, kh, ko, vh, vo), lo, ek, eq,
        grid=(pairs,),
        in_specs=[
            SCALARS,
            spec(rows), spec(halo), spec(rows), spec(halo), spec(rows),
            pl.BlockSpec((1, rows, 1), lambda p: (which, 0, 0)),
            fixed(halo + rows, LANES),
            pl.BlockSpec((1, 2, LANES), lambda p: (p, 0, 0)),
        ],
        out_specs=[
            pl.BlockSpec((1, rows, LANES), lambda p: (0, 0, p)),
            pl.BlockSpec((1, 2, rows, LANES), lambda p: (0, p, 0, 0)),
        ],
        flops=count * 1024,
        moved=6 << 20,
        exps=count,
        name="attention_forward",
    )


def backward_kernel(
    rows, halo, block, begin, end, final,
    word, q_ref, kh_ref, ko_ref, vh_ref, vo_ref, o_ref, do_ref, e_ref, lo_ref, ek_ref, *refs,
):
    acc_ref = refs[-1]
    refs = list(refs[:-1])
    start_ref = refs.pop(0) if begin > 0 else None
    dq_ref = refs.pop(0)
    dkh_ref, dvh_ref = (refs.pop(0), refs.pop(0)) if begin == 0 else (None, None)
    dko_ref, dvo_ref = (refs.pop(0), refs.pop(0)) if final else (None, None)
    q = q_ref[0]
    do = do_ref[0]
    lo = lo_ref[0]
    lane = lax.broadcasted_iota(jnp.int32, (rows, LANES), 1)
    ones = jnp.where(lax.broadcasted_iota(jnp.int32, (block, LANES), 1) < 3, 1.0, 0.0).astype(BF16)
    product = do.astype(F32) * o_ref[0].astype(F32)
    qcats, docats, qts, dots = [], [], [], []
    for t in range(2):
        keep = lanes_of(rows, t == 0)
        delta = jnp.sum(jnp.where(keep, product, 0.0), axis=1, keepdims=True)
        first, second, third = split3(-delta)
        ed = jnp.where(lane == 0, first.astype(F32), 0.0)
        ed = jnp.where(lane == 1, second.astype(F32), ed)
        ed = jnp.where(lane == 2, third.astype(F32), ed)
        qcats.append(jnp.concatenate([q, e_ref[0, t]], axis=1))
        docats.append(jnp.concatenate([do, ed.astype(BF16)], axis=1))
        qts.append(jnp.where(keep, q, jnp.zeros_like(q)))
        dots.append(jnp.where(keep, do, jnp.zeros_like(do)))
    acc_ref[...] = jnp.zeros_like(acc_ref) if start_ref is None else start_ref[0]
    for kb in range(begin, end, block):
        if kb < halo:
            k_in, v_in, dk_out, dv_out, at = kh_ref, vh_ref, dkh_ref, dvh_ref, kb
        else:
            k_in, v_in, dk_out, dv_out, at = ko_ref, vo_ref, dko_ref, dvo_ref, kb - halo
        qlo = max(0, kb - halo)
        qhi = min(rows, -(-(kb + block - 1 + WIN - halo) // block) * block)
        if qhi <= qlo:
            dk_out[0, at : at + block, :] = jnp.zeros((block, LANES), BF16)
            dv_out[0, at : at + block, :] = jnp.zeros((block, LANES), BF16)
            continue
        k = k_in[0, at : at + block, :]
        v = v_in[0, at : at + block, :]
        ek = ek_ref[kb : kb + block, :]
        kidx = lax.broadcasted_iota(jnp.int32, (block, qhi - qlo), 0) + kb
        allowed = kidx >= lo[:, qlo:qhi]
        if kb + block > halo + qlo:
            qidx = lax.broadcasted_iota(jnp.int32, (block, qhi - qlo), 1) + (halo + qlo)
            allowed = allowed & (kidx <= qidx)
        pts, dss, kts = [], [], []
        for t in range(2):
            keep = lanes_of(block, t == 0)
            kt = jnp.where(keep, k, jnp.zeros_like(k))
            vt = jnp.where(keep, v, jnp.zeros_like(v))
            st = dot_nt(jnp.concatenate([kt, ek], axis=1), qcats[t][qlo:qhi])
            pt = jnp.exp(jnp.where(allowed, st, MASKED))
            dpt = dot_nt(jnp.concatenate([vt, ones], axis=1), docats[t][qlo:qhi])
            pts.append(pt.astype(BF16))
            dss.append((pt * dpt).astype(BF16))
            kts.append(kt)
        dv = dot_nn(jnp.concatenate(pts, axis=1), jnp.concatenate([d[qlo:qhi] for d in dots], axis=0))
        dk = dot_nn(jnp.concatenate(dss, axis=1), jnp.concatenate([d[qlo:qhi] for d in qts], axis=0))
        dv_out[0, at : at + block, :] = dv.astype(BF16)
        dk_out[0, at : at + block, :] = dk.astype(BF16)
        acc_ref[:, qlo:qhi] += dot_tn(jnp.concatenate(kts, axis=0), jnp.concatenate(dss, axis=0))
    if final:
        scale = 1.0 / math.sqrt(LANES // 2)
        dq_ref[0] = (acc_ref[...].T * scale).astype(BF16)
    else:
        dq_ref[0] = acc_ref[...]


def attend_back(word, which, q, kh, ko, vh, vo, o, do, e, lo, ek, start=None):
    _, rows, width = q.shape
    halo = kh.shape[1]
    pairs = width // LANES
    block = min(256, rows)
    begin, end, final = (0, halo, False) if start is None else (halo, halo + rows, True)
    spec = lambda n: pl.BlockSpec((1, n, LANES), lambda p: (which, 0, p))
    only = lambda n: pl.BlockSpec((1, n, LANES), lambda p: (0, 0, p))
    sums = pl.BlockSpec((1, LANES, rows), lambda p: (0, p, 0))
    count = pairs * 2 * rows * (WIN + block) * (end - begin) // (halo + rows)
    if final:
        shapes, specs = [sds(1, rows, width)] * 3, [only(rows)] * 3
    else:
        shapes = [sds(1, width, rows, dtype=F32)] + [sds(1, halo, width)] * 2
        specs = [sums, only(halo), only(halo)]
    return call(
        functools.partial(backward_kernel, rows, halo, block, begin, end, final),
        shapes,
        word, *streamed(q, kh, ko, vh, vo), o, do, *streamed(e), lo, ek,
        *([] if start is None else [start]),
        grid=(pairs,),
        in_specs=[
            SCALARS,
            spec(rows), spec(halo), spec(rows), spec(halo), spec(rows), only(rows), spec(rows),
            pl.BlockSpec((1, 2, rows, LANES), lambda p: (0, p, 0, 0)),
            pl.BlockSpec((1, 1, rows), lambda p: (which, 0, 0)),
            fixed(halo + rows, LANES),
        ]
        + ([] if start is None else [sums]),
        out_specs=specs,
        scratch_shapes=[pltpu.VMEM((LANES, rows), F32)],
        flops=count * 2304,
        moved=8 << 20,
        exps=count,
        name="attention_backward",
    )


def act_back_kernel(
    me_ref, own, other, slope_own, slope_other, w0, w1, w2, w3, w4,
    du_own, du_other, sums, w, sems,
):
    copies = fetches(me_ref[0], (w0, w1, w2, w3, w4), wanted_down(w), sems)
    step = pl.program_id(0)

    @pl.when(step == 0)
    def _():
        start_all(copies)
        for group in copies:
            wait_group(group)

    rows = own.shape[0]
    piece = min(256, rows)
    w_part = w[pl.ds(pl.multiple_of(step * 512, 512), 512), :]
    total = jnp.zeros((1, 512), F32)
    for dy, slope, du in ((other, slope_other, du_other), (own, slope_own, du_own)):
        for r in range(0, rows, piece):
            grad = dot_nt(dy[r : r + piece], w_part) * slope[r : r + piece].astype(F32)
            rounded = grad.astype(BF16)
            du[r : r + piece] = rounded
            total += column_sum(rounded)
    sums[...] = jnp.broadcast_to(total, (8, 512))


def act_back(me, own, other, slope_own, slope_other, pieces):
    rows = own.shape[0]
    half = FF // 2
    columns = pl.BlockSpec((rows, 512), lambda j: (0, j))
    return call(
        act_back_kernel,
        [sds(rows, half), sds(rows, half), sds(8, half, dtype=F32)],
        me, own, other, *streamed(slope_own, slope_other), *pieces,
        grid=(4,),
        in_specs=[SCALARS, fixed(rows, D), fixed(rows, D), columns, columns] + [ANYWHERE] * 5,
        out_specs=[columns, columns, pl.BlockSpec((8, 512), lambda j: (0, j))],
        scratch_shapes=[pltpu.VMEM((half, D), BF16), pltpu.SemaphoreType.DMA((4, 4))],
        flops=4 * rows * half * D,
        moved=16 << 20,
        name="act_back",
    )


def up_back_kernel(me_ref, du, w0, w1, w2, w3, w4, p_ref, w, sems):
    copies = fetches(me_ref[0], (w0, w1, w2, w3, w4), wanted_up(w), sems)
    start_all(copies)
    for group in copies:
        wait_group(group)
    p_ref[...] = dot_nt(du[...], w[...]).astype(BF16)


def up_back_other(me, du, pieces):
    rows, half = du.shape
    return call(
        up_back_kernel,
        sds(rows, D),
        me, du, *pieces,
        grid=(1,),
        in_specs=[SCALARS, fixed(rows, half)] + [ANYWHERE] * 5,
        out_specs=fixed(rows, D),
        scratch_shapes=[pltpu.VMEM((D, half), BF16), pltpu.SemaphoreType.DMA((4, 4))],
        flops=2 * rows * half * D,
        moved=7 << 20,
        name="up_back_other",
    )


def middle_back_kernel(
    me_ref, du, got, x1, dy, gain, w0, w1, w2, w3, w4, dx1_ref, db_ref, sums, w, sems
):
    copies = fetches(me_ref[0], (w0, w1, w2, w3, w4), wanted_up(w), sems)
    start_all(copies)
    normal, inverse = normalize(x1[...])
    for group in copies:
        wait_group(group)
    dh = dot_nt(du[...], w[...]) + got[...].astype(F32)
    top = dy[...].astype(F32)
    dx1 = top + norm_back(dh * gain[...], normal, inverse)
    dx1_ref[...] = dx1
    db = dx1.astype(BF16)
    db_ref[...] = db
    sums[0:1] = column_sum(dh * normal)
    sums[1:2] = column_sum(dh)
    sums[2:3] = column_sum(db)
    sums[3:4] = column_sum(top)
    sums[4:8] = jnp.zeros((4, D), F32)


def middle_back(me, du, got, x1, dy, gain, pieces):
    rows, half = du.shape
    return call(
        middle_back_kernel,
        [sds(rows, D, dtype=F32), sds(rows, D), sds(8, D, dtype=F32)],
        me, du, got, x1, dy, gain, *pieces,
        grid=(1,),
        in_specs=[SCALARS, fixed(rows, half)]
        + [fixed(rows, D)] * 3
        + [fixed(1, D)]
        + [ANYWHERE] * 5,
        out_specs=[fixed(rows, D), fixed(rows, D), fixed(8, D)],
        scratch_shapes=[pltpu.VMEM((D, half), BF16), pltpu.SemaphoreType.DMA((4, 4))],
        flops=2 * rows * half * D,
        moved=14 << 20,
        name="middle_back",
    )


def out_back_kernel(me_ref, own, other, w0, w1, w2, w3, w4, do_ref, w, sems):
    copies = fetches(me_ref[0], (w0, w1, w2, w3, w4), wanted_out(w), sems)
    start_all(copies)
    for group in copies:
        wait_group(group)
    do_ref[0] = dot_nt(own[...], w[...]).astype(BF16)
    do_ref[1] = dot_nt(other[...], w[...]).astype(BF16)


def out_back(me, own, other, pieces):
    rows = own.shape[0]
    half = D // 2
    return call(
        out_back_kernel,
        sds(2, rows, half),
        me, own, other, *pieces,
        grid=(1,),
        in_specs=[SCALARS, fixed(rows, D), fixed(rows, D)] + [ANYWHERE] * 5,
        out_specs=fixed(2, rows, half),
        scratch_shapes=[pltpu.VMEM((half, D), BF16), pltpu.SemaphoreType.DMA((2, 4))],
        flops=4 * rows * half * D,
        moved=4 << 20,
        name="out_back",
    )


def store_parts(step, parts_x, parts_y, send_x, send_y, keep_x, keep_y):
    def put(ref, pieces):
        row = 0
        for piece in pieces:
            ref[0, row : row + piece.shape[0]] = piece
            row += piece.shape[0]

    @pl.when(step < 2)
    def _():
        put(send_x, parts_x)

    @pl.when(step >= 2)
    def _():
        put(keep_x, parts_x)

    @pl.when(step % 2 == 0)
    def _():
        put(send_y, parts_y)

    @pl.when(step % 2 == 1)
    def _():
        put(keep_y, parts_y)


def part_outputs(rows):
    shapes = [kept(2, rows, 512)] * 4
    specs = [
        pl.BlockSpec((1, rows, 512), lambda i, order: (jnp.minimum(i, 1), 0, 0)),
        pl.BlockSpec((1, rows, 512), lambda i, order: (i // 2, 0, 0)),
        pl.BlockSpec((1, rows, 512), lambda i, order: (i // 3, 0, 0)),
        pl.BlockSpec((1, rows, 512), lambda i, order: (i // 3, 0, 0)),
    ]
    return shapes, specs


def down_grad_kernel(order, act_own, act_other, own, other, *outs):
    grad = (dot_tn(act_own[...], own[...]) + dot_tn(act_other[...], other[...])).astype(BF16)
    store_parts(
        pl.program_id(0),
        [grad[:256, :512], grad[:256, 512:]],
        [grad[256:, :512], grad[256:, 512:]],
        *outs,
    )


def down_grad(order, act_own, act_other, own, other):
    rows = own.shape[0]
    shapes, specs = part_outputs(512)
    columns = pl.BlockSpec((rows, 512), lambda i, order: (0, order[i]))
    full = pl.BlockSpec((rows, D), lambda i, order: (0, 0))
    return call(
        down_grad_kernel,
        shapes,
        order, *streamed(act_own, act_other), own, other,
        grid_spec=pltpu.PrefetchScalarGridSpec(
            num_scalar_prefetch=1,
            grid=(4,),
            in_specs=[columns, columns, full, full],
            out_specs=specs,
        ),
        flops=4 * rows * (FF // 2) * D,
        moved=10 << 20,
        name="down_grad",
    )


def up_grad_kernel(
    order, h_own, h_other, du_own, du_other, o_own, o_other, db_own, db_other, *outs
):
    grad = (dot_tn(h_own[...], du_own[...]) + dot_tn(h_other[...], du_other[...])).astype(BF16)
    out_part = (dot_tn(o_own[0], db_own[...]) + dot_tn(o_other[0], db_other[...])).astype(BF16)
    store_parts(
        pl.program_id(0),
        [grad[:, :512], grad[:, 512:1024], out_part[:, :512]],
        [grad[:, 1024:1536], grad[:, 1536:], out_part[:, 512:]],
        *outs,
    )


def up_grad(order, h_own, h_other, du_own, du_other, o_own, o_other, db_own, db_other):
    rows = h_own.shape[0]
    half = FF // 2
    shapes, specs = part_outputs(640)
    columns = pl.BlockSpec((rows, 256), lambda i, order: (0, order[i]))
    full = lambda width: pl.BlockSpec((rows, width), lambda i, order: (0, 0))
    heads = pl.BlockSpec((1, rows, 128), lambda i, order: (0, 0, order[i]))
    return call(
        up_grad_kernel,
        shapes,
        order, h_own, h_other, du_own, du_other, o_own, o_other, db_own, db_other,
        grid_spec=pltpu.PrefetchScalarGridSpec(
            num_scalar_prefetch=1,
            grid=(4,),
            in_specs=[columns, columns, full(half), full(half), heads, heads, full(D), full(D)],
            out_specs=specs,
        ),
        flops=4 * rows * half * D + 2 * rows * D * D,
        moved=14 << 20,
        name="up_grad",
    )


def qkv_grad_kernel(order, a_own, a_halo, *refs):
    dq, dko, dvo, dkh, dvh = (refs[2 * i : 2 * i + 2] for i in range(5))
    *parts, sums = refs[10:]

    def total(pairs):
        return sum(dot_tn(left[m], right[m][0]) for left, right in pairs for m in range(2)).astype(BF16)

    k_part = total([(a_own, dko), (a_halo, dkh)])
    first = [total([(a_own, dq)]), k_part[:128]]
    second = [k_part[128:], total([(a_own, dvo), (a_halo, dvh)])]
    store_parts(pl.program_id(0), first, second, *parts)

    @pl.when(pl.program_id(0) == 0)
    def _():
        sums[0:1] = column_sum(dq[0][0]) + column_sum(dq[1][0])
        sums[1:2] = sum(column_sum(ref[0]) for ref in (*dvo, *dvh))
        sums[2:8] = jnp.zeros((6, sums.shape[1]), F32)


def qkv_grad(order, a_own, a_halo, *grads):
    rows, halo = a_own.shape[1], a_halo.shape[1]
    half = D // 2
    shapes, specs = part_outputs(384)
    full = lambda n: pl.BlockSpec((1, n, half), lambda i, order: (0, 0, 0))
    columns = lambda n: pl.BlockSpec((2, n, 256), lambda i, order: (0, 0, order[i]))
    return call(
        qkv_grad_kernel,
        shapes + [sds(8, half, dtype=F32)],
        order, a_own, a_halo, *[ref for pair in grads for ref in pair],
        grid_spec=pltpu.PrefetchScalarGridSpec(
            num_scalar_prefetch=1,
            grid=(4,),
            in_specs=[columns(rows), columns(halo)]
            + [full(rows)] * 6
            + [full(halo)] * 4,
            out_specs=specs + [pl.BlockSpec((8, half), lambda i, order: (0, 0))],
        ),
        flops=4 * D * half * (3 * rows + 2 * halo),
        moved=16 << 20,
        name="qkv_grad",
    )


def normed_back_kernel(hops, me_ref, *refs):
    wanted = (1, 2) if hops else (0, 1, 2)
    count = len(wanted)
    grads, a_ref, refs = refs[:count], refs[count], refs[count + 1 :]
    *outs, sums, w, sems = refs[5:]
    got = outs.pop(0) if len(outs) > max(hops, 1) else None
    copies = fetches(me_ref[0], refs[:5], wanted_qkv(w, wanted), sems)
    start_all(copies)
    for group in copies:
        wait_group(group)
    weighted = jnp.zeros((1, D), F32)
    plain = jnp.zeros((1, D), F32)
    rows = outs[0].shape[0] if got is not None else a_ref.shape[1] // max(hops, 1)
    for number in range(max(hops, 1)):
        r = slice(number * rows, (number + 1) * rows)
        da = sum(dot_nt(grad[0, r], w[i]) for i, grad in enumerate(grads))
        weighted += column_sum(da * a_ref[0, r].astype(F32))
        plain += column_sum(da)
        if got is None:
            outs[0][r] = da.astype(BF16)
        else:
            da = da + got[r].astype(F32)
            outs[number][...] = da.astype(outs[number].dtype)
    sums[0:1] = weighted
    sums[1:2] = plain
    sums[2:8] = jnp.zeros((6, D), F32)


def normed_back(me, which, hops, grads, a, pieces, got=None):
    length = a.shape[1]
    rows = length // max(hops, 1)
    half = D // 2
    count = len(grads)
    if got is None:
        outs, out_specs = [sds(length, D)], [fixed(length, D)]
    elif hops:
        outs, out_specs = [sds(rows, D)] * hops, [fixed(rows, D)] * hops
    else:
        outs, out_specs = [sds(rows, D, dtype=F32)], [fixed(rows, D)]
    return call(
        functools.partial(normed_back_kernel, hops),
        outs + [sds(8, D, dtype=F32)],
        me, *grads, a, *pieces, *([] if got is None else [got]),
        grid=(1,),
        in_specs=[SCALARS]
        + [fixed(1, length, half)] * count
        + [pl.BlockSpec((1, length, D), lambda i: (which, 0, 0))]
        + [ANYWHERE] * 5
        + ([] if got is None else [fixed(length, D)]),
        out_specs=out_specs + [fixed(8, D)],
        scratch_shapes=[pltpu.VMEM((count, D, half), BF16), pltpu.SemaphoreType.DMA((count, 4))],
        flops=2 * count * length * half * D,
        moved=8 << 20,
        name="normed_back",
    )


def first_back_kernel(word, da_ref, got, x_ref, dx1, gain, dx_ref, low_ref):
    da = da_ref[...] + got[...].astype(F32)
    normal, inverse = normalize(x_ref[...].astype(F32))
    dx = dx1[...] + norm_back(da * gain[...], normal, inverse)
    dx_ref[...] = dx
    low_ref[...] = dx.astype(BF16)


def first_back(word, da, got, x, dx1, gain):
    rows = da.shape[0]
    return call(
        first_back_kernel,
        [sds(rows, D, dtype=F32), sds(rows, D)],
        word, da, got, x, dx1, gain,
        grid=(1,),
        in_specs=[SCALARS] + [fixed(rows, D)] * 4 + [fixed(1, D)],
        out_specs=[fixed(rows, D), fixed(rows, D)],
        moved=10 << 20,
        name="first_back",
    )


def unpack_down_kernel(core_ref, kept, got, out):
    core = core_ref[0]
    for half, source in ((core, kept), (1 - core, got)):
        for rh in range(2):
            for j in range(2):
                at = (rh * 2 + j) * 256
                rows = pl.ds(pl.multiple_of(half * 512 + rh * 256, 256), 256)
                out[0, rows, j * 512 : (j + 1) * 512] = source[at : at + 256].astype(F32)


def unpack_up_kernel(core_ref, kept_part, got, out_up, out_out):
    core = core_ref[0]
    for half, source in ((core, kept_part), (1 - core, got)):
        for j in range(4):
            at = (j // 2) * 640 + (j % 2) * 256
            columns = pl.ds(pl.multiple_of(j * 1024 + half * 512, 512), 512)
            out_up[0, :, columns] = source[at : at + 256].astype(F32)
        rows = pl.ds(pl.multiple_of(half * 128, 128), 128)
        for j in range(2):
            at = j * 640 + 512
            out_out[0, rows, j * 512 : (j + 1) * 512] = source[at : at + 128].astype(F32)


def unpack_qkv_kernel(core_ref, kept_part, got, out):
    core = core_ref[0]
    for half, source in ((core, kept_part), (1 - core, got)):
        for g in range(3):
            for f in range(4):
                columns = pl.ds(pl.multiple_of((g * 4 + f) * 256 + half * 128, 128), 128)
                out[0, :, columns] = source[
                    g * 256 : (g + 1) * 256, f * 128 : (f + 1) * 128
                ].astype(F32)


def unpack(kernel, core, pieces, shapes, name):
    return call(
        kernel,
        shapes,
        core, *pieces,
        in_specs=[SCALARS] + [INSIDE] * len(pieces),
        out_specs=jax.tree.map(lambda _: INSIDE, shapes),
        moved=10 << 20,
        name=name,
    )


def split_vector(values):
    pieces, offset = [], 0
    for length in (D, D, D, D, D, D, D, FF, D):
        pieces.append(values[offset : offset + length])
        offset += length
    return pieces


def shards(inputs, cotangent, segments, w_qkv, w_out, w_up, w_down, vectors):
    core = lax.axis_index("section")
    column = lax.axis_index("ctx")
    fs = lax.axis_index("fsdp")
    nf = lax.axis_size("fsdp")
    rows = inputs.shape[2]
    reach = (WIN - 1) // rows + 1
    halo = reach * rows
    first_core = core == 0
    me = fs.astype(jnp.int32).reshape(1)
    core_word = core.astype(jnp.int32).reshape(1)
    order = jnp.stack([fs ^ r for r in ROLL]).astype(jnp.int32)

    def pick(here, there):
        return jnp.where(first_core, here, there), jnp.where(first_core, there, here)

    mine = lambda values: lax.dynamic_index_in_dim(values, core, 0, keepdims=False)
    theirs = lambda values: lax.dynamic_index_in_dim(values, 1 - core, 0, keepdims=False)
    x_own, x_other = mine(inputs[:, 0]), theirs(inputs[:, 0])
    keep_a, send_a, keep_u, send_u, keep_d, send_d = pack_weights(
        tie(core_word, x_own), w_qkv, w_out, w_up, w_down
    )
    shard_a = pick(keep_a, swap(send_a))
    later = lambda value: tie(value, shard_a[0])

    shard_u = pick(keep_u, swap(later(send_u)))
    shard_d = pick(keep_d, swap(later(send_d)))
    both = tie(jnp.concatenate(pick(vectors, swap(vectors))), shard_u, shard_d)
    near = flip(both, "fsdp", 1)
    low_x = (fs & 1) == 0
    pair = jnp.concatenate([jnp.where(low_x, both, near), jnp.where(low_x, near, both)], 1)
    far = flip(pair, "fsdp", 2)
    low_y = (fs & 2) == 0
    packed = jnp.concatenate([jnp.where(low_y, pair, far), jnp.where(low_y, far, pair)], 1)
    packed = packed.astype(F32)

    a0 = Gather(shard_a[0])
    u0 = Gather(shard_u[0], a0.far)
    d0 = Gather(shard_d[0], a0.far)
    a1 = Gather(shard_a[1], d0.near)
    u1 = Gather(shard_u[1], a1.far)
    d1 = Gather(shard_d[1], a1.far)
    weights = ((a0, u0, d0), (a1, u1, d1))

    top = later(cotangent[:, 0])
    top_own, top_other = mine(top), theirs(top)
    marks = later(segments[:, 0])
    starts = jnp.stack([mine(marks), theirs(marks)])
    position = column * rows + jnp.arange(rows, dtype=jnp.int32)
    lo = jnp.maximum(starts, position[None] - (WIN - 1)) - (column * rows - halo)
    lo_column, lo = lo[:, :, None], lo[:, None, :]

    nought = later(jnp.zeros((), jnp.int32))
    key_index = lax.broadcasted_iota(jnp.int32, (halo + rows, LANES), 0) + nought
    lane = lax.broadcasted_iota(jnp.int32, (halo + rows, LANES), 1)
    placed = jnp.where(lane % 2 == 0, key_index // 256 * 256, key_index % 256)
    ek = jnp.where(lane < 6, placed, jnp.where(lane < 9, 1, 0)).astype(BF16)
    local_heads = HEADS // 2
    per_group = local_heads // nf
    local = jnp.arange(local_heads) + nought
    head = (local // per_group) * (2 * per_group) + core * per_group + local % per_group
    slopes = jnp.exp2(-0.5 * (head.astype(F32) + 1.0)) * (4.0 / WIN)
    first, second, third = [values.astype(F32) for values in split3(slopes)]
    eq = jnp.concatenate(
        [
            jnp.stack([first, first, second, second, third, third], 1),
            jnp.zeros((local_heads, LANES - 6), F32),
        ],
        1,
    ).reshape(local_heads // 2, 2, LANES)

    def start_halo(own, *after):
        pieces, block = [], own
        for hop in range(reach):
            block = step_along(tie(block, *after) if hop == 1 else block, "ctx", 1)
            pieces.append(block)
        return pieces

    def finish_return(first, hops, *after):
        carried, sent = first, first
        for hop, piece in enumerate(hops[1:]):
            sent = add_bf16(piece, tie(carried, *after) if hop == 0 else carried)
            carried = step_along(sent, "ctx", -1)
        return carried, sent

    def my_half(values, groups):
        view = values.reshape(groups, 2, -1)
        return jnp.where(first_core, view[:, 0], view[:, 1]).reshape(1, -1)

    def widen(values, groups):
        view = values.reshape(groups, 1, -1)
        zero = jnp.zeros_like(view)
        return jnp.where(
            first_core, jnp.concatenate([view, zero], 1), jnp.concatenate([zero, view], 1)
        ).reshape(-1)

    line = Line()
    run = line.run

    def forward(layer, x_own, x_other, first_hops):
        g1, b1, bq, bv, bo, g2, b2, bu, bd = [
            values.reshape(1, -1) for values in split_vector(packed[layer])
        ]
        bq, bv, bu = my_half(bq, nf), my_half(bv, nf), my_half(bu, nf)
        ga, gu, gd = weights[layer]
        wa, wu, wd = ga.pieces, gu.pieces, gd.pieces
        a_own, q, ko, vo = run(
            make_qkv, me, x_own, x_other, g1, b1, bq, bv, wa,
            after=(ek, eq, lo, lo_column, bu, first_hops if layer == 0 else ()),
        )
        earlier = ()
        for hop, block in enumerate(first_hops):
            block = tie(block, line.token if hop == 0 else ())
            earlier = run(
                make_kv, me, block, swap(block), reach, reach - 1 - hop, earlier, g1, b1, bv, wa,
                after=first_hops if hop == 0 else (),
            )
        a_halo, kh, vh = earlier
        o_other, e_other = run(
            attend, me, 1, q, kh, ko, vh, vo, lo_column, ek, eq, after=(gu.near,)
        )
        part = run(out_other, me, o_other, wa)
        o_own, e_own = run(
            attend, me, 0, q, kh, ko, vh, vo, lo_column, ek, eq, after=(gd.near,)
        )
        x1, h_own = run(
            middle, me, o_own, swap(part), x_own, bo, g2, b2, wa, after=(gu.far,)
        )
        o, e = (o_own, o_other), (e_own, e_other)
        h_other = swap(h_own)
        act_own, slope_own = run(up, me, h_own, bu, wu)
        act_other, slope_other = run(up, me, h_other, bu, wu)
        part = run(down_other, me, act_other, wd)
        y = run(last, me, act_own, swap(part), x1, bd, wd)
        stored = (
            x_own, a_own, a_halo, q, kh, ko, vh, vo, o, e, x1, h_own, h_other,
            act_own, slope_own, act_other, slope_other, g1, b1, g2,
        )
        return y, stored

    y0, stored0 = forward(0, x_own, x_other, start_halo(x_own, shard_a[0]))
    y0_other = swap(y0)
    y1, stored1 = forward(1, y0, y0_other, start_halo(y0, a1.near))
    y1_other = swap(y1)

    column_sums = Column()

    def step(block, *after):
        column_sums.step(block, line.token, *after)
        line.also += column_sums.sent

    def backward(layer, top_own, top_other, stored, before=()):
        last_layer = layer == 0
        (
            x_own, a_own, a_halo, q, kh, ko, vh, vo, o, e, x1, h_own, h_other,
            act_own, slope_own, act_other, slope_other, g1, b1, g2,
        ) = stored
        wa, wu, wd = (group.pieces for group in weights[layer])
        du_own, du_other, sums_up = run(
            act_back, me, top_own, top_other, slope_own, slope_other, wd
        )
        got = swap(run(up_back_other, me, du_other, wu))
        down_part = Scatter(*run(down_grad, order, act_own, act_other, top_own, top_other))
        if last_layer:
            before[1].third(line.token)
        dx1, db_own, sums_middle = run(middle_back, me, du_own, got, x1, top_own, g2, wu)
        db_other = swap(db_own)
        do = run(out_back, me, db_own, db_other, wa)
        up_part = Scatter(
            *run(up_grad, order, h_own, h_other, du_own, du_other, *o, db_own, db_other)
        )
        if last_layer:
            step(before[0].piece)

        def early(m):
            return run(attend_back, me, m, q, kh, ko, vh, vo, o[m], do, e[m], lo, ek)

        def own(m, start):
            return run(attend_back, me, m, q, kh, ko, vh, vo, o[m], do, e[m], lo, ek, start)

        begun_other, dkh_other, dvh_other = early(1)
        down_part.second(line.token)
        line.also += (down_part.half,)
        if last_layer:
            step(before[1].piece)
        part, sums_a = run(normed_back, me, 1, reach, (dkh_other, dvh_other), a_halo, wa)
        got = swap(part)
        begun_own, dkh_own, dvh_own = early(0)
        down_part.third(line.token)
        line.also = (down_part.piece,)
        *hops, sums_b = run(normed_back, me, 0, reach, (dkh_own, dvh_own), a_halo, wa, got)
        first = step_along(hops[0], "ctx", -1)
        carried = sent = first
        if last_layer:
            step(down_part.piece, hops)
        else:
            carried, sent = finish_return(first, hops)
        dq_other, dko_other, dvo_other = own(1, begun_other)
        part, sums_c = run(normed_back, me, 1, 0, (dq_other, dko_other, dvo_other), a_own, wa)
        got = swap(part)
        up_part.second(line.token)
        line.also += (up_part.half,)
        dq_own, dko_own, dvo_own = own(0, begun_own)
        *parts, sums_qkv = run(
            qkv_grad, order, a_own, a_halo, (dq_own, dq_other), (dko_own, dko_other),
            (dvo_own, dvo_other), (dkh_own, dkh_other), (dvh_own, dvh_other),
            after=(column_sums.outer_got, column_sums.inner_got) if last_layer else (sent,),
        )
        qkv_part = Scatter(*parts)
        up_part.third(line.token)
        line.also = (up_part.piece,)
        if last_layer:
            step(up_part.piece)
        da, sums_d = run(
            normed_back, me, 0, 0, (dq_own, dko_own, dvo_own), a_own, wa, got,
            after=() if last_layer else (carried,),
        )
        qkv_part.second(line.token)
        line.also += (qkv_part.half,)
        if last_layer:
            carried, sent = finish_return(first, hops, line.token)
            line.also += (sent,)
            qkv_part.third()
            step(qkv_part.piece)
        dx, dx_low = run(first_back, me, da, carried, x_own, dx1, g1)
        if not last_layer:
            step(down_part.piece)
        plain = sums_a[1] + sums_b[1] + sums_c[1] + sums_d[1]
        weighted = sums_a[0] + sums_b[0] + sums_c[0] + sums_d[0]
        vector = jnp.concatenate(
            [
                (weighted - b1[0] * plain) / g1[0], plain, widen(sums_qkv[0], nf),
                widen(sums_qkv[1], nf), sums_middle[2], sums_middle[0], sums_middle[1],
                widen(sums_up[0], nf), sums_middle[3],
            ]
        )
        return dx, dx_low, (up_part, qkv_part), vector

    _, dx1, parts1, vector1 = backward(1, top_own, top_other, stored1)
    dx1_other = swap(dx1)
    dx0, _, _, vector0 = backward(0, dx1, dx1_other, stored0, parts1)
    dx0_other = swap(dx0)
    stages = sums_over_all(jnp.stack([vector0, vector1]))
    step(None, stages[2])
    def by_micro(own, other):
        return jnp.where(first_core, jnp.stack([own, other]), jnp.stack([other, own]))

    activations = jnp.where(first_core, by_micro(y0, y0_other), by_micro(y1, y1_other))
    input_grad = jnp.where(
        first_core, by_micro(dx0, dx0_other), by_micro(dx1, dx1_other).astype(F32)
    )

    def exchange(first, second):
        kept, sent = pick(first, second)
        return kept, swap(sent)

    waiting = column_sums.outer_got, column_sums.inner_got
    waiting, activations, input_grad = lax.optimization_barrier((waiting, activations, input_grad))
    column_sums.outer_got, column_sums.inner_got = waiting
    step(None, stages[4])
    size = D // nf
    down1_sum, up1_sum, qkv1_sum, down0_sum, up0_sum, *_ = column_sums.sums
    grad_down = unpack(
        unpack_down_kernel, core_word, exchange(down0_sum, down1_sum),
        sds(1, FF // nf, D, dtype=F32), "unpack_down",
    )
    grad_up, grad_out = unpack(
        unpack_up_kernel, core_word, exchange(up0_sum, up1_sum),
        [sds(1, size, FF, dtype=F32), sds(1, size, D, dtype=F32)], "unpack_up",
    )
    waiting = column_sums.outer_got
    waiting, grad_down, grad_up, grad_out = lax.optimization_barrier(
        (waiting, grad_down, grad_up, grad_out)
    )
    column_sums.outer_got = waiting
    step(None, stages[-1])
    qkv0_sum = column_sums.sums[-1]
    grad_qkv = unpack(
        unpack_qkv_kernel, core_word, exchange(qkv0_sum, qkv1_sum),
        sds(1, size, 3 * D, dtype=F32), "unpack_qkv",
    )
    summed = stages[-1]
    length = summed.shape[1] // nf
    grad_vectors = lax.dynamic_slice(summed, (core, fs * length), (1, length))
    return (
        activations[None, :, None], input_grad[None, :, None],
        grad_qkv, grad_out, grad_up, grad_down, grad_vectors,
    )


def solution(mesh):
    placed = (
        P(None, "fsdp", "ctx", None),
        P(None, "fsdp", "ctx", None),
        P(None, "fsdp", "ctx"),
        P("section", "fsdp", None),
        P("section", "fsdp", None),
        P("section", "fsdp", None),
        P("section", "fsdp", None),
        P("section", "fsdp"),
    )
    return jax.shard_map(
        shards,
        mesh=mesh,
        in_specs=placed,
        out_specs=(
            P("section", None, "fsdp", "ctx", None),
            P("section", None, "fsdp", "ctx", None),
            P("section", "fsdp", None),
            P("section", "fsdp", None),
            P("section", "fsdp", None),
            P("section", "fsdp", None),
            P("section", "fsdp"),
        ),
        check_vma=False,
    )
```

```python
import functools
import math

import jax
import jax.numpy as jnp
from jax import lax
from jax.experimental import pallas as pl
from jax.experimental.pallas import tpu as pltpu
from jax.sharding import PartitionSpec as P

D = 1024
HEADS = 16
FF = 4096
WIN = 1024

EPSILON = 1e-05
F32 = jnp.float32
BF16 = jnp.bfloat16
LANES = 128
MASKED = -1e30


LEAST = 256
ROLL = (3, 1, 2, 0)


def flip(block, axis, bit):
    count = lax.axis_size(axis)
    return lax.ppermute(block, axis, [(i, i ^ bit) for i in range(count)])


def step_along(block, axis, distance):
    devices = range(lax.axis_size(axis))
    route = [(i - distance, i) for i in devices if i - distance in devices]
    return lax.ppermute(block, axis, route)


def swap(block):
    return flip(block, "section", 1)


def tie(value, *after):
    return lax.optimization_barrier((value, after))[0]


class Gather:
    def __init__(self, shard, *after, then=()):
        shard = tie(shard, *after) if after else shard
        half = shard.shape[0] // 2
        self.near = flip(shard, "fsdp", 1), flip(shard, "fsdp", 2)
        from_x, from_y = tie(self.near, *then) if then else self.near
        self.far = flip(from_x[:half], "fsdp", 2), flip(from_y[half:], "fsdp", 1)
        self.pieces = (shard, *self.near, *self.far)


def add_bf16(*terms):
    return sum(term.astype(F32) for term in terms).astype(BF16)


class Scatter:
    def __init__(self, send_x, send_y, keep_x, keep_y):
        self.near = flip(send_x, "fsdp", 1), flip(send_y, "fsdp", 2)
        self.keep = keep_x, keep_y

    def second(self, *after):
        (got_x, got_y), (keep_x, keep_y) = tie(self.near, *after), self.keep
        self.half = add_bf16(keep_x[0], got_x[0]), add_bf16(keep_y[0], got_y[0])
        self.far = flip(self.half[0], "fsdp", 2), flip(self.half[1], "fsdp", 1)

    def third(self, *after):
        far_x, far_y = tie(self.far, *after)
        (got_x, got_y), (keep_x, keep_y) = self.near, self.keep
        self.piece = jnp.concatenate(
            [add_bf16(keep_x[1], got_x[1], far_x), add_bf16(keep_y[1], got_y[1], far_y)]
        )


class Column:
    def __init__(self):
        self.line = lax.axis_size("ctx") == 4
        me = lax.axis_index("ctx")
        self.inner = (me == 1) | (me == 2)
        self.block = self.half = self.total = self.outer_got = self.inner_got = None
        self.sums = []
        self.sent = ()

    def step(self, block, *after):
        if not self.line:
            if block is not None:
                self.sums.append(lax.psum(block, "ctx"))
            return
        outer_got, inner_got, block = tie((self.outer_got, self.inner_got, block), *after)
        half = total = None
        if self.block is not None:
            half = add_bf16(self.block, outer_got[: self.block.shape[0]])
        if self.half is not None:
            total = add_bf16(self.half, inner_got)
        if self.total is not None:
            outer_sum = outer_got[: self.total.shape[0]]
            self.sums.append(jnp.where(self.inner, self.total, outer_sum))
        self.block, self.half, self.total = block, half, total
        self.sent = ()
        if block is not None or total is not None:
            sent = total if block is None else block
            if block is not None and total is not None:
                rows = max(total.shape[0], block.shape[0])
                fill = lambda part: jnp.pad(part, ((0, rows - part.shape[0]), (0, 0)))
                sent = jnp.where(self.inner, fill(total), fill(block))
            self.outer_got = flip(sent, "ctx", 1)
            self.sent += (sent,)
        if half is not None:
            self.inner_got = lax.ppermute(half, "ctx", [(1, 2), (2, 1)])
            self.sent += (half,)


class Line:
    def __init__(self):
        self.token = ()
        self.also = ()

    def run(self, kernel, word, *args, after=()):
        word = tie(word, self.token, self.also, after)
        self.also = ()
        out = kernel(word, *args)
        self.token = out[0] if isinstance(out, (list, tuple)) else out
        return out


def sums_over_all(block):
    stages = [block]
    for axis in ("section", "fsdp", "ctx"):
        bit = 1
        while bit < lax.axis_size(axis):
            stages.append(stages[-1] + flip(stages[-1], axis, bit))
            bit *= 2
    return stages


def streamed(*arrays):
    return [pltpu.with_memory_space_constraint(array, pltpu.HBM) for array in arrays]


def call(kernel, out_shape, *operands, limit=24, flops=0, moved=0, exps=0, name=None, **rest):
    return pl.pallas_call(
        kernel,
        out_shape=out_shape,
        compiler_params=pltpu.CompilerParams(vmem_limit_bytes=limit * 1024 * 1024),
        cost_estimate=pl.CostEstimate(flops=flops, bytes_accessed=moved, transcendentals=exps),
        name=name,
        **rest,
    )(*operands)


def sds(*shape, dtype=BF16):
    return jax.ShapeDtypeStruct(shape, dtype)


def kept(*shape, dtype=BF16):
    return pltpu.HBM(shape, dtype)


ANYWHERE = pl.BlockSpec(memory_space=pltpu.HBM)
SCALARS = pl.BlockSpec(memory_space=pltpu.SMEM)
INSIDE = pl.BlockSpec(memory_space=pltpu.VMEM)


def fixed(*shape):
    return pl.BlockSpec(shape, lambda *_: (0,) * len(shape))


def fetches(me, pieces, wanted, sems):
    half = pieces[0].shape[0] // 2
    copies = []
    for number, (row, count, place) in enumerate(wanted):
        group = []
        for r in range(4):
            if r < 3:
                source = pieces[r].at[row : row + count]
            elif row < half:
                source = pieces[3].at[row : row + count]
            else:
                source = pieces[4].at[row - half : row - half + count]
            group.append(pltpu.make_async_copy(source, place(me ^ r), sems.at[number, r]))
        copies.append(group)
    return copies


def start_all(copies):
    for group in copies:
        for copy in group:
            copy.start()


def wait_group(group):
    for copy in group:
        copy.wait()


def part(a, size):
    return pl.ds(pl.multiple_of(a * size, size), size)


def wanted_qkv(w, which=(0, 1, 2)):
    return [
        (g * LEAST, LEAST, lambda a, i=i: w.at[i, part(a, LEAST)]) for i, g in enumerate(which)
    ]


def wanted_out(w):
    return [
        (3 * LEAST + j * 128, 128, lambda a, j=j: w.at[part(a, 128), j * 512 : (j + 1) * 512])
        for j in range(2)
    ]


def wanted_up(w):
    return [
        (j * LEAST, LEAST, lambda a, j=j: w.at[part(a, LEAST), j * 512 : (j + 1) * 512])
        for j in range(4)
    ]


def wanted_down(w):
    def place(a, rh, j):
        return w.at[pl.ds(pl.multiple_of(a * 512 + rh * 256, 256), 256), j * 512 : (j + 1) * 512]

    return [
        (
            (rh * 2 + j) * LEAST,
            LEAST,
            lambda a, rh=rh, j=j: place(a, rh, j),
        )
        for j in range(2)
        for rh in range(2)
    ]


def dot_nn(left, right):
    return lax.dot_general(left, right, (((1,), (0,)), ((), ())), preferred_element_type=F32)


def dot_nt(left, right):
    return lax.dot_general(left, right, (((1,), (1,)), ((), ())), preferred_element_type=F32)


def dot_tn(left, right):
    return lax.dot_general(left, right, (((0,), (0,)), ((), ())), preferred_element_type=F32)


def mean_last(values):
    return jnp.mean(values, axis=-1, keepdims=True)


def normalize(values):
    centred = values - mean_last(values)
    inverse = lax.rsqrt(mean_last(centred * centred) + EPSILON)
    return centred * inverse, inverse


def norm_back(grad_norm, normal, inverse):
    return inverse * (grad_norm - mean_last(grad_norm) - normal * mean_last(grad_norm * normal))


def column_sum(values):
    return jnp.sum(values.astype(F32), axis=0, keepdims=True)


def pack_kernel(
    core_ref, qkv, out, up, down, keep_a, send_a, keep_u, send_u, keep_d, send_d, sems
):
    core = core_ref[0]
    number = 0
    copies = []
    for target_a, target_u, target_d, half in (
        (send_a, send_u, send_d, 1 - core), (keep_a, keep_u, keep_d, core)
    ):
        for g in range(3):
            for f in range(4):
                columns = pl.ds(pl.multiple_of((g * 4 + f) * 256 + half * 128, 128), 128)
                copies.append(
                    (
                        qkv.at[0, :, columns],
                        target_a.at[g * LEAST : (g + 1) * LEAST, f * 128 : (f + 1) * 128],
                    )
                )
        for j in range(2):
            rows = pl.ds(pl.multiple_of(half * 128, 128), 128)
            copies.append(
                (
                    out.at[0, rows, j * 512 : (j + 1) * 512],
                    target_a.at[3 * LEAST + j * 128 : 3 * LEAST + (j + 1) * 128],
                )
            )
        for j in range(4):
            columns = pl.ds(pl.multiple_of(j * 1024 + half * 512, 512), 512)
            copies.append((up.at[0, :, columns], target_u.at[j * LEAST : (j + 1) * LEAST]))
        for rh in range(2):
            for j in range(2):
                rows = pl.ds(pl.multiple_of(half * 512 + rh * 256, 256), 256)
                at = (rh * 2 + j) * LEAST
                copies.append(
                    (down.at[0, rows, j * 512 : (j + 1) * 512], target_d.at[at : at + LEAST])
                )
    started = []
    for number, (source, target) in enumerate(copies):
        copy = pltpu.make_async_copy(source, target, sems.at[number])
        copy.start()
        started.append(copy)
    for copy in started:
        copy.wait()


def pack_weights(core, qkv, out, up, down):
    return call(
        pack_kernel,
        [kept(4 * LEAST, 512)] * 6,
        core, qkv, out, up, down,
        in_specs=[SCALARS] + [ANYWHERE] * 4,
        out_specs=[ANYWHERE] * 6,
        scratch_shapes=[pltpu.SemaphoreType.DMA((44,))],
        moved=12 << 20,
        limit=16,
        name="pack_weights",
    )


def qkv_kernel(
    me_ref, own_ref, other_ref, gain, bias, bq, bv, w0, w1, w2, w3, w4,
    a_ref, q_ref, k_ref, v_ref, w, sems,
):
    copies = fetches(me_ref[0], (w0, w1, w2, w3, w4), wanted_qkv(w), sems)
    start_all(copies)
    scale = BF16(1.0 / math.sqrt(D // HEADS))
    for m, x_ref in enumerate((own_ref, other_ref)):
        normed = (normalize(x_ref[...].astype(F32))[0] * gain[...] + bias[...]).astype(BF16)
        a_ref[m] = normed
        if m == 0:
            for group in copies:
                wait_group(group)
        q_ref[m] = (dot_nn(normed, w[0]) + bq[...]).astype(BF16) * scale
        k_ref[m] = dot_nn(normed, w[1]).astype(BF16)
        v_ref[m] = (dot_nn(normed, w[2]) + bv[...]).astype(BF16)


def make_qkv(me, own, other, gain, bias, bq, bv, pieces):
    rows = own.shape[0]
    half = D // 2
    return call(
        qkv_kernel,
        [kept(2, rows, D)] + [kept(2, rows, half)] * 3,
        me, own, other, gain, bias, bq, bv, *pieces,
        grid=(1,),
        in_specs=[SCALARS, fixed(rows, D), fixed(rows, D)]
        + [fixed(1, D), fixed(1, D), fixed(1, half), fixed(1, half)]
        + [ANYWHERE] * 5,
        out_specs=[fixed(2, rows, D)] + [fixed(2, rows, half)] * 3,
        scratch_shapes=[pltpu.VMEM((3, D, half), BF16), pltpu.SemaphoreType.DMA((3, 4))],
        flops=4 * rows * D * 3 * half,
        moved=14 << 20,
        name="project_qkv",
    )


def kv_kernel(me_ref, own_ref, other_ref, gain, bias, bv, w0, w1, w2, w3, w4, *rest):
    a_ref, k_ref, v_ref, w, sems = rest[-5:]
    copies = fetches(me_ref[0], (w0, w1, w2, w3, w4), wanted_qkv(w, (1, 2)), sems)
    start_all(copies)
    for m, x_ref in enumerate((own_ref, other_ref)):
        normed = (normalize(x_ref[...].astype(F32))[0] * gain[...] + bias[...]).astype(BF16)
        a_ref[m] = normed
        if m == 0:
            for group in copies:
                wait_group(group)
        k_ref[m] = dot_nn(normed, w[0]).astype(BF16)
        v_ref[m] = (dot_nn(normed, w[1]) + bv[...]).astype(BF16)


def make_kv(me, own, other, hops, at, earlier, gain, bias, bv, pieces):
    rows = own.shape[0]
    halo = hops * rows
    half = D // 2
    row = lambda width: pl.BlockSpec((2, rows, width), lambda i: (0, at, 0))
    first = 11
    return call(
        kv_kernel,
        [kept(2, halo, D), kept(2, halo, half), kept(2, halo, half)],
        me, own, other, gain, bias, bv, *pieces, *earlier,
        grid=(1,),
        in_specs=[SCALARS, fixed(rows, D), fixed(rows, D), fixed(1, D), fixed(1, D), fixed(1, half)]
        + [ANYWHERE] * 5
        + [ANYWHERE] * len(earlier),
        out_specs=[row(D), row(half), row(half)],
        input_output_aliases={first + i: i for i in range(len(earlier))},
        scratch_shapes=[pltpu.VMEM((2, D, half), BF16), pltpu.SemaphoreType.DMA((2, 4))],
        flops=2 * 2 * rows * D * 2 * half,
        moved=8 << 20,
        name="project_earlier",
    )


def out_kernel(me_ref, o_ref, w0, w1, w2, w3, w4, p_ref, w, sems):
    copies = fetches(me_ref[0], (w0, w1, w2, w3, w4), wanted_out(w), sems)
    start_all(copies)
    for group in copies:
        wait_group(group)
    p_ref[...] = dot_nn(o_ref[0], w[...]).astype(BF16)


def out_other(me, o, pieces):
    _, rows, half = o.shape
    return call(
        out_kernel,
        sds(rows, D),
        me, o, *pieces,
        grid=(1,),
        in_specs=[SCALARS, fixed(1, rows, half)] + [ANYWHERE] * 5,
        out_specs=fixed(rows, D),
        scratch_shapes=[pltpu.VMEM((half, D), BF16), pltpu.SemaphoreType.DMA((2, 4))],
        flops=2 * rows * half * D,
        moved=3 << 20,
        name="out_other",
    )


def middle_kernel(
    me_ref, o_ref, got, x_ref, bo, gain, bias, w0, w1, w2, w3, w4, x1_ref, h_ref, w, sems
):
    copies = fetches(me_ref[0], (w0, w1, w2, w3, w4), wanted_out(w), sems)
    start_all(copies)
    base = x_ref[...].astype(F32) + got[...].astype(F32) + bo[...]
    for group in copies:
        wait_group(group)
    x1 = base + dot_nn(o_ref[0], w[...])
    x1_ref[...] = x1
    h_ref[...] = (normalize(x1)[0] * gain[...] + bias[...]).astype(BF16)


def middle(me, o, got, x, bo, gain, bias, pieces):
    _, rows, half = o.shape
    return call(
        middle_kernel,
        [sds(rows, D, dtype=F32), sds(rows, D)],
        me, o, got, x, bo, gain, bias, *pieces,
        grid=(1,),
        in_specs=[SCALARS, fixed(1, rows, half)]
        + [fixed(rows, D)] * 2
        + [fixed(1, D)] * 3
        + [ANYWHERE] * 5,
        out_specs=[fixed(rows, D)] * 2,
        scratch_shapes=[pltpu.VMEM((half, D), BF16), pltpu.SemaphoreType.DMA((2, 4))],
        flops=2 * rows * half * D,
        moved=8 << 20,
        name="middle",
    )


def gelu_and_slope(u):
    c = math.sqrt(2.0 / math.pi)
    square = u * u
    half = 0.5 + 0.5 * jnp.tanh(u * (c + (c * 0.044715) * square))
    value = u * half
    slope = half + value * (1.0 - half) * (2.0 * c + (6.0 * c * 0.044715) * square)
    return value, slope


def up_kernel(me_ref, h_ref, bu, w0, w1, w2, w3, w4, act_ref, slope_ref, w, sems):
    copies = fetches(me_ref[0], (w0, w1, w2, w3, w4), wanted_up(w), sems)
    step = pl.program_id(0)

    @pl.when(step == 0)
    def _():
        start_all(copies)

    for j in range(4):

        @pl.when(step == j)
        def _(j=j):
            wait_group(copies[j])
            columns = slice(j * 512, (j + 1) * 512)
            rows = h_ref.shape[0]
            piece = min(256, rows)
            for r in range(0, rows, piece):
                u = dot_nn(h_ref[r : r + piece], w[:, columns]) + bu[:, columns]
                value, slope = gelu_and_slope(u)
                act_ref[r : r + piece] = value.astype(BF16)
                slope_ref[r : r + piece] = slope.astype(BF16)


def up(me, h, bu, pieces):
    rows = h.shape[0]
    half = FF // 2
    out = pl.BlockSpec((rows, 512), lambda j: (0, j))
    return call(
        up_kernel,
        [sds(rows, half), kept(rows, half)],
        me, h, bu, *pieces,
        grid=(4,),
        in_specs=[SCALARS, fixed(rows, D), fixed(1, half)] + [ANYWHERE] * 5,
        out_specs=[out, out],
        scratch_shapes=[pltpu.VMEM((D, half), BF16), pltpu.SemaphoreType.DMA((4, 4))],
        flops=2 * rows * half * D,
        moved=9 << 20,
        exps=rows * half,
        name="up",
    )


def down_kernel(me_ref, act, w0, w1, w2, w3, w4, p_ref, w, sems):
    copies = fetches(me_ref[0], (w0, w1, w2, w3, w4), wanted_down(w), sems)
    start_all(copies)
    for j in range(2):
        wait_group(copies[2 * j])
        wait_group(copies[2 * j + 1])
        columns = slice(j * 512, (j + 1) * 512)
        p_ref[:, columns] = dot_nn(act[...], w[:, columns]).astype(BF16)


def down_other(me, act, pieces):
    rows, half = act.shape
    return call(
        down_kernel,
        sds(rows, D),
        me, act, *pieces,
        grid=(1,),
        in_specs=[SCALARS, fixed(rows, half)] + [ANYWHERE] * 5,
        out_specs=fixed(rows, D),
        scratch_shapes=[pltpu.VMEM((half, D), BF16), pltpu.SemaphoreType.DMA((4, 4))],
        flops=2 * rows * half * D,
        moved=7 << 20,
        name="down_other",
    )


def last_kernel(me_ref, act, got, x1, bd, w0, w1, w2, w3, w4, y_ref, w, sems):
    copies = fetches(me_ref[0], (w0, w1, w2, w3, w4), wanted_down(w), sems)
    start_all(copies)
    for j in range(2):
        wait_group(copies[2 * j])
        wait_group(copies[2 * j + 1])
        columns = slice(j * 512, (j + 1) * 512)
        base = x1[:, columns] + got[:, columns].astype(F32) + bd[:, columns]
        y_ref[:, columns] = (base + dot_nn(act[...], w[:, columns])).astype(BF16)


def last(me, act, got, x1, bd, pieces):
    rows, half = act.shape
    return call(
        last_kernel,
        sds(rows, D),
        me, act, got, x1, bd, *pieces,
        grid=(1,),
        in_specs=[SCALARS, fixed(rows, half), fixed(rows, D), fixed(rows, D), fixed(1, D)]
        + [ANYWHERE] * 5,
        out_specs=fixed(rows, D),
        scratch_shapes=[pltpu.VMEM((half, D), BF16), pltpu.SemaphoreType.DMA((4, 4))],
        flops=2 * rows * half * D,
        moved=10 << 20,
        name="down_own",
    )


def lanes_of(rows, low):
    lane = lax.broadcasted_iota(jnp.int32, (rows, LANES), 1)
    return lane < LANES // 2 if low else lane >= LANES // 2


def split3(values):
    first = values.astype(BF16)
    rest = values - first.astype(F32)
    second = rest.astype(BF16)
    third = (rest - second.astype(F32)).astype(BF16)
    return first, second, third


def forward_kernel(
    rows, halo, block,
    word, q_ref, kh_ref, ko_ref, vh_ref, vo_ref, lo_ref, ek_ref, eq_ref, o_ref, e_ref,
):
    lane = lax.broadcasted_iota(jnp.int32, (block, LANES), 1)
    for q0 in range(0, rows, block):
        k0 = max(0, halo + q0 - WIN) // block * block
        k1 = halo + q0 + block
        q = q_ref[0, q0 : q0 + block, :]
        lo = lo_ref[0, q0 : q0 + block, :]
        outs = []
        for t in range(2):
            keep = lanes_of(block, t == 0)
            eq = jnp.broadcast_to(eq_ref[0, t : t + 1, :], (block, LANES))
            qcat = jnp.concatenate([q, eq.astype(BF16)], axis=1)
            tiles = []
            for kb in range(k0, k1, block):
                k = kh_ref[0, kb : kb + block, :] if kb < halo else ko_ref[0, kb - halo : kb - halo + block, :]
                kcat = jnp.concatenate(
                    [jnp.where(keep, k, jnp.zeros_like(k)), ek_ref[kb : kb + block, :]], axis=1
                )
                s = dot_nt(qcat, kcat)
                kidx = lax.broadcasted_iota(jnp.int32, (block, block), 1) + kb
                allowed = kidx >= lo
                if kb + block == k1:
                    qidx = lax.broadcasted_iota(jnp.int32, (block, block), 0) + (halo + q0)
                    allowed = allowed & (kidx <= qidx)
                tiles.append(jnp.where(allowed, s, MASKED))
            top = functools.reduce(jnp.maximum, tiles)
            m = jnp.max(top, axis=1, keepdims=True)
            product = None
            for kb, s in zip(range(k0, k1, block), tiles):
                if kb < halo:
                    v = vh_ref[0, kb : kb + block, :]
                else:
                    v = vo_ref[0, kb - halo : kb - halo + block, :]
                part = dot_nn(
                    jnp.exp(s - m).astype(BF16), jnp.concatenate([v, jnp.ones_like(v)], axis=1)
                )
                product = part if product is None else product + part
            total = product[:, LANES : LANES + 1]
            outs.append(product[:, :LANES] / total)
            first, second, third = split3(-(m + jnp.log(total)))
            e = jnp.where(lane == 6, first.astype(F32), eq)
            e = jnp.where(lane == 7, second.astype(F32), e)
            e = jnp.where(lane == 8, third.astype(F32), e)
            e_ref[0, t, q0 : q0 + block, :] = e.astype(BF16)
        o_ref[0, q0 : q0 + block, :] = jnp.where(lanes_of(block, True), outs[0], outs[1]).astype(
            BF16
        )


def attend(word, which, q, kh, ko, vh, vo, lo, ek, eq):
    _, rows, width = q.shape
    halo = kh.shape[1]
    pairs = width // LANES
    block = min(256, rows)
    spec = lambda n: pl.BlockSpec((1, n, LANES), lambda p: (which, 0, p))
    count = pairs * 2 * rows * (WIN + block)
    return call(
        functools.partial(forward_kernel, rows, halo, block),
        [sds(1, rows, width), kept(1, 2 * pairs, rows, LANES)],
        word, *streamed(q, kh, ko, vh, vo), lo, ek, eq,
        grid=(pairs,),
        in_specs=[
            SCALARS,
            spec(rows), spec(halo), spec(rows), spec(halo), spec(rows),
            pl.BlockSpec((1, rows, 1), lambda p: (which, 0, 0)),
            fixed(halo + rows, LANES),
            pl.BlockSpec((1, 2, LANES), lambda p: (p, 0, 0)),
        ],
        out_specs=[
            pl.BlockSpec((1, rows, LANES), lambda p: (0, 0, p)),
            pl.BlockSpec((1, 2, rows, LANES), lambda p: (0, p, 0, 0)),
        ],
        flops=count * 1024,
        moved=6 << 20,
        exps=count,
        name="attention_forward",
    )


def backward_kernel(
    rows, halo, block, begin, end, final,
    word, q_ref, kh_ref, ko_ref, vh_ref, vo_ref, o_ref, do_ref, e_ref, lo_ref, ek_ref, *refs,
):
    acc_ref = refs[-1]
    refs = list(refs[:-1])
    start_ref = refs.pop(0) if begin > 0 else None
    dq_ref = refs.pop(0)
    dkh_ref, dvh_ref = (refs.pop(0), refs.pop(0)) if begin == 0 else (None, None)
    dko_ref, dvo_ref = (refs.pop(0), refs.pop(0)) if final else (None, None)
    q = q_ref[0]
    do = do_ref[0]
    lo = lo_ref[0]
    lane = lax.broadcasted_iota(jnp.int32, (rows, LANES), 1)
    ones = jnp.where(lax.broadcasted_iota(jnp.int32, (block, LANES), 1) < 3, 1.0, 0.0).astype(BF16)
    product = do.astype(F32) * o_ref[0].astype(F32)
    qcats, docats, qts, dots = [], [], [], []
    for t in range(2):
        keep = lanes_of(rows, t == 0)
        delta = jnp.sum(jnp.where(keep, product, 0.0), axis=1, keepdims=True)
        first, second, third = split3(-delta)
        ed = jnp.where(lane == 0, first.astype(F32), 0.0)
        ed = jnp.where(lane == 1, second.astype(F32), ed)
        ed = jnp.where(lane == 2, third.astype(F32), ed)
        qcats.append(jnp.concatenate([q, e_ref[0, t]], axis=1))
        docats.append(jnp.concatenate([do, ed.astype(BF16)], axis=1))
        qts.append(jnp.where(keep, q, jnp.zeros_like(q)))
        dots.append(jnp.where(keep, do, jnp.zeros_like(do)))
    acc_ref[...] = jnp.zeros_like(acc_ref) if start_ref is None else start_ref[0]
    for kb in range(begin, end, block):
        if kb < halo:
            k_in, v_in, dk_out, dv_out, at = kh_ref, vh_ref, dkh_ref, dvh_ref, kb
        else:
            k_in, v_in, dk_out, dv_out, at = ko_ref, vo_ref, dko_ref, dvo_ref, kb - halo
        qlo = max(0, kb - halo)
        qhi = min(rows, -(-(kb + block - 1 + WIN - halo) // block) * block)
        if qhi <= qlo:
            dk_out[0, at : at + block, :] = jnp.zeros((block, LANES), BF16)
            dv_out[0, at : at + block, :] = jnp.zeros((block, LANES), BF16)
            continue
        k = k_in[0, at : at + block, :]
        v = v_in[0, at : at + block, :]
        ek = ek_ref[kb : kb + block, :]
        kidx = lax.broadcasted_iota(jnp.int32, (block, qhi - qlo), 0) + kb
        allowed = kidx >= lo[:, qlo:qhi]
        if kb + block > halo + qlo:
            qidx = lax.broadcasted_iota(jnp.int32, (block, qhi - qlo), 1) + (halo + qlo)
            allowed = allowed & (kidx <= qidx)
        pts, dss, kts = [], [], []
        for t in range(2):
            keep = lanes_of(block, t == 0)
            kt = jnp.where(keep, k, jnp.zeros_like(k))
            vt = jnp.where(keep, v, jnp.zeros_like(v))
            st = dot_nt(jnp.concatenate([kt, ek], axis=1), qcats[t][qlo:qhi])
            pt = jnp.exp(jnp.where(allowed, st, MASKED))
            dpt = dot_nt(jnp.concatenate([vt, ones], axis=1), docats[t][qlo:qhi])
            pts.append(pt.astype(BF16))
            dss.append((pt * dpt).astype(BF16))
            kts.append(kt)
        dv = dot_nn(jnp.concatenate(pts, axis=1), jnp.concatenate([d[qlo:qhi] for d in dots], axis=0))
        dk = dot_nn(jnp.concatenate(dss, axis=1), jnp.concatenate([d[qlo:qhi] for d in qts], axis=0))
        dv_out[0, at : at + block, :] = dv.astype(BF16)
        dk_out[0, at : at + block, :] = dk.astype(BF16)
        acc_ref[:, qlo:qhi] += dot_tn(jnp.concatenate(kts, axis=0), jnp.concatenate(dss, axis=0))
    if final:
        scale = 1.0 / math.sqrt(LANES // 2)
        dq_ref[0] = (acc_ref[...].T * scale).astype(BF16)
    else:
        dq_ref[0] = acc_ref[...]


def attend_back(word, which, q, kh, ko, vh, vo, o, do, e, lo, ek, start=None):
    _, rows, width = q.shape
    halo = kh.shape[1]
    pairs = width // LANES
    block = min(256, rows)
    begin, end, final = (0, halo, False) if start is None else (halo, halo + rows, True)
    spec = lambda n: pl.BlockSpec((1, n, LANES), lambda p: (which, 0, p))
    only = lambda n: pl.BlockSpec((1, n, LANES), lambda p: (0, 0, p))
    sums = pl.BlockSpec((1, LANES, rows), lambda p: (0, p, 0))
    count = pairs * 2 * rows * (WIN + block) * (end - begin) // (halo + rows)
    if final:
        shapes, specs = [sds(1, rows, width)] * 3, [only(rows)] * 3
    else:
        shapes = [sds(1, width, rows, dtype=F32)] + [sds(1, halo, width)] * 2
        specs = [sums, only(halo), only(halo)]
    return call(
        functools.partial(backward_kernel, rows, halo, block, begin, end, final),
        shapes,
        word, *streamed(q, kh, ko, vh, vo), o, do, *streamed(e), lo, ek,
        *([] if start is None else [start]),
        grid=(pairs,),
        in_specs=[
            SCALARS,
            spec(rows), spec(halo), spec(rows), spec(halo), spec(rows), only(rows), spec(rows),
            pl.BlockSpec((1, 2, rows, LANES), lambda p: (0, p, 0, 0)),
            pl.BlockSpec((1, 1, rows), lambda p: (which, 0, 0)),
            fixed(halo + rows, LANES),
        ]
        + ([] if start is None else [sums]),
        out_specs=specs,
        scratch_shapes=[pltpu.VMEM((LANES, rows), F32)],
        flops=count * 2304,
        moved=8 << 20,
        exps=count,
        name="attention_backward",
    )


def act_back_kernel(
    me_ref, own, other, slope_own, slope_other, w0, w1, w2, w3, w4,
    du_own, du_other, sums, w, sems,
):
    copies = fetches(me_ref[0], (w0, w1, w2, w3, w4), wanted_down(w), sems)
    step = pl.program_id(0)

    @pl.when(step == 0)
    def _():
        start_all(copies)
        for group in copies:
            wait_group(group)

    rows = own.shape[0]
    piece = min(256, rows)
    w_part = w[pl.ds(pl.multiple_of(step * 512, 512), 512), :]
    total = jnp.zeros((1, 512), F32)
    for dy, slope, du in ((other, slope_other, du_other), (own, slope_own, du_own)):
        for r in range(0, rows, piece):
            grad = dot_nt(dy[r : r + piece], w_part) * slope[r : r + piece].astype(F32)
            rounded = grad.astype(BF16)
            du[r : r + piece] = rounded
            total += column_sum(rounded)
    sums[...] = jnp.broadcast_to(total, (8, 512))


def act_back(me, own, other, slope_own, slope_other, pieces):
    rows = own.shape[0]
    half = FF // 2
    columns = pl.BlockSpec((rows, 512), lambda j: (0, j))
    return call(
        act_back_kernel,
        [sds(rows, half), sds(rows, half), sds(8, half, dtype=F32)],
        me, own, other, *streamed(slope_own, slope_other), *pieces,
        grid=(4,),
        in_specs=[SCALARS, fixed(rows, D), fixed(rows, D), columns, columns] + [ANYWHERE] * 5,
        out_specs=[columns, columns, pl.BlockSpec((8, 512), lambda j: (0, j))],
        scratch_shapes=[pltpu.VMEM((half, D), BF16), pltpu.SemaphoreType.DMA((4, 4))],
        flops=4 * rows * half * D,
        moved=16 << 20,
        name="act_back",
    )


def up_back_kernel(me_ref, du, w0, w1, w2, w3, w4, p_ref, w, sems):
    copies = fetches(me_ref[0], (w0, w1, w2, w3, w4), wanted_up(w), sems)
    start_all(copies)
    for group in copies:
        wait_group(group)
    p_ref[...] = dot_nt(du[...], w[...]).astype(BF16)


def up_back_other(me, du, pieces):
    rows, half = du.shape
    return call(
        up_back_kernel,
        sds(rows, D),
        me, du, *pieces,
        grid=(1,),
        in_specs=[SCALARS, fixed(rows, half)] + [ANYWHERE] * 5,
        out_specs=fixed(rows, D),
        scratch_shapes=[pltpu.VMEM((D, half), BF16), pltpu.SemaphoreType.DMA((4, 4))],
        flops=2 * rows * half * D,
        moved=7 << 20,
        name="up_back_other",
    )


def middle_back_kernel(
    me_ref, du, got, x1, dy, gain, w0, w1, w2, w3, w4, dx1_ref, db_ref, sums, w, sems
):
    copies = fetches(me_ref[0], (w0, w1, w2, w3, w4), wanted_up(w), sems)
    start_all(copies)
    normal, inverse = normalize(x1[...])
    for group in copies:
        wait_group(group)
    dh = dot_nt(du[...], w[...]) + got[...].astype(F32)
    top = dy[...].astype(F32)
    dx1 = top + norm_back(dh * gain[...], normal, inverse)
    dx1_ref[...] = dx1
    db = dx1.astype(BF16)
    db_ref[...] = db
    sums[0:1] = column_sum(dh * normal)
    sums[1:2] = column_sum(dh)
    sums[2:3] = column_sum(db)
    sums[3:4] = column_sum(top)
    sums[4:8] = jnp.zeros((4, D), F32)


def middle_back(me, du, got, x1, dy, gain, pieces):
    rows, half = du.shape
    return call(
        middle_back_kernel,
        [sds(rows, D, dtype=F32), sds(rows, D), sds(8, D, dtype=F32)],
        me, du, got, x1, dy, gain, *pieces,
        grid=(1,),
        in_specs=[SCALARS, fixed(rows, half)]
        + [fixed(rows, D)] * 3
        + [fixed(1, D)]
        + [ANYWHERE] * 5,
        out_specs=[fixed(rows, D), fixed(rows, D), fixed(8, D)],
        scratch_shapes=[pltpu.VMEM((D, half), BF16), pltpu.SemaphoreType.DMA((4, 4))],
        flops=2 * rows * half * D,
        moved=14 << 20,
        name="middle_back",
    )


def out_back_kernel(me_ref, own, other, w0, w1, w2, w3, w4, do_ref, w, sems):
    copies = fetches(me_ref[0], (w0, w1, w2, w3, w4), wanted_out(w), sems)
    start_all(copies)
    for group in copies:
        wait_group(group)
    do_ref[0] = dot_nt(own[...], w[...]).astype(BF16)
    do_ref[1] = dot_nt(other[...], w[...]).astype(BF16)


def out_back(me, own, other, pieces):
    rows = own.shape[0]
    half = D // 2
    return call(
        out_back_kernel,
        sds(2, rows, half),
        me, own, other, *pieces,
        grid=(1,),
        in_specs=[SCALARS, fixed(rows, D), fixed(rows, D)] + [ANYWHERE] * 5,
        out_specs=fixed(2, rows, half),
        scratch_shapes=[pltpu.VMEM((half, D), BF16), pltpu.SemaphoreType.DMA((2, 4))],
        flops=4 * rows * half * D,
        moved=4 << 20,
        name="out_back",
    )


def store_parts(step, parts_x, parts_y, send_x, send_y, keep_x, keep_y):
    def put(ref, pieces):
        row = 0
        for piece in pieces:
            ref[0, row : row + piece.shape[0]] = piece
            row += piece.shape[0]

    @pl.when(step < 2)
    def _():
        put(send_x, parts_x)

    @pl.when(step >= 2)
    def _():
        put(keep_x, parts_x)

    @pl.when(step % 2 == 0)
    def _():
        put(send_y, parts_y)

    @pl.when(step % 2 == 1)
    def _():
        put(keep_y, parts_y)


def part_outputs(rows):
    shapes = [kept(2, rows, 512)] * 4
    specs = [
        pl.BlockSpec((1, rows, 512), lambda i, order: (jnp.minimum(i, 1), 0, 0)),
        pl.BlockSpec((1, rows, 512), lambda i, order: (i // 2, 0, 0)),
        pl.BlockSpec((1, rows, 512), lambda i, order: (i // 3, 0, 0)),
        pl.BlockSpec((1, rows, 512), lambda i, order: (i // 3, 0, 0)),
    ]
    return shapes, specs


def down_grad_kernel(order, act_own, act_other, own, other, *outs):
    grad = (dot_tn(act_own[...], own[...]) + dot_tn(act_other[...], other[...])).astype(BF16)
    store_parts(
        pl.program_id(0),
        [grad[:256, :512], grad[:256, 512:]],
        [grad[256:, :512], grad[256:, 512:]],
        *outs,
    )


def down_grad(order, act_own, act_other, own, other):
    rows = own.shape[0]
    shapes, specs = part_outputs(512)
    columns = pl.BlockSpec((rows, 512), lambda i, order: (0, order[i]))
    full = pl.BlockSpec((rows, D), lambda i, order: (0, 0))
    return call(
        down_grad_kernel,
        shapes,
        order, *streamed(act_own, act_other), own, other,
        grid_spec=pltpu.PrefetchScalarGridSpec(
            num_scalar_prefetch=1,
            grid=(4,),
            in_specs=[columns, columns, full, full],
            out_specs=specs,
        ),
        flops=4 * rows * (FF // 2) * D,
        moved=10 << 20,
        name="down_grad",
    )


def up_grad_kernel(
    order, h_own, h_other, du_own, du_other, o_own, o_other, db_own, db_other, *outs
):
    grad = (dot_tn(h_own[...], du_own[...]) + dot_tn(h_other[...], du_other[...])).astype(BF16)
    out_part = (dot_tn(o_own[0], db_own[...]) + dot_tn(o_other[0], db_other[...])).astype(BF16)
    store_parts(
        pl.program_id(0),
        [grad[:, :512], grad[:, 512:1024], out_part[:, :512]],
        [grad[:, 1024:1536], grad[:, 1536:], out_part[:, 512:]],
        *outs,
    )


def up_grad(order, h_own, h_other, du_own, du_other, o_own, o_other, db_own, db_other):
    rows = h_own.shape[0]
    half = FF // 2
    shapes, specs = part_outputs(640)
    columns = pl.BlockSpec((rows, 256), lambda i, order: (0, order[i]))
    full = lambda width: pl.BlockSpec((rows, width), lambda i, order: (0, 0))
    heads = pl.BlockSpec((1, rows, 128), lambda i, order: (0, 0, order[i]))
    return call(
        up_grad_kernel,
        shapes,
        order, h_own, h_other, du_own, du_other, o_own, o_other, db_own, db_other,
        grid_spec=pltpu.PrefetchScalarGridSpec(
            num_scalar_prefetch=1,
            grid=(4,),
            in_specs=[columns, columns, full(half), full(half), heads, heads, full(D), full(D)],
            out_specs=specs,
        ),
        flops=4 * rows * half * D + 2 * rows * D * D,
        moved=14 << 20,
        name="up_grad",
    )


def qkv_grad_kernel(order, a_own, a_halo, *refs):
    dq, dko, dvo, dkh, dvh = (refs[2 * i : 2 * i + 2] for i in range(5))
    *parts, sums = refs[10:]

    def total(pairs):
        return sum(dot_tn(left[m], right[m][0]) for left, right in pairs for m in range(2)).astype(BF16)

    k_part = total([(a_own, dko), (a_halo, dkh)])
    first = [total([(a_own, dq)]), k_part[:128]]
    second = [k_part[128:], total([(a_own, dvo), (a_halo, dvh)])]
    store_parts(pl.program_id(0), first, second, *parts)

    @pl.when(pl.program_id(0) == 0)
    def _():
        sums[0:1] = column_sum(dq[0][0]) + column_sum(dq[1][0])
        sums[1:2] = sum(column_sum(ref[0]) for ref in (*dvo, *dvh))
        sums[2:8] = jnp.zeros((6, sums.shape[1]), F32)


def qkv_grad(order, a_own, a_halo, *grads):
    rows, halo = a_own.shape[1], a_halo.shape[1]
    half = D // 2
    shapes, specs = part_outputs(384)
    full = lambda n: pl.BlockSpec((1, n, half), lambda i, order: (0, 0, 0))
    columns = lambda n: pl.BlockSpec((2, n, 256), lambda i, order: (0, 0, order[i]))
    return call(
        qkv_grad_kernel,
        shapes + [sds(8, half, dtype=F32)],
        order, a_own, a_halo, *[ref for pair in grads for ref in pair],
        grid_spec=pltpu.PrefetchScalarGridSpec(
            num_scalar_prefetch=1,
            grid=(4,),
            in_specs=[columns(rows), columns(halo)]
            + [full(rows)] * 6
            + [full(halo)] * 4,
            out_specs=specs + [pl.BlockSpec((8, half), lambda i, order: (0, 0))],
        ),
        flops=4 * D * half * (3 * rows + 2 * halo),
        moved=16 << 20,
        name="qkv_grad",
    )


def normed_back_kernel(hops, me_ref, *refs):
    wanted = (1, 2) if hops else (0, 1, 2)
    count = len(wanted)
    grads, a_ref, refs = refs[:count], refs[count], refs[count + 1 :]
    *outs, sums, w, sems = refs[5:]
    got = outs.pop(0) if len(outs) > max(hops, 1) else None
    copies = fetches(me_ref[0], refs[:5], wanted_qkv(w, wanted), sems)
    start_all(copies)
    for group in copies:
        wait_group(group)
    weighted = jnp.zeros((1, D), F32)
    plain = jnp.zeros((1, D), F32)
    rows = outs[0].shape[0] if got is not None else a_ref.shape[1] // max(hops, 1)
    for number in range(max(hops, 1)):
        r = slice(number * rows, (number + 1) * rows)
        da = sum(dot_nt(grad[0, r], w[i]) for i, grad in enumerate(grads))
        weighted += column_sum(da * a_ref[0, r].astype(F32))
        plain += column_sum(da)
        if got is None:
            outs[0][r] = da.astype(BF16)
        else:
            da = da + got[r].astype(F32)
            outs[number][...] = da.astype(outs[number].dtype)
    sums[0:1] = weighted
    sums[1:2] = plain
    sums[2:8] = jnp.zeros((6, D), F32)


def normed_back(me, which, hops, grads, a, pieces, got=None):
    length = a.shape[1]
    rows = length // max(hops, 1)
    half = D // 2
    count = len(grads)
    if got is None:
        outs, out_specs = [sds(length, D)], [fixed(length, D)]
    elif hops:
        outs, out_specs = [sds(rows, D)] * hops, [fixed(rows, D)] * hops
    else:
        outs, out_specs = [sds(rows, D, dtype=F32)], [fixed(rows, D)]
    return call(
        functools.partial(normed_back_kernel, hops),
        outs + [sds(8, D, dtype=F32)],
        me, *grads, a, *pieces, *([] if got is None else [got]),
        grid=(1,),
        in_specs=[SCALARS]
        + [fixed(1, length, half)] * count
        + [pl.BlockSpec((1, length, D), lambda i: (which, 0, 0))]
        + [ANYWHERE] * 5
        + ([] if got is None else [fixed(length, D)]),
        out_specs=out_specs + [fixed(8, D)],
        scratch_shapes=[pltpu.VMEM((count, D, half), BF16), pltpu.SemaphoreType.DMA((count, 4))],
        flops=2 * count * length * half * D,
        moved=8 << 20,
        name="normed_back",
    )


def first_back_kernel(word, da_ref, got, x_ref, dx1, gain, dx_ref, low_ref):
    da = da_ref[...] + got[...].astype(F32)
    normal, inverse = normalize(x_ref[...].astype(F32))
    dx = dx1[...] + norm_back(da * gain[...], normal, inverse)
    dx_ref[...] = dx
    low_ref[...] = dx.astype(BF16)


def first_back(word, da, got, x, dx1, gain):
    rows = da.shape[0]
    return call(
        first_back_kernel,
        [sds(rows, D, dtype=F32), sds(rows, D)],
        word, da, got, x, dx1, gain,
        grid=(1,),
        in_specs=[SCALARS] + [fixed(rows, D)] * 4 + [fixed(1, D)],
        out_specs=[fixed(rows, D), fixed(rows, D)],
        moved=10 << 20,
        name="first_back",
    )


def unpack_down_kernel(core_ref, kept, got, out):
    core = core_ref[0]
    for half, source in ((core, kept), (1 - core, got)):
        for rh in range(2):
            for j in range(2):
                at = (rh * 2 + j) * 256
                rows = pl.ds(pl.multiple_of(half * 512 + rh * 256, 256), 256)
                out[0, rows, j * 512 : (j + 1) * 512] = source[at : at + 256].astype(F32)


def unpack_up_kernel(core_ref, kept_part, got, out_up, out_out):
    core = core_ref[0]
    for half, source in ((core, kept_part), (1 - core, got)):
        for j in range(4):
            at = (j // 2) * 640 + (j % 2) * 256
            columns = pl.ds(pl.multiple_of(j * 1024 + half * 512, 512), 512)
            out_up[0, :, columns] = source[at : at + 256].astype(F32)
        rows = pl.ds(pl.multiple_of(half * 128, 128), 128)
        for j in range(2):
            at = j * 640 + 512
            out_out[0, rows, j * 512 : (j + 1) * 512] = source[at : at + 128].astype(F32)


def unpack_qkv_kernel(core_ref, kept_part, got, out):
    core = core_ref[0]
    for half, source in ((core, kept_part), (1 - core, got)):
        for g in range(3):
            for f in range(4):
                columns = pl.ds(pl.multiple_of((g * 4 + f) * 256 + half * 128, 128), 128)
                out[0, :, columns] = source[
                    g * 256 : (g + 1) * 256, f * 128 : (f + 1) * 128
                ].astype(F32)


def unpack(kernel, core, pieces, shapes, name):
    return call(
        kernel,
        shapes,
        core, *pieces,
        in_specs=[SCALARS] + [INSIDE] * len(pieces),
        out_specs=jax.tree.map(lambda _: INSIDE, shapes),
        moved=10 << 20,
        name=name,
    )


def split_vector(values):
    pieces, offset = [], 0
    for length in (D, D, D, D, D, D, D, FF, D):
        pieces.append(values[offset : offset + length])
        offset += length
    return pieces


def shards(inputs, cotangent, segments, w_qkv, w_out, w_up, w_down, vectors):
    core = lax.axis_index("section")
    column = lax.axis_index("ctx")
    fs = lax.axis_index("fsdp")
    nf = lax.axis_size("fsdp")
    rows = inputs.shape[2]
    reach = (WIN - 1) // rows + 1
    halo = reach * rows
    first_core = core == 0
    me = fs.astype(jnp.int32).reshape(1)
    core_word = core.astype(jnp.int32).reshape(1)
    order = jnp.stack([fs ^ r for r in ROLL]).astype(jnp.int32)

    def pick(here, there):
        return jnp.where(first_core, here, there), jnp.where(first_core, there, here)

    mine = lambda values: lax.dynamic_index_in_dim(values, core, 0, keepdims=False)
    theirs = lambda values: lax.dynamic_index_in_dim(values, 1 - core, 0, keepdims=False)
    x_own, x_other = mine(inputs[:, 0]), theirs(inputs[:, 0])
    keep_a, send_a, keep_u, send_u, keep_d, send_d = pack_weights(
        tie(core_word, x_own), w_qkv, w_out, w_up, w_down
    )
    shard_a = pick(keep_a, swap(send_a))
    later = lambda value: tie(value, shard_a[0])

    shard_u = pick(keep_u, swap(later(send_u)))
    shard_d = pick(keep_d, swap(later(send_d)))
    both = tie(jnp.concatenate(pick(vectors, swap(vectors))), shard_u, shard_d)
    near = flip(both, "fsdp", 1)
    low_x = (fs & 1) == 0
    pair = jnp.concatenate([jnp.where(low_x, both, near), jnp.where(low_x, near, both)], 1)
    far = flip(pair, "fsdp", 2)
    low_y = (fs & 2) == 0
    packed = jnp.concatenate([jnp.where(low_y, pair, far), jnp.where(low_y, far, pair)], 1)
    packed = packed.astype(F32)

    a0 = Gather(shard_a[0])
    u0 = Gather(shard_u[0], a0.far)
    d0 = Gather(shard_d[0], a0.far)
    a1 = Gather(shard_a[1], d0.near)
    u1 = Gather(shard_u[1], a1.far)
    d1 = Gather(shard_d[1], a1.far)
    weights = ((a0, u0, d0), (a1, u1, d1))

    top = later(cotangent[:, 0])
    top_own, top_other = mine(top), theirs(top)
    marks = later(segments[:, 0])
    starts = jnp.stack([mine(marks), theirs(marks)])
    position = column * rows + jnp.arange(rows, dtype=jnp.int32)
    lo = jnp.maximum(starts, position[None] - (WIN - 1)) - (column * rows - halo)
    lo_column, lo = lo[:, :, None], lo[:, None, :]

    nought = later(jnp.zeros((), jnp.int32))
    key_index = lax.broadcasted_iota(jnp.int32, (halo + rows, LANES), 0) + nought
    lane = lax.broadcasted_iota(jnp.int32, (halo + rows, LANES), 1)
    placed = jnp.where(lane % 2 == 0, key_index // 256 * 256, key_index % 256)
    ek = jnp.where(lane < 6, placed, jnp.where(lane < 9, 1, 0)).astype(BF16)
    local_heads = HEADS // 2
    per_group = local_heads // nf
    local = jnp.arange(local_heads) + nought
    head = (local // per_group) * (2 * per_group) + core * per_group + local % per_group
    slopes = jnp.exp2(-0.5 * (head.astype(F32) + 1.0)) * (4.0 / WIN)
    first, second, third = [values.astype(F32) for values in split3(slopes)]
    eq = jnp.concatenate(
        [
            jnp.stack([first, first, second, second, third, third], 1),
            jnp.zeros((local_heads, LANES - 6), F32),
        ],
        1,
    ).reshape(local_heads // 2, 2, LANES)

    def start_halo(own, *after):
        pieces, block = [], own
        for hop in range(reach):
            block = step_along(tie(block, *after) if hop == 1 else block, "ctx", 1)
            pieces.append(block)
        return pieces

    def finish_return(first, hops, *after):
        carried, sent = first, first
        for hop, piece in enumerate(hops[1:]):
            sent = add_bf16(piece, tie(carried, *after) if hop == 0 else carried)
            carried = step_along(sent, "ctx", -1)
        return carried, sent

    def my_half(values, groups):
        view = values.reshape(groups, 2, -1)
        return jnp.where(first_core, view[:, 0], view[:, 1]).reshape(1, -1)

    def widen(values, groups):
        view = values.reshape(groups, 1, -1)
        zero = jnp.zeros_like(view)
        return jnp.where(
            first_core, jnp.concatenate([view, zero], 1), jnp.concatenate([zero, view], 1)
        ).reshape(-1)

    line = Line()
    run = line.run

    def forward(layer, x_own, x_other, first_hops):
        g1, b1, bq, bv, bo, g2, b2, bu, bd = [
            values.reshape(1, -1) for values in split_vector(packed[layer])
        ]
        bq, bv, bu = my_half(bq, nf), my_half(bv, nf), my_half(bu, nf)
        ga, gu, gd = weights[layer]
        wa, wu, wd = ga.pieces, gu.pieces, gd.pieces
        a_own, q, ko, vo = run(
            make_qkv, me, x_own, x_other, g1, b1, bq, bv, wa,
            after=(ek, eq, lo, lo_column, bu, first_hops if layer == 0 else ()),
        )
        earlier = ()
        for hop, block in enumerate(first_hops):
            block = tie(block, line.token if hop == 0 else ())
            earlier = run(
                make_kv, me, block, swap(block), reach, reach - 1 - hop, earlier, g1, b1, bv, wa,
                after=first_hops if hop == 0 else (),
            )
        a_halo, kh, vh = earlier
        o_other, e_other = run(
            attend, me, 1, q, kh, ko, vh, vo, lo_column, ek, eq, after=(gu.near,)
        )
        part = run(out_other, me, o_other, wa)
        o_own, e_own = run(
            attend, me, 0, q, kh, ko, vh, vo, lo_column, ek, eq, after=(gd.near,)
        )
        x1, h_own = run(
            middle, me, o_own, swap(part), x_own, bo, g2, b2, wa, after=(gu.far,)
        )
        o, e = (o_own, o_other), (e_own, e_other)
        h_other = swap(h_own)
        act_own, slope_own = run(up, me, h_own, bu, wu)
        act_other, slope_other = run(up, me, h_other, bu, wu)
        part = run(down_other, me, act_other, wd)
        y = run(last, me, act_own, swap(part), x1, bd, wd)
        stored = (
            x_own, a_own, a_halo, q, kh, ko, vh, vo, o, e, x1, h_own, h_other,
            act_own, slope_own, act_other, slope_other, g1, b1, g2,
        )
        return y, stored

    y0, stored0 = forward(0, x_own, x_other, start_halo(x_own, shard_a[0]))
    y0_other = swap(y0)
    y1, stored1 = forward(1, y0, y0_other, start_halo(y0, a1.near))
    y1_other = swap(y1)

    column_sums = Column()

    def step(block, *after):
        column_sums.step(block, line.token, *after)
        line.also += column_sums.sent

    def backward(layer, top_own, top_other, stored, before=()):
        last_layer = layer == 0
        (
            x_own, a_own, a_halo, q, kh, ko, vh, vo, o, e, x1, h_own, h_other,
            act_own, slope_own, act_other, slope_other, g1, b1, g2,
        ) = stored
        wa, wu, wd = (group.pieces for group in weights[layer])
        du_own, du_other, sums_up = run(
            act_back, me, top_own, top_other, slope_own, slope_other, wd
        )
        got = swap(run(up_back_other, me, du_other, wu))
        down_part = Scatter(*run(down_grad, order, act_own, act_other, top_own, top_other))
        if last_layer:
            before[1].third(line.token)
        dx1, db_own, sums_middle = run(middle_back, me, du_own, got, x1, top_own, g2, wu)
        db_other = swap(db_own)
        do = run(out_back, me, db_own, db_other, wa)
        up_part = Scatter(
            *run(up_grad, order, h_own, h_other, du_own, du_other, *o, db_own, db_other)
        )
        if last_layer:
            step(before[0].piece)

        def early(m):
            return run(attend_back, me, m, q, kh, ko, vh, vo, o[m], do, e[m], lo, ek)

        def own(m, start):
            return run(attend_back, me, m, q, kh, ko, vh, vo, o[m], do, e[m], lo, ek, start)

        begun_other, dkh_other, dvh_other = early(1)
        down_part.second(line.token)
        line.also += (down_part.half,)
        if last_layer:
            step(before[1].piece)
        part, sums_a = run(normed_back, me, 1, reach, (dkh_other, dvh_other), a_halo, wa)
        got = swap(part)
        begun_own, dkh_own, dvh_own = early(0)
        down_part.third(line.token)
        line.also = (down_part.piece,)
        *hops, sums_b = run(normed_back, me, 0, reach, (dkh_own, dvh_own), a_halo, wa, got)
        first = step_along(hops[0], "ctx", -1)
        carried = sent = first
        if last_layer:
            step(down_part.piece, hops)
        else:
            carried, sent = finish_return(first, hops)
        dq_other, dko_other, dvo_other = own(1, begun_other)
        part, sums_c = run(normed_back, me, 1, 0, (dq_other, dko_other, dvo_other), a_own, wa)
        got = swap(part)
        up_part.second(line.token)
        line.also += (up_part.half,)
        dq_own, dko_own, dvo_own = own(0, begun_own)
        *parts, sums_qkv = run(
            qkv_grad, order, a_own, a_halo, (dq_own, dq_other), (dko_own, dko_other),
            (dvo_own, dvo_other), (dkh_own, dkh_other), (dvh_own, dvh_other),
            after=(column_sums.outer_got, column_sums.inner_got) if last_layer else (sent,),
        )
        qkv_part = Scatter(*parts)
        up_part.third(line.token)
        line.also = (up_part.piece,)
        if last_layer:
            step(up_part.piece)
        da, sums_d = run(
            normed_back, me, 0, 0, (dq_own, dko_own, dvo_own), a_own, wa, got,
            after=() if last_layer else (carried,),
        )
        qkv_part.second(line.token)
        line.also += (qkv_part.half,)
        if last_layer:
            carried, sent = finish_return(first, hops, line.token)
            line.also += (sent,)
            qkv_part.third()
            step(qkv_part.piece)
        dx, dx_low = run(first_back, me, da, carried, x_own, dx1, g1)
        if not last_layer:
            step(down_part.piece)
        plain = sums_a[1] + sums_b[1] + sums_c[1] + sums_d[1]
        weighted = sums_a[0] + sums_b[0] + sums_c[0] + sums_d[0]
        vector = jnp.concatenate(
            [
                (weighted - b1[0] * plain) / g1[0], plain, widen(sums_qkv[0], nf),
                widen(sums_qkv[1], nf), sums_middle[2], sums_middle[0], sums_middle[1],
                widen(sums_up[0], nf), sums_middle[3],
            ]
        )
        return dx, dx_low, (up_part, qkv_part), vector

    _, dx1, parts1, vector1 = backward(1, top_own, top_other, stored1)
    dx1_other = swap(dx1)
    dx0, _, _, vector0 = backward(0, dx1, dx1_other, stored0, parts1)
    dx0_other = swap(dx0)
    stages = sums_over_all(jnp.stack([vector0, vector1]))
    step(None, stages[2])
    def by_micro(own, other):
        return jnp.where(first_core, jnp.stack([own, other]), jnp.stack([other, own]))

    activations = jnp.where(first_core, by_micro(y0, y0_other), by_micro(y1, y1_other))
    input_grad = jnp.where(
        first_core, by_micro(dx0, dx0_other), by_micro(dx1, dx1_other).astype(F32)
    )

    def exchange(first, second):
        kept, sent = pick(first, second)
        return kept, swap(sent)

    waiting = column_sums.outer_got, column_sums.inner_got
    waiting, activations, input_grad = lax.optimization_barrier((waiting, activations, input_grad))
    column_sums.outer_got, column_sums.inner_got = waiting
    step(None, stages[4])
    size = D // nf
    down1_sum, up1_sum, qkv1_sum, down0_sum, up0_sum, *_ = column_sums.sums
    grad_down = unpack(
        unpack_down_kernel, core_word, exchange(down0_sum, down1_sum),
        sds(1, FF // nf, D, dtype=F32), "unpack_down",
    )
    grad_up, grad_out = unpack(
        unpack_up_kernel, core_word, exchange(up0_sum, up1_sum),
        [sds(1, size, FF, dtype=F32), sds(1, size, D, dtype=F32)], "unpack_up",
    )
    waiting = column_sums.outer_got
    waiting, grad_down, grad_up, grad_out = lax.optimization_barrier(
        (waiting, grad_down, grad_up, grad_out)
    )
    column_sums.outer_got = waiting
    step(None, stages[-1])
    qkv0_sum = column_sums.sums[-1]
    grad_qkv = unpack(
        unpack_qkv_kernel, core_word, exchange(qkv0_sum, qkv1_sum),
        sds(1, size, 3 * D, dtype=F32), "unpack_qkv",
    )
    summed = stages[-1]
    length = summed.shape[1] // nf
    grad_vectors = lax.dynamic_slice(summed, (core, fs * length), (1, length))
    return (
        activations[None, :, None], input_grad[None, :, None],
        grad_qkv, grad_out, grad_up, grad_down, grad_vectors,
    )


def solution(mesh):
    placed = (
        P(None, "fsdp", "ctx", None),
        P(None, "fsdp", "ctx", None),
        P(None, "fsdp", "ctx"),
        P("section", "fsdp", None),
        P("section", "fsdp", None),
        P("section", "fsdp", None),
        P("section", "fsdp", None),
        P("section", "fsdp"),
    )
    return jax.shard_map(
        shards,
        mesh=mesh,
        in_specs=placed,
        out_specs=(
            P("section", None, "fsdp", "ctx", None),
            P("section", None, "fsdp", "ctx", None),
            P("section", "fsdp", None),
            P("section", "fsdp", None),
            P("section", "fsdp", None),
            P("section", "fsdp", None),
            P("section", "fsdp"),
        ),
        check_vma=False,
    )
```
